32 devices in a mesh: seq: 8 (over y, x, core), dp: 4 (over z).
Axes of the slice: x: 2, y: 2, z: 4, core: 2. Of those that a mesh axis runs over, the one named last changes fastest.
Arguments:
- query_heads: bfloat16 [4, 2048, 1024], P('dp', 'seq'), may hold values from -6 to 6
- key_heads: bfloat16 [4, 2048, 1024], P('dp', 'seq'), may hold values from -6 to 6
- value_heads: bfloat16 [4, 2048, 1024], P('dp', 'seq'), may hold values from -6 to 6
- beta_logits: float32 [4, 2048, 8], P('dp', 'seq'), may hold values from -8 to 3.5
- segment_ids: int32 [4, 2048], P('dp', 'seq'), may hold values from 0 to 5, as said below
- output_cotangent: bfloat16 [4, 2048, 1024], P('dp', 'seq'), may hold values from -6 to 6
- norm_gain: float32 [128], replicated, may hold values from 0.25 to 1.75
Outputs:
- mixed_heads: bfloat16 [4, 2048, 1024], P('dp', 'seq')
- grad_query: bfloat16 [4, 2048, 1024], P('dp', 'seq')
- grad_key: bfloat16 [4, 2048, 1024], P('dp', 'seq')
- grad_value: bfloat16 [4, 2048, 1024], P('dp', 'seq')
- grad_beta: float32 [4, 2048, 8], P('dp', 'seq')
- grad_gain: float32 [128], replicated
The draws below stay inside these ranges and needn't reach their ends.
Inputs may be any that keep to these rules, and one draw needn't show every extreme that they name: `segment_ids`: in every row the ids start at 0, never fall, and rise by at most one from a token to the next; the row's first span of 256 tokens and each span in the row's second half hold exactly one document start after the span's first token, the other spans none.
All inputs are finite; a program needn't handle non-finite values.
Results may differ from the reference program's by a relative error of at most 0.001.
Values sent between devices are 32-bit elements; how exact they have to be, the bound alone decides.
No kernel may reach another device: no remote copies, remote signals or barrier semaphores. Data moves between devices by JAX's collectives and lax.ppermute only.
A program may use at most 192 MiB of HBM per device.

```python
from functools import partial
import jax
import jax.numpy as jnp
from jax import lax

HEADS = 8
HEAD_DIM = 128
BLOCK = 64
SPAN = 256
HEAD_WIDTH = 1024
SEQ = 2048
BATCH = 4


def draw_segment_ids(key, part):
    key_start = jax.random.fold_in(key, 11)
    spans_row = SEQ // SPAN
    coin = jax.random.randint(key_start, (BATCH, spans_row), 1, SPAN)
    position = jnp.arange(SEQ)
    span_index = position // SPAN
    within = position % SPAN
    chosen = coin[:, span_index]
    opened = (span_index[None, :] >= spans_row // 2) | (span_index[None, :] == 0)
    starts = jnp.where((within[None, :] == chosen) & opened, 1, 0).astype(jnp.int32)
    return jnp.cumsum(starts, axis=1).astype(jnp.int32)


def draw_beta_logits(key, part):
    key_center = jax.random.fold_in(key, 21)
    key_noise = jax.random.fold_in(key, 22)
    center = jax.random.uniform(key_center, (BATCH, 1, HEADS), jnp.float32, -5.0, 1.0)
    noise = jnp.clip(0.7 * jax.random.normal(key_noise, (BATCH, SEQ, HEADS), jnp.float32), -2.0, 2.0)
    return (center + noise).astype(jnp.float32)


def block_levels(stream_key, shape, split, least, top_value):
    factor_of = 1.0
    for axis_at, shards_of in split:
        heights = jax.random.uniform(jax.random.fold_in(jax.random.fold_in(stream_key, 6), axis_at), (shards_of,), jnp.float32, least / len(split), top_value / len(split))
        factor_of = factor_of * jnp.repeat(jnp.exp(heights), shape[axis_at] // shards_of).reshape((-1,) + (1,) * (len(shape) - 1 - axis_at))
    return factor_of


def bell_draw(rng, extent, scale, limit, pieces=(), kind=jnp.bfloat16):
    level = block_levels(rng, extent, pieces, -0.22, 0.18) if pieces else 1.0
    entries = jax.random.normal(rng, extent, jnp.float32) * scale * level
    return jnp.minimum(jnp.maximum(entries, -limit), limit).astype(kind)


def setup_inputs(seed: int = 0) -> dict:
    keys = jax.random.split(jax.random.key(seed), 8)
    return {
        "query_heads": bell_draw(keys[0], (BATCH, SEQ, HEAD_WIDTH), 1.0, 6.0, ((0, 4), (1, 8))),
        "key_heads": bell_draw(keys[1], (BATCH, SEQ, HEAD_WIDTH), 1.0, 6.0, ((0, 4), (1, 8))),
        "value_heads": bell_draw(keys[2], (BATCH, SEQ, HEAD_WIDTH), 1.0, 6.0, ((0, 4), (1, 8))),
        "beta_logits": draw_beta_logits(jax.random.fold_in(keys[7], 71), 0),
        "segment_ids": draw_segment_ids(jax.random.fold_in(keys[7], 71), 0),
        "output_cotangent": bell_draw(keys[5], (BATCH, SEQ, HEAD_WIDTH), 1.0, 6.0, ((0, 4), (1, 8))),
        "norm_gain": jnp.clip(1.0 + 0.15 * jax.random.normal(keys[6], (HEAD_DIM,), jnp.float32), 0.25, 1.75),
    }


HIGHEST = lax.Precision.HIGHEST

def normalize(vectors):
    return vectors * lax.rsqrt(lax.optimization_barrier(jnp.sum(vectors * vectors, axis=-1, keepdims=True)) + 1e-06)

def block_step(carried, inputs, want_out):
    memory, prior_id = carried
    query_block, keys_block, value_block, rates_block, ident_block = inputs
    block_size = keys_block.shape[0]
    position = jnp.arange(block_size)
    same_doc = ident_block[:, None] == ident_block[None, :]
    strict = (position[:, None] > position[None, :]) & same_doc
    causal = (position[:, None] >= position[None, :]) & same_doc
    keep_in = (ident_block == prior_id).astype(jnp.float32)
    in_last = (ident_block == ident_block[block_size - 1]).astype(jnp.float32)
    carry_on = (ident_block[block_size - 1] == prior_id).astype(jnp.float32)
    rate_rows = jnp.transpose(rates_block)[:, :, None]
    key_inner = jnp.einsum('thd,shd->hts', keys_block, keys_block, precision=HIGHEST)
    system = jnp.eye(block_size, dtype=jnp.float32)[None] + jnp.where(strict[None], key_inner, 0.0) * rate_rows
    recalled = jnp.einsum('thd,hvd->htv', keys_block, memory, precision=HIGHEST)
    target = rate_rows * (jnp.transpose(value_block, (1, 0, 2)) - keep_in[None, :, None] * recalled)
    update = lax.linalg.triangular_solve(system, target, left_side=True, lower=True, unit_diagonal=True)
    new_memory = carry_on * memory + jnp.einsum('hsv,shd->hvd', update * in_last[None, :, None], keys_block, precision=HIGHEST)
    output = None
    if want_out:
        scores = jnp.where(causal[None], jnp.einsum('thd,shd->hts', query_block, keys_block, precision=HIGHEST), 0.0)
        output = keep_in[:, None, None] * jnp.einsum('thd,hvd->thv', query_block, memory, precision=HIGHEST)
        output = output + jnp.einsum('hts,hsv->thv', scores, update, precision=HIGHEST)
    return ((new_memory, ident_block[block_size - 1]), output)

def span_pass(query_norm, key_norm, values_in, rates, doc_ids, prior_id, memory, want_out):
    tokens_here = doc_ids.shape[0]
    count_blocks = tokens_here // BLOCK
    blocks = (query_norm.reshape(count_blocks, BLOCK, query_norm.shape[1], query_norm.shape[2]), key_norm.reshape(count_blocks, BLOCK, key_norm.shape[1], key_norm.shape[2]), values_in.reshape(count_blocks, BLOCK, values_in.shape[1], values_in.shape[2]), rates.reshape(count_blocks, BLOCK, rates.shape[1]), doc_ids.reshape(count_blocks, BLOCK))
    final, outputs = lax.scan(partial(block_step, want_out=want_out), (memory, prior_id), blocks)
    if want_out:
        outputs = outputs.reshape(tokens_here, outputs.shape[2], outputs.shape[3])
    return (final[0], outputs)

def local_layer(query_wide, key_wide, value_wide, logits, gain_vec, memory, doc_ids, prior_id):
    tokens_here = doc_ids.shape[0]
    query_norm = normalize(query_wide.reshape(tokens_here, HEADS, HEAD_DIM))
    key_norm = normalize(key_wide.reshape(tokens_here, HEADS, HEAD_DIM))
    values_in = value_wide.reshape(tokens_here, HEADS, HEAD_DIM)
    rates = jax.nn.sigmoid(logits)
    final_memory, output = span_pass(query_norm, key_norm, values_in, rates, doc_ids, prior_id, memory, True)
    inverse_rms = lax.rsqrt(lax.optimization_barrier(jnp.mean(output * output, axis=-1, keepdims=True)) + 1e-05)
    mixed = (output * inverse_rms * gain_vec).reshape(tokens_here, HEADS * HEAD_DIM)
    return (mixed, final_memory)

def reference(query_heads, key_heads, value_heads, beta_logits, segment_ids, output_cotangent, norm_gain):

    def one_row(row_data):
        query_row, key_row, value_row, logit_row, ident_row, cotangent_row = row_data
        start_memory = jnp.zeros((HEADS, HEAD_DIM, HEAD_DIM), jnp.float32)
        start_id = jnp.array(-1, dtype=jnp.int32)

        def layer_fn(query_wide, key_wide, value_wide, logits, gain_vec):
            mixed, final_memory = local_layer(query_wide, key_wide, value_wide, logits, gain_vec, start_memory, ident_row, start_id)
            return mixed
        mixed, pullback = jax.vjp(layer_fn, query_row.astype(jnp.float32), key_row.astype(jnp.float32), value_row.astype(jnp.float32), logit_row, norm_gain)
        gradients = pullback(cotangent_row.astype(jnp.float32))
        return (mixed.astype(jnp.bfloat16), gradients[0].astype(jnp.bfloat16), gradients[1].astype(jnp.bfloat16), gradients[2].astype(jnp.bfloat16), gradients[3], gradients[4])
    results = lax.map(one_row, (query_heads, key_heads, value_heads, beta_logits, segment_ids, output_cotangent))
    return (results[0], results[1], results[2], results[3], results[4], lax.optimization_barrier(jnp.sum(results[5], axis=0)))
```

```python
import functools

import jax
import jax.numpy as jnp
from jax import lax
from jax.experimental import pallas as pl
from jax.experimental.pallas import tpu as pltpu
from jax.sharding import PartitionSpec as P

HEADS = 8
DIM = 128
GROUP = 2
HIGHEST = lax.Precision.HIGHEST
F32 = jnp.float32
BF16 = jnp.bfloat16

NN = (((1,), (0,)), ((), ()))
NT = (((1,), (1,)), ((), ()))
TN = (((0,), (0,)), ((), ()))


def split(x):
    hi = x.astype(BF16)
    return hi, (x - hi.astype(F32)).astype(BF16)


def mm(a, b, dims=NN):
    return lax.dot_general(a, b, dims, preferred_element_type=F32)


def dot3(a, b, dims=NN):
    return mm(a[0], b[0], dims) + (mm(a[0], b[1], dims) + mm(a[1], b[0], dims))


def dot2(a, b, dims=NN):
    return mm(a[0], b, dims) + mm(a[1], b, dims)


def dot2r(a, b, dims=NN):
    return mm(a, b[0], dims) + mm(a, b[1], dims)


def id_masks(ids_ref):
    row = ids_ref[...].astype(F32)
    n = row.shape[1]
    ii = lax.broadcasted_iota(jnp.int32, (n, n), 0)
    jj = lax.broadcasted_iota(jnp.int32, (n, n), 1)
    col = jnp.sum(jnp.where(ii == jj, row, 0.0), axis=1, keepdims=True)
    same = col == row
    first, last = row[:, :1], row[:, n - 1 :]
    keep = (col == first).astype(F32)
    tail = (col == last).astype(F32)
    through = (first == last).astype(F32)
    return same, ii, jj, keep, tail, through


def head(ref, j):
    return ref[:, DIM * j : DIM * (j + 1)]


def put(ref, j, value):
    ref[:, DIM * j : DIM * (j + 1)] = value.astype(ref.dtype)


def inv_norm(x):
    return lax.rsqrt(jnp.sum(x * x, axis=-1, keepdims=True) + 1e-06)


def logit_of(beta_ref, j):
    at = pl.program_id(0) * GROUP + j
    lane = lax.broadcasted_iota(jnp.int32, beta_ref.shape, 1)
    return jnp.sum(jnp.where(lane == at, beta_ref[...], 0.0), axis=1, keepdims=True)


def inverse(blocks):
    n = DIM
    ii = lax.broadcasted_iota(jnp.int32, (n, n), 0)
    jj = lax.broadcasted_iota(jnp.int32, (n, n), 1)
    eye = (ii == jj).astype(F32)

    def off(block, s):
        inside = (ii // (2 * s) == jj // (2 * s)) & (ii // s != jj // s)
        return jnp.where(inside, block, 0.0)

    ts = [eye - off(b, 1) for b in blocks]
    s = 2
    while s < n:
        offs = [split(off(b, s)) for b in blocks]
        tss = [split(t) for t in ts]
        mids = [dot3(o, t) for o, t in zip(offs, tss)]
        mids = [split(m) for m in mids]
        ts = [t - dot3(p, m) for t, p, m in zip(ts, tss, mids)]
        s *= 2
    return ts


def kernel_a(ids_ref, k_ref, v_ref, beta_ref, at_ref, bt_ref, th_ref, tl_ref, uw_ref):
    same, ii, jj, keep, tail, through = id_masks(ids_ref)
    strict = same & (ii > jj)
    heads = range(GROUP)
    ks = [head(k_ref, j) for j in heads]
    k32 = [k.astype(F32) for k in ks]
    iks = [inv_norm(k) for k in k32]
    rates = [jax.nn.sigmoid(logit_of(beta_ref, j)) for j in heads]
    cs = [r * i * i for r, i in zip(rates, iks)]
    ns = [jnp.where(strict, mm(k, k, NT), 0.0) * c for k, c in zip(ks, cs)]
    blocks = []
    for n in ns:
        blocks += [n[:DIM, :DIM], n[DIM:, DIM:]]
    ts = inverse(blocks)
    t1s = [split(t) for t in ts[0::2]]
    t2s = [split(t) for t in ts[1::2]]
    mids = [split(dot3(split(n[DIM:, :DIM]), t)) for n, t in zip(ns, t1s)]
    lows = [split(-dot3(t, m)) for t, m in zip(t2s, mids)]
    zero = jnp.zeros((DIM, DIM), BF16)
    fulls = [
        tuple(
            jnp.concatenate(
                [
                    jnp.concatenate([t1[p], zero], axis=1),
                    jnp.concatenate([lo[p], t2[p]], axis=1),
                ],
                axis=0,
            )
            for p in range(2)
        )
        for t1, t2, lo in zip(t1s, t2s, lows)
    ]
    eye = (
        lax.broadcasted_iota(jnp.int32, (DIM, DIM), 0)
        == lax.broadcasted_iota(jnp.int32, (DIM, DIM), 1)
    ).astype(F32)
    for j in heads:
        value = head(v_ref, j).astype(F32)
        right = jnp.concatenate(
            [value * (rates[j] * iks[j]), k32[j] * (cs[j] * keep)], axis=1
        )
        uw = dot3(fulls[j], split(right))
        ending = (k32[j] * tail).astype(BF16)
        both = dot2r(ending, split(uw), TN)
        bt_ref[j] = both[:, :DIM]
        at_ref[j] = eye * through - both[:, DIM:]
        th_ref[j] = fulls[j][0]
        tl_ref[j] = fulls[j][1]
        uw_ref[j] = uw


def kernel_b(ids_ref, q_ref, k_ref, uw_ref, o_ref, e_ref):
    same, ii, jj, keep, tail, through = id_masks(ids_ref)
    causal = same & (ii >= jj)
    for j in range(GROUP):
        q, k = head(q_ref, j), head(k_ref, j)
        scores = jnp.where(causal, mm(q, k, NT), 0.0)
        both = dot3(split(scores), split(uw_ref[j]))
        put(o_ref, j, both[:, :DIM])
        put(e_ref, j, q.astype(F32) * keep - both[:, DIM:])


def kernel_c(q_ref, o_ref, e_ref, s_ref, cot_ref, gain_ref, y_ref, do_ref, c_ref, dg_ref):
    gain = gain_ref[...]
    dgain = jnp.zeros((1, DIM), F32)
    for j in range(GROUP):
        iq = inv_norm(head(q_ref, j).astype(F32))
        effective = split(head(e_ref, j))
        raw = head(o_ref, j) + dot3(effective, split(s_ref[j]))
        out = raw * iq
        inv = lax.rsqrt(jnp.mean(out * out, axis=-1, keepdims=True) + 1e-05)
        unit = out * inv
        put(y_ref, j, unit * gain)
        cot = head(cot_ref, j).astype(F32)
        dgain = dgain + jnp.sum(cot * unit, axis=0, keepdims=True)
        pulled = cot * gain
        dout = inv * (pulled - unit * jnp.mean(pulled * unit, axis=-1, keepdims=True))
        draw = dout * iq
        put(do_ref, j, draw)
        c_ref[j] = dot3(effective, split(draw), TN)

    @pl.when(pl.program_id(0) == 0)
    def _():
        dg_ref[...] = jnp.zeros_like(dg_ref)

    dg_ref[...] += dgain


def kernel_d(ids_ref, q_ref, k_ref, do_ref, uw_ref, s_ref, dq_ref, u_ref, du_ref, dk_ref):
    same, ii, jj, keep, tail, through = id_masks(ids_ref)
    causal = same & (ii >= jj)
    for j in range(GROUP):
        q, k = head(q_ref, j), head(k_ref, j)
        q32 = q.astype(F32)
        state = split(s_ref[j])
        uw = uw_ref[j]
        update = uw[:, :DIM] - dot3(split(uw[:, DIM:]), state)
        draw = head(do_ref, j)
        draws = split(draw)
        scores = split(jnp.where(causal, mm(q, k, NT), 0.0))
        weights = split(jnp.where(causal, dot3(draws, split(update), NT), 0.0))
        dq = dot3(split(draw * keep), state, NT) + dot2(weights, k)
        iq = inv_norm(q32)
        dq = dq - q32 * (iq * iq * jnp.sum(q32 * dq, axis=-1, keepdims=True))
        put(dq_ref, j, dq)
        put(u_ref, j, update)
        put(du_ref, j, dot3(scores, draws, TN))
        put(dk_ref, j, dot2(weights, q, TN))


def kernel_e(
    ids_ref, k_ref, v_ref, beta_ref, th_ref, tl_ref, u_ref, du_ref, dkl_ref, s_ref, g_ref,
    dk_ref, dv_ref, db_ref,
):
    same, ii, jj, keep, tail, through = id_masks(ids_ref)
    strict = same & (ii > jj)
    lane = lax.broadcasted_iota(jnp.int32, db_ref.shape, 1)
    dbeta = jnp.zeros(db_ref.shape, F32)
    for j in range(GROUP):
        k = head(k_ref, j)
        k32 = k.astype(F32)
        ik = inv_norm(k32)
        logit = logit_of(beta_ref, j)
        rate = jax.nn.sigmoid(logit)
        update = head(u_ref, j)
        updates = split(update)
        back = split(g_ref[j])
        dupdate = head(du_ref, j) + tail * dot2r(k, back)
        dright = dot3((th_ref[j], tl_ref[j]), split(dupdate), TN)
        put(dv_ref, j, dright * (rate * ik))
        at = pl.program_id(0) * GROUP + j
        dlogit = jax.nn.sigmoid(-logit) * jnp.sum(dright * update, axis=-1, keepdims=True)
        dbeta = jnp.where(lane == at, dlogit, dbeta)
        scaled = dright * (rate * ik * ik)
        inner = split(jnp.where(strict, -dot3(split(scaled), updates, NT), 0.0))
        dk = head(dkl_ref, j) + (dot2(inner, k) + dot2(inner, k, TN))
        dk = dk + tail * dot3(updates, back, NT)
        dk = dk - dot3(split(scaled * keep), split(s_ref[j]), NT)
        dk = dk - k32 * (ik * ik * jnp.sum(k32 * dk, axis=-1, keepdims=True))
        put(dk_ref, j, dk)

    @pl.when(pl.program_id(0) == 0)
    def _():
        db_ref[...] = jnp.zeros_like(db_ref)

    db_ref[...] += dbeta


def call(kernel, ins, outs, kinds, flops, name):
    tokens = None
    for kind, arg in zip(kinds[0], ins):
        if kind == "wide":
            tokens = arg.shape[0]
    specs = {
        "wide": pl.BlockSpec((tokens, GROUP * DIM), lambda h: (0, h)),
        "state": pl.BlockSpec((GROUP, DIM, DIM), lambda h: (h, 0, 0)),
        "square": pl.BlockSpec((GROUP, tokens, tokens), lambda h: (h, 0, 0)),
        "uw": pl.BlockSpec((GROUP, tokens, 2 * DIM), lambda h: (h, 0, 0)),
        "ids": pl.BlockSpec((1, tokens), lambda h: (0, 0)),
        "beta": pl.BlockSpec((tokens, HEADS), lambda h: (0, 0)),
        "row": pl.BlockSpec((1, DIM), lambda h: (0, 0)),
    }
    return pl.pallas_call(
        kernel,
        grid=(HEADS // GROUP,),
        in_specs=[specs[kind] for kind in kinds[0]],
        out_specs=[specs[kind] for kind in kinds[1]],
        out_shape=outs,
        compiler_params=pltpu.CompilerParams(vmem_limit_bytes=48 * 1024 * 1024),
        cost_estimate=pl.CostEstimate(flops=flops, bytes_accessed=4_000_000, transcendentals=0),
        name=name,
    )(*ins)


def local(
    query_heads, key_heads, value_heads, beta_logits, segment_ids, output_cotangent, norm_gain
):
    q, k, v = query_heads[0], key_heads[0], value_heads[0]
    beta, ids, cot = beta_logits[0], segment_ids, output_cotangent[0]
    gain = norm_gain[None]
    tokens = q.shape[0]
    spans = lax.axis_size("seq")
    here = lax.axis_index("seq")
    half = spans // 2

    wide = jax.ShapeDtypeStruct((tokens, HEADS * DIM), F32)
    wide16 = jax.ShapeDtypeStruct((tokens, HEADS * DIM), BF16)
    states = jax.ShapeDtypeStruct((HEADS, DIM, DIM), F32)
    square = jax.ShapeDtypeStruct((HEADS, tokens, tokens), BF16)
    uw_shape = jax.ShapeDtypeStruct((HEADS, tokens, 2 * DIM), F32)
    unit = 2 * HEADS * tokens**3

    prior = lax.ppermute(ids[:, tokens - 1 :], "seq", [(s, s + 1) for s in range(spans - 1)])
    joined = ((prior == ids[:, :1]) & (here > 0)).astype(F32)[:, :, None]

    at, bt, th, tl, uw = call(
        kernel_a, (ids, k, v, beta), (states, states, square, square, uw_shape),
        (("ids", "wide", "wide", "beta"), ("state", "state", "square", "square", "uw")),
        20 * unit, "span_state",
    )
    o0, eff = call(
        kernel_b, (ids, q, k, uw), (wide, wide),
        (("ids", "wide", "wide", "uw"), ("wide", "wide")), 4 * unit, "span_out",
    )

    def advance(matrix, state, dims):
        return lax.dot_general(matrix, state, dims, precision=HIGHEST, preferred_element_type=F32)

    FWD = (((2,), (1,)), ((0,), (0,)))
    BWD = (((1,), (1,)), ((0,), (0,)))

    entering = jnp.zeros((HEADS, DIM, DIM), F32)
    outgoing = bt
    for turn in range(half):
        pairs = [(turn, turn + 1)]
        if turn == 0:
            pairs += [(s, s + 1) for s in range(half, spans - 1)]
        entering = entering + joined * lax.ppermute(outgoing, "seq", pairs)
        if turn < half - 1:
            outgoing = advance(at, entering, FWD) + bt

    mixed, draw, cs, dgain = call(
        kernel_c, (q, o0, eff, entering, cot, gain),
        (wide16, wide, states, jax.ShapeDtypeStruct((1, DIM), F32)),
        (("wide", "wide", "wide", "state", "wide", "row"), ("wide", "wide", "state", "row")),
        3 * unit, "span_norm",
    )
    gain_total = lax.psum(dgain[0], ("seq", "dp"))

    back = jnp.zeros((HEADS, DIM, DIM), F32)
    outgoing = joined * cs
    for turn in range(half):
        pairs = [(half - turn, half - turn - 1)]
        if turn == 0:
            pairs += [(s, s - 1) for s in range(half + 1, spans)]
        back = back + lax.ppermute(outgoing, "seq", pairs)
        if turn < half - 1:
            outgoing = joined * (advance(at, back, BWD) + cs)

    dq, update, dupdate, dkl = call(
        kernel_d, (ids, q, k, draw, uw, entering), (wide16, wide, wide, wide),
        (("ids", "wide", "wide", "wide", "uw", "state"), ("wide", "wide", "wide", "wide")),
        10 * unit, "span_query_grad",
    )
    dk, dv, dbeta = call(
        kernel_e, (ids, k, v, beta, th, tl, update, dupdate, dkl, entering, back),
        (wide16, wide16, jax.ShapeDtypeStruct((tokens, HEADS), F32)),
        (
            ("ids", "wide", "wide", "beta", "square", "square", "wide", "wide", "wide", "state",
             "state"),
            ("wide", "wide", "beta"),
        ),
        12 * unit, "span_key_grad",
    )
    return (mixed[None], dq[None], dk[None], dv[None], dbeta[None], gain_total)


def solution(mesh):
    rows = P("dp", "seq", None)
    return jax.shard_map(
        local,
        mesh=mesh,
        in_specs=(rows, rows, rows, rows, P("dp", "seq"), rows, P()),
        out_specs=(rows, rows, rows, rows, rows, P()),
        check_vma=False,
    )
```

```python
import functools

import jax
import jax.numpy as jnp
from jax import lax
from jax.experimental import pallas as pl
from jax.experimental.pallas import tpu as pltpu
from jax.sharding import PartitionSpec as P

HEADS = 8
DIM = 128
GROUP = 8
BASE = 16
HIGHEST = lax.Precision.HIGHEST
F32 = jnp.float32
BF16 = jnp.bfloat16

NN = (((1,), (0,)), ((), ()))
NT = (((1,), (1,)), ((), ()))
TN = (((0,), (0,)), ((), ()))


def split(x):
    hi = x.astype(BF16)
    return hi, (x - hi.astype(F32)).astype(BF16)


def mm(a, b, dims=NN):
    return lax.dot_general(a, b, dims, preferred_element_type=F32)


def dot3(a, b, dims=NN):
    return mm(a[0], b[0], dims) + (mm(a[0], b[1], dims) + mm(a[1], b[0], dims))


def dot2(a, b, dims=NN):
    return mm(a[0], b, dims) + mm(a[1], b, dims)


def dot2r(a, b, dims=NN):
    return mm(a, b[0], dims) + mm(a, b[1], dims)


def id_masks(ids_ref):
    row = ids_ref[...].astype(F32)
    n = row.shape[1]
    ii = lax.broadcasted_iota(jnp.int32, (n, n), 0)
    jj = lax.broadcasted_iota(jnp.int32, (n, n), 1)
    col = jnp.sum(jnp.where(ii == jj, row, 0.0), axis=1, keepdims=True)
    same = col == row
    first, last = row[:, :1], row[:, n - 1 :]
    keep = (col == first).astype(F32)
    tail = (col == last).astype(F32)
    through = (first == last).astype(F32)
    return same, ii, jj, keep, tail, through


def head(ref, j):
    return ref[:, DIM * j : DIM * (j + 1)]


def put(ref, j, value):
    ref[:, DIM * j : DIM * (j + 1)] = value.astype(ref.dtype)


def inv_norm(x):
    return lax.rsqrt(jnp.sum(x * x, axis=-1, keepdims=True) + 1e-06)


def logit_of(beta_ref, j):
    at = pl.program_id(0) * GROUP + j
    beta = jnp.transpose(beta_ref[...])
    lane = lax.broadcasted_iota(jnp.int32, beta.shape, 1)
    return jnp.sum(jnp.where(lane == at, beta, 0.0), axis=1, keepdims=True)


def base_inverses(blocks):
    n, base = DIM, BASE
    groups = n // base
    lane = lax.broadcasted_iota(jnp.int32, (base, n), 1)
    row = lax.broadcasted_iota(jnp.int32, (base, n), 0)
    compact = []
    for block in blocks:
        kept = [
            jnp.where(lane // base == g, block[g * base : (g + 1) * base], 0.0)
            for g in range(groups)
        ]
        while len(kept) > 1:
            kept = [x + y for x, y in zip(kept[0::2], kept[1::2])]
        compact.append(kept[0])
    ii = lax.broadcasted_iota(jnp.int32, (n, n), 0)
    jj = lax.broadcasted_iota(jnp.int32, (n, n), 1)
    together = ii // base == jj // base
    pick = jnp.concatenate(
        [(together & (ii % base == j)).astype(F32).astype(BF16) for j in range(base - 1)], axis=1
    )
    high, low = split(jnp.concatenate(compact, axis=0))
    columns = mm(high, pick) + mm(low, pick)
    start = (lane % base == row).astype(F32)
    ts = [start for _ in blocks]
    for j in range(base - 1):
        part = columns[:, j * n : (j + 1) * n]
        ts = [
            t - part[i * base : (i + 1) * base] * t[j : j + 1] for i, t in enumerate(ts)
        ]
    return [
        jnp.concatenate([jnp.where(lane // base == g, t, 0.0) for g in range(groups)], axis=0)
        for t in ts
    ]


def inverse(blocks):
    n = DIM
    ii = lax.broadcasted_iota(jnp.int32, (n, n), 0)
    jj = lax.broadcasted_iota(jnp.int32, (n, n), 1)

    def off(block, s):
        inside = (ii // (2 * s) == jj // (2 * s)) & (ii // s != jj // s)
        return jnp.where(inside, block, 0.0)

    ts = base_inverses(blocks)
    s = BASE
    while s < n:
        offs = [split(off(b, s)) for b in blocks]
        tss = [split(t) for t in ts]
        mids = [dot3(o, t) for o, t in zip(offs, tss)]
        mids = [split(m) for m in mids]
        ts = [t - dot3(p, m) for t, p, m in zip(ts, tss, mids)]
        s *= 2
    return ts


def kernel_a(ids_ref, k_ref, v_ref, beta_ref, at_ref, bt_ref, th_ref, tl_ref, z_ref):
    same, ii, jj, keep, tail, through = id_masks(ids_ref)
    strict = same & (ii > jj)
    heads = range(GROUP)
    ks = [head(k_ref, j) for j in heads]
    k32 = [k.astype(F32) for k in ks]
    iks = [inv_norm(k) for k in k32]
    rates = [jax.nn.sigmoid(logit_of(beta_ref, j)) for j in heads]
    cs = [r * i * i for r, i in zip(rates, iks)]
    ns = [jnp.where(strict, mm(k, k, NT), 0.0) * c for k, c in zip(ks, cs)]
    blocks = []
    for n in ns:
        blocks += [n[:DIM, :DIM], n[DIM:, DIM:]]
    ts = inverse(blocks)
    t1s = [split(t) for t in ts[0::2]]
    t2s = [split(t) for t in ts[1::2]]
    mids = [split(dot3(split(n[DIM:, :DIM]), t)) for n, t in zip(ns, t1s)]
    lows = [split(-dot3(t, m)) for t, m in zip(t2s, mids)]
    zero = jnp.zeros((DIM, DIM), BF16)
    fulls = [
        tuple(
            jnp.concatenate(
                [
                    jnp.concatenate([t1[p], zero], axis=1),
                    jnp.concatenate([lo[p], t2[p]], axis=1),
                ],
                axis=0,
            )
            for p in range(2)
        )
        for t1, t2, lo in zip(t1s, t2s, lows)
    ]
    eye = (
        lax.broadcasted_iota(jnp.int32, (DIM, DIM), 0)
        == lax.broadcasted_iota(jnp.int32, (DIM, DIM), 1)
    ).astype(F32)
    zs = [dot2r((k * tail).astype(BF16), full, TN) for k, full in zip(k32, fulls)]
    for j in heads:
        right = writes(head(v_ref, j).astype(F32), k32[j], rates[j], iks[j], keep)
        both = dot3(split(zs[j]), split(right))
        bt_ref[j] = both[:, :DIM]
        at_ref[j] = eye * through - both[:, DIM:]
        th_ref[j] = fulls[j][0]
        tl_ref[j] = fulls[j][1]
        z_ref[j] = zs[j]


def writes(value, key, rate, ik, keep):
    return jnp.concatenate([value * (rate * ik), key * (rate * ik * ik * keep)], axis=1)


def kernel_b(
    ids_ref, q_ref, k_ref, v_ref, beta_ref, th_ref, tl_ref, o_ref, e_ref, uw_ref
):
    same, ii, jj, keep, tail, through = id_masks(ids_ref)
    causal = same & (ii >= jj)
    for j in range(GROUP):
        q, k = head(q_ref, j), head(k_ref, j)
        k32 = k.astype(F32)
        rate = jax.nn.sigmoid(logit_of(beta_ref, j))
        right = writes(head(v_ref, j).astype(F32), k32, rate, inv_norm(k32), keep)
        uw = dot3((th_ref[j], tl_ref[j]), split(right))
        scores = jnp.where(causal, mm(q, k, NT), 0.0)
        both = dot3(split(scores), split(uw))
        put(o_ref, j, both[:, :DIM])
        put(e_ref, j, q.astype(F32) * keep - both[:, DIM:])
        uw_ref[j] = uw


def kernel_c(q_ref, o_ref, e_ref, s_ref, cot_ref, gain_ref, y_ref, do_ref, c_ref, dg_ref):
    gain = gain_ref[...]
    dgain = jnp.zeros((1, DIM), F32)
    for j in range(GROUP):
        iq = inv_norm(head(q_ref, j).astype(F32))
        effective = split(head(e_ref, j))
        raw = head(o_ref, j) + dot3(effective, split(s_ref[j]))
        out = raw * iq
        inv = lax.rsqrt(jnp.mean(out * out, axis=-1, keepdims=True) + 1e-05)
        unit = out * inv
        put(y_ref, j, unit * gain)
        cot = head(cot_ref, j).astype(F32)
        dgain = dgain + jnp.sum(cot * unit, axis=0, keepdims=True)
        pulled = cot * gain
        dout = inv * (pulled - unit * jnp.mean(pulled * unit, axis=-1, keepdims=True))
        draw = dout * iq
        put(do_ref, j, draw)
        c_ref[j] = dot3(effective, split(draw), TN)

    @pl.when(pl.program_id(0) == 0)
    def _():
        dg_ref[...] = jnp.zeros_like(dg_ref)

    dg_ref[...] += dgain


def kernel_d(
    ids_ref, q_ref, k_ref, th_ref, tl_ref, do_ref, uw_ref, s_ref,
    dq_ref, u_ref, dr_ref, dk_ref,
):
    same, ii, jj, keep, tail, through = id_masks(ids_ref)
    causal = same & (ii >= jj)
    for j in range(GROUP):
        q, k = head(q_ref, j), head(k_ref, j)
        q32 = q.astype(F32)
        state = split(s_ref[j])
        uw = uw_ref[j]
        update = uw[:, :DIM] - dot3(split(uw[:, DIM:]), state)
        draw = head(do_ref, j)
        draws = split(draw)
        scores = split(jnp.where(causal, mm(q, k, NT), 0.0))
        weights = split(jnp.where(causal, dot3(draws, split(update), NT), 0.0))
        dq = dot3(split(draw * keep), state, NT) + dot2(weights, k)
        iq = inv_norm(q32)
        dq = dq - q32 * (iq * iq * jnp.sum(q32 * dq, axis=-1, keepdims=True))
        put(dq_ref, j, dq)
        put(u_ref, j, update)
        dupdate = dot3(scores, draws, TN)
        put(dr_ref, j, dot3((th_ref[j], tl_ref[j]), split(dupdate), TN))
        put(dk_ref, j, dot2(weights, q, TN))


def kernel_e(
    ids_ref, k_ref, v_ref, beta_ref, z_ref, u_ref, dr_ref, dkl_ref, s_ref, g_ref,
    dk_ref, dv_ref, db_ref,
):
    same, ii, jj, keep, tail, through = id_masks(ids_ref)
    strict = same & (ii > jj)
    shape = (db_ref.shape[1], db_ref.shape[0])
    lane = lax.broadcasted_iota(jnp.int32, shape, 1)
    dbeta = jnp.zeros(shape, F32)
    heads = range(GROUP)
    for j in heads:
        k = head(k_ref, j)
        k32 = k.astype(F32)
        ik = inv_norm(k32)
        logit = logit_of(beta_ref, j)
        rate = jax.nn.sigmoid(logit)
        update = head(u_ref, j)
        updates = split(update)
        back = split(g_ref[j])
        dright = head(dr_ref, j) + dot3(split(z_ref[j]), back, TN)
        put(dv_ref, j, dright * (rate * ik))
        at = pl.program_id(0) * GROUP + j
        dlogit = jax.nn.sigmoid(-logit) * jnp.sum(dright * update, axis=-1, keepdims=True)
        dbeta = jnp.where(lane == at, dlogit, dbeta)
        scaled = dright * (rate * ik * ik)
        inner = split(jnp.where(strict, -dot3(split(scaled), updates, NT), 0.0))
        dk = head(dkl_ref, j) + (dot2(inner, k) + dot2(inner, k, TN))
        dk = dk + tail * dot3(updates, back, NT)
        dk = dk - dot3(split(scaled * keep), split(s_ref[j]), NT)
        dk = dk - k32 * (ik * ik * jnp.sum(k32 * dk, axis=-1, keepdims=True))
        put(dk_ref, j, dk)

    @pl.when(pl.program_id(0) == 0)
    def _():
        db_ref[...] = jnp.zeros_like(db_ref)

    db_ref[...] += jnp.transpose(dbeta)


def exchange_sum(value, axis):
    size = lax.axis_size(axis)
    step = 1
    while step < size:
        value = value + lax.ppermute(value, axis, [(i, i ^ step) for i in range(size)])
        step *= 2
    return value


def call(kernel, ins, outs, kinds, flops, name):
    tokens = None
    for kind, arg in zip(kinds[0], ins):
        if kind == "wide":
            tokens = arg.shape[0]
    specs = {
        "wide": pl.BlockSpec((tokens, GROUP * DIM), lambda h: (0, h)),
        "state": pl.BlockSpec((GROUP, DIM, DIM), lambda h: (h, 0, 0)),
        "square": pl.BlockSpec((GROUP, tokens, tokens), lambda h: (h, 0, 0)),
        "z": pl.BlockSpec((GROUP, DIM, tokens), lambda h: (h, 0, 0)),
        "uw": pl.BlockSpec((GROUP, tokens, 2 * DIM), lambda h: (h, 0, 0)),
        "ids": pl.BlockSpec((1, tokens), lambda h: (0, 0)),
        "beta": pl.BlockSpec((HEADS, tokens), lambda h: (0, 0)),
        "row": pl.BlockSpec((1, DIM), lambda h: (0, 0)),
    }
    return pl.pallas_call(
        kernel,
        grid=(HEADS // GROUP,),
        in_specs=[specs[kind] for kind in kinds[0]],
        out_specs=[specs[kind] for kind in kinds[1]],
        out_shape=outs,
        compiler_params=pltpu.CompilerParams(vmem_limit_bytes=16 * 1024 * 1024),
        cost_estimate=pl.CostEstimate(flops=flops, bytes_accessed=4_000_000, transcendentals=0),
        name=name,
    )(*ins)


def local(
    query_heads, key_heads, value_heads, beta_logits, segment_ids, output_cotangent, norm_gain
):
    q, k, v = query_heads[0], key_heads[0], value_heads[0]
    beta, ids, cot = jnp.transpose(beta_logits[0]), segment_ids, output_cotangent[0]
    gain = norm_gain[None]
    tokens = q.shape[0]
    spans = lax.axis_size("seq")
    here = lax.axis_index("seq")
    half = spans // 2

    wide = jax.ShapeDtypeStruct((tokens, HEADS * DIM), F32)
    wide16 = jax.ShapeDtypeStruct((tokens, HEADS * DIM), BF16)
    states = jax.ShapeDtypeStruct((HEADS, DIM, DIM), F32)
    square = jax.ShapeDtypeStruct((HEADS, tokens, tokens), BF16)
    uw_shape = jax.ShapeDtypeStruct((HEADS, tokens, 2 * DIM), F32)
    unit = 2 * HEADS * tokens**3

    prior = lax.ppermute(ids[:, tokens - 1 :], "seq", [(s, s + 1) for s in range(spans - 1)])
    joined = ((prior == ids[:, :1]) & (here > 0)).astype(F32)[:, :, None]

    z_shape = jax.ShapeDtypeStruct((HEADS, DIM, tokens), F32)
    at, bt, th, tl, z = call(
        kernel_a, (ids, k, v, beta), (states, states, square, square, z_shape),
        (("ids", "wide", "wide", "beta"), ("state", "state", "square", "square", "z")),
        20 * unit, "span_state",
    )
    o0, eff, uw = call(
        kernel_b, (ids, q, k, v, beta, th, tl), (wide, wide, uw_shape),
        (("ids", "wide", "wide", "wide", "beta", "square", "square"), ("wide", "wide", "uw")),
        8 * unit, "span_out",
    )

    def advance(matrix, state, dims):
        return lax.dot_general(matrix, state, dims, precision=HIGHEST, preferred_element_type=F32)

    FWD = (((2,), (1,)), ((0,), (0,)))
    BWD = (((1,), (1,)), ((0,), (0,)))

    entering = jnp.zeros((HEADS, DIM, DIM), F32)
    outgoing = bt
    for turn in range(half):
        pairs = [(turn, turn + 1)]
        if turn == 0:
            pairs += [(s, s + 1) for s in range(half, spans - 1)]
        entering = entering + joined * lax.ppermute(outgoing, "seq", pairs)
        if turn < half - 1:
            outgoing = advance(at, entering, FWD) + bt

    mixed, draw, cs, dgain = call(
        kernel_c, (q, o0, eff, entering, cot, gain),
        (wide16, wide, states, jax.ShapeDtypeStruct((1, DIM), F32)),
        (("wide", "wide", "wide", "state", "wide", "row"), ("wide", "wide", "state", "row")),
        3 * unit, "span_norm",
    )
    gain_total = exchange_sum(exchange_sum(dgain, "seq"), "dp")[0]

    back = jnp.zeros((HEADS, DIM, DIM), F32)
    outgoing = joined * cs
    for turn in range(half):
        pairs = [(half - turn, half - turn - 1)]
        if turn == 0:
            pairs += [(s, s - 1) for s in range(half + 1, spans)]
        back = back + lax.ppermute(outgoing, "seq", pairs)
        if turn < half - 1:
            outgoing = joined * (advance(at, back, BWD) + cs)

    dq, update, dright, dkl = call(
        kernel_d, (ids, q, k, th, tl, draw, uw, entering), (wide16, wide, wide, wide),
        (
            ("ids", "wide", "wide", "square", "square", "wide", "uw", "state"),
            ("wide", "wide", "wide", "wide"),
        ),
        12 * unit, "span_query_grad",
    )
    dk, dv, dbeta = call(
        kernel_e, (ids, k, v, beta, z, update, dright, dkl, entering, back),
        (wide16, wide16, jax.ShapeDtypeStruct((HEADS, tokens), F32)),
        (
            ("ids", "wide", "wide", "beta", "z", "wide", "wide", "wide", "state", "state"),
            ("wide", "wide", "beta"),
        ),
        12 * unit, "span_key_grad",
    )
    return (mixed[None], dq[None], dk[None], dv[None], jnp.transpose(dbeta)[None], gain_total)


def solution(mesh):
    rows = P("dp", "seq", None)
    return jax.shard_map(
        local,
        mesh=mesh,
        in_specs=(rows, rows, rows, rows, P("dp", "seq"), rows, P()),
        out_specs=(rows, rows, rows, rows, rows, P()),
        check_vma=False,
    )
```

```python
import functools

import jax
import jax.numpy as jnp
from jax import lax
from jax.experimental import pallas as pl
from jax.experimental.pallas import tpu as pltpu
from jax.sharding import PartitionSpec as P

HEADS = 8
DIM = 128
BASE = 16
ROWS = HEADS * DIM
META = 8
HIGHEST = lax.Precision.HIGHEST
F32 = jnp.float32
BF16 = jnp.bfloat16

NN = (((1,), (0,)), ((), ()))
NT = (((1,), (1,)), ((), ()))
TN = (((0,), (0,)), ((), ()))


def split(x):
    hi = x.astype(BF16)
    return hi, (x - hi.astype(F32)).astype(BF16)


def mm(a, b, dims=NN):
    return lax.dot_general(a, b, dims, preferred_element_type=F32)


def dot3(a, b, dims=NN):
    return mm(a[0], b[0], dims) + (mm(a[0], b[1], dims) + mm(a[1], b[0], dims))


def dot2(a, b, dims=NN):
    return mm(a[0], b, dims) + mm(a[1], b, dims)


def dot2r(a, b, dims=NN):
    return mm(a, b[0], dims) + mm(a, b[1], dims)


def id_masks(ids_ref):
    row = ids_ref[...].astype(F32)
    n = row.shape[1]
    ii = lax.broadcasted_iota(jnp.int32, (n, n), 0)
    jj = lax.broadcasted_iota(jnp.int32, (n, n), 1)
    col = jnp.sum(jnp.where(ii == jj, row, 0.0), axis=1, keepdims=True)
    same = col == row
    first, last = row[:, :1], row[:, n - 1 :]
    keep = (col == first).astype(F32)
    tail = (col == last).astype(F32)
    through = (first == last).astype(F32)
    return same, ii, jj, keep, tail, through


def head(ref, j):
    return ref[:, DIM * j : DIM * (j + 1)]


def block(ref, j):
    return ref.at[DIM * j : DIM * (j + 1)]


def notes(*values):
    lane = lax.broadcasted_iota(jnp.int32, (META, DIM), 1)
    out = jnp.zeros((META, DIM), F32)
    for at, value in enumerate(values):
        out = jnp.where(lane == at, value, out)
    return out


def note(rows, at):
    return rows[:1, at : at + 1]


def put(ref, j, value):
    ref[:, DIM * j : DIM * (j + 1)] = value.astype(ref.dtype)


def inv_norm(x):
    return lax.rsqrt(jnp.sum(x * x, axis=-1, keepdims=True) + 1e-06)


def logit_of(beta_ref, j):
    beta = jnp.transpose(beta_ref[...])
    lane = lax.broadcasted_iota(jnp.int32, beta.shape, 1)
    return jnp.sum(jnp.where(lane == j, beta, 0.0), axis=1, keepdims=True)


def base_inverses(blocks):
    n, base = DIM, BASE
    groups = n // base
    lane = lax.broadcasted_iota(jnp.int32, (base, n), 1)
    row = lax.broadcasted_iota(jnp.int32, (base, n), 0)
    compact = []
    for block in blocks:
        kept = [
            jnp.where(lane // base == g, block[g * base : (g + 1) * base], 0.0)
            for g in range(groups)
        ]
        while len(kept) > 1:
            kept = [x + y for x, y in zip(kept[0::2], kept[1::2])]
        compact.append(kept[0])
    ii = lax.broadcasted_iota(jnp.int32, (n, n), 0)
    jj = lax.broadcasted_iota(jnp.int32, (n, n), 1)
    together = ii // base == jj // base
    pick = jnp.concatenate(
        [(together & (ii % base == j)).astype(F32).astype(BF16) for j in range(base - 1)], axis=1
    )
    high, low = split(jnp.concatenate(compact, axis=0))
    columns = mm(high, pick) + mm(low, pick)
    start = (lane % base == row).astype(F32)
    ts = [start for _ in blocks]
    for j in range(base - 1):
        part = columns[:, j * n : (j + 1) * n]
        ts = [
            t - part[i * base : (i + 1) * base] * t[j : j + 1] for i, t in enumerate(ts)
        ]
    return [
        jnp.concatenate([jnp.where(lane // base == g, t, 0.0) for g in range(groups)], axis=0)
        for t in ts
    ]


def inverse(blocks):
    n = DIM
    ii = lax.broadcasted_iota(jnp.int32, (n, n), 0)
    jj = lax.broadcasted_iota(jnp.int32, (n, n), 1)

    def off(block, s):
        inside = (ii // (2 * s) == jj // (2 * s)) & (ii // s != jj // s)
        return jnp.where(inside, block, 0.0)

    ts = base_inverses(blocks)
    s = BASE
    while s < n:
        offs = [split(off(b, s)) for b in blocks]
        tss = [split(t) for t in ts]
        mids = [dot3(o, t) for o, t in zip(offs, tss)]
        mids = [split(m) for m in mids]
        ts = [t - dot3(p, m) for t, p, m in zip(ts, tss, mids)]
        s *= 2
    return ts


def kernel_a(ids_ref, k_ref, v_ref, beta_ref, ab_ref, th_ref, tl_ref, z_ref):
    same, ii, jj, keep, tail, through = id_masks(ids_ref)
    strict = same & (ii > jj)
    heads = range(HEADS)
    ks = [head(k_ref, j) for j in heads]
    k32 = [k.astype(F32) for k in ks]
    iks = [inv_norm(k) for k in k32]
    rates = [jax.nn.sigmoid(logit_of(beta_ref, j)) for j in heads]
    cs = [r * i * i for r, i in zip(rates, iks)]
    ns = [jnp.where(strict, mm(k, k, NT), 0.0) * c for k, c in zip(ks, cs)]
    blocks = []
    for n in ns:
        blocks += [n[:DIM, :DIM], n[DIM:, DIM:]]
    ts = inverse(blocks)
    t1s = [split(t) for t in ts[0::2]]
    t2s = [split(t) for t in ts[1::2]]
    mids = [split(dot3(split(n[DIM:, :DIM]), t)) for n, t in zip(ns, t1s)]
    lows = [split(-dot3(t, m)) for t, m in zip(t2s, mids)]
    zero = jnp.zeros((DIM, DIM), BF16)
    fulls = [
        tuple(
            jnp.concatenate(
                [
                    jnp.concatenate([t1[p], zero], axis=1),
                    jnp.concatenate([lo[p], t2[p]], axis=1),
                ],
                axis=0,
            )
            for p in range(2)
        )
        for t1, t2, lo in zip(t1s, t2s, lows)
    ]
    eye = (
        lax.broadcasted_iota(jnp.int32, (DIM, DIM), 0)
        == lax.broadcasted_iota(jnp.int32, (DIM, DIM), 1)
    ).astype(F32)
    zs = [dot2r((k * tail).astype(BF16), full, TN) for k, full in zip(k32, fulls)]
    for j in heads:
        right = writes(head(v_ref, j).astype(F32), k32[j], rates[j], iks[j], keep)
        both = dot3(split(zs[j]), split(right))
        block(ab_ref, j)[...] = eye * through - both[:, DIM:]
        block(ab_ref, HEADS + j)[...] = both[:, :DIM]
        th_ref[j] = fulls[j][0]
        tl_ref[j] = fulls[j][1]
        z_ref[j] = zs[j]
    row = ids_ref[...].astype(F32)
    ab_ref[2 * ROWS :] = notes(row[:, :1], row[:, row.shape[1] - 1 :], 1.0)


def writes(value, key, rate, ik, keep):
    return jnp.concatenate([value * (rate * ik), key * (rate * ik * ik * keep)], axis=1)


def kernel_b(
    ids_ref, q_ref, k_ref, v_ref, beta_ref, th_ref, tl_ref, o_ref, e_ref, uw_ref
):
    same, ii, jj, keep, tail, through = id_masks(ids_ref)
    causal = same & (ii >= jj)
    for j in range(HEADS):
        q, k = head(q_ref, j), head(k_ref, j)
        k32 = k.astype(F32)
        rate = jax.nn.sigmoid(logit_of(beta_ref, j))
        right = writes(head(v_ref, j).astype(F32), k32, rate, inv_norm(k32), keep)
        uw = dot3((th_ref[j], tl_ref[j]), split(right))
        scores = jnp.where(causal, mm(q, k, NT), 0.0)
        both = dot3(split(scores), split(uw))
        put(o_ref, j, both[:, :DIM])
        put(e_ref, j, q.astype(F32) * keep - both[:, DIM:])
        uw_ref[j] = uw


def kernel_join(ids_ref, ab_ref, prev_ref, both_ref, mid_ref, map_ref):
    row = ids_ref[...].astype(F32)
    last = row[:, row.shape[1] - 1 :]
    before = prev_ref[2 * ROWS :]
    joined = (note(before, 1) == row[:, :1]).astype(F32)
    for j in range(HEADS):
        right = jnp.concatenate(
            [block(prev_ref, j)[...], block(prev_ref, HEADS + j)[...]], axis=1
        )
        made = joined * dot3(split(block(ab_ref, j)[...]), split(right))
        matrix, offset = made[:, :DIM], made[:, DIM:] + block(ab_ref, HEADS + j)[...]
        block(both_ref, j)[...] = matrix
        block(map_ref, j)[...] = matrix
        block(both_ref, HEADS + j)[...] = offset
        block(mid_ref, j)[...] = offset
    tail = notes(note(before, 0), last, 1.0)
    both_ref[2 * ROWS :] = tail
    mid_ref[ROWS:] = tail


def kernel_c(
    ids_ref, q_ref, o_ref, e_ref, p1_ref, p3_ref, m2_ref, m4_ref, m5_ref, cot_ref, gain_ref,
    y_ref, do_ref, c_ref, s_ref, dg_ref,
):
    first = ids_ref[...].astype(F32)[:, :1]
    before = p1_ref[2 * ROWS :] + p3_ref[2 * ROWS :]
    middle = m2_ref[ROWS:] + m4_ref[ROWS:] + m5_ref[ROWS:]
    known = note(before, 2)
    inner = (note(middle, 1) == note(before, 0)).astype(F32)
    direct = (1.0 - known) * (note(middle, 1) == first).astype(F32)
    joined = known * (note(before, 1) == first).astype(F32)
    states = []
    for j in range(HEADS):
        mid = block(m2_ref, j)[...] + block(m4_ref, j)[...] + block(m5_ref, j)[...]
        matrix = block(p1_ref, j)[...] + block(p3_ref, j)[...]
        offset = block(p1_ref, HEADS + j)[...] + block(p3_ref, HEADS + j)[...]
        made = dot3(split(matrix), split(inner * mid)) + offset
        states.append(joined * made + direct * mid)
        s_ref[j] = states[j]
    norm_part(
        states, joined + direct, q_ref, o_ref, e_ref, cot_ref, gain_ref, y_ref, do_ref, c_ref,
        dg_ref,
    )


def kernel_c_known(
    joined_ref, q_ref, o_ref, e_ref, s_ref, cot_ref, gain_ref, y_ref, do_ref, c_ref, dg_ref
):
    states = [s_ref[j] for j in range(HEADS)]
    norm_part(
        states, joined_ref[...], q_ref, o_ref, e_ref, cot_ref, gain_ref, y_ref, do_ref, c_ref,
        dg_ref,
    )


def norm_part(
    states, joined, q_ref, o_ref, e_ref, cot_ref, gain_ref, y_ref, do_ref, c_ref, dg_ref
):
    gain = gain_ref[...]
    dgain = jnp.zeros((1, DIM), F32)
    for j in range(HEADS):
        iq = inv_norm(head(q_ref, j).astype(F32))
        effective = split(head(e_ref, j))
        raw = head(o_ref, j) + dot3(effective, split(states[j]))
        out = raw * iq
        inv = lax.rsqrt(jnp.mean(out * out, axis=-1, keepdims=True) + 1e-05)
        unit = out * inv
        put(y_ref, j, unit * gain)
        cot = head(cot_ref, j).astype(F32)
        dgain = dgain + jnp.sum(cot * unit, axis=0, keepdims=True)
        pulled = cot * gain
        dout = inv * (pulled - unit * jnp.mean(pulled * unit, axis=-1, keepdims=True))
        draw = dout * iq
        put(do_ref, j, draw)
        block(c_ref, j)[...] = joined * dot3(effective, split(draw), TN)
    c_ref[ROWS:] = notes(joined)
    dg_ref[...] = dgain


def kernel_back(ab_ref, c_ref, back_ref, out_ref):
    joined = note(c_ref[ROWS:], 0)
    for j in range(HEADS):
        made = dot3(split(block(ab_ref, j)[...]), split(block(back_ref, j)[...]), TN)
        block(out_ref, j)[...] = block(c_ref, j)[...] + joined * made
    out_ref[ROWS:] = c_ref[ROWS:]


def kernel_back_far(ab_ref, c_ref, map_ref, h_ref, far_ref, near_ref, g_ref, out_ref):
    joined = note(c_ref[ROWS:], 0)
    beyond = note(h_ref[ROWS:], 0)
    for j in range(HEADS):
        far = dot3(split(block(map_ref, j)[...]), split(block(far_ref, j)[...]), TN)
        back = block(near_ref, j)[...] + block(h_ref, j)[...] + beyond * far
        g_ref[j] = back
        made = dot3(split(block(ab_ref, j)[...]), split(back), TN)
        block(out_ref, j)[...] = block(c_ref, j)[...] + joined * made


def kernel_d(
    ids_ref, q_ref, k_ref, th_ref, tl_ref, do_ref, uw_ref, s_ref,
    dq_ref, u_ref, dr_ref, dk_ref,
):
    same, ii, jj, keep, tail, through = id_masks(ids_ref)
    causal = same & (ii >= jj)
    for j in range(HEADS):
        q, k = head(q_ref, j), head(k_ref, j)
        q32 = q.astype(F32)
        state = split(s_ref[j])
        uw = uw_ref[j]
        update = uw[:, :DIM] - dot3(split(uw[:, DIM:]), state)
        draw = head(do_ref, j)
        draws = split(draw)
        scores = split(jnp.where(causal, mm(q, k, NT), 0.0))
        weights = split(jnp.where(causal, dot3(draws, split(update), NT), 0.0))
        dq = dot3(split(draw * keep), state, NT) + dot2(weights, k)
        iq = inv_norm(q32)
        dq = dq - q32 * (iq * iq * jnp.sum(q32 * dq, axis=-1, keepdims=True))
        put(dq_ref, j, dq)
        put(u_ref, j, update)
        dupdate = dot3(scores, draws, TN)
        put(dr_ref, j, dot3((th_ref[j], tl_ref[j]), split(dupdate), TN))
        put(dk_ref, j, dot2(weights, q, TN))


def kernel_e(
    ids_ref, k_ref, v_ref, beta_ref, z_ref, u_ref, dr_ref, dkl_ref, s_ref, g_ref, h_ref,
    dk_ref, dv_ref, db_ref,
):
    same, ii, jj, keep, tail, through = id_masks(ids_ref)
    strict = same & (ii > jj)
    shape = (db_ref.shape[1], db_ref.shape[0])
    lane = lax.broadcasted_iota(jnp.int32, shape, 1)
    dbeta = jnp.zeros(shape, F32)
    heads = range(HEADS)
    for j in heads:
        k = head(k_ref, j)
        k32 = k.astype(F32)
        ik = inv_norm(k32)
        logit = logit_of(beta_ref, j)
        rate = jax.nn.sigmoid(logit)
        update = head(u_ref, j)
        updates = split(update)
        back = split(g_ref[j] + block(h_ref, j)[...])
        dright = head(dr_ref, j) + dot3(split(z_ref[j]), back, TN)
        put(dv_ref, j, dright * (rate * ik))
        dlogit = jax.nn.sigmoid(-logit) * jnp.sum(dright * update, axis=-1, keepdims=True)
        dbeta = jnp.where(lane == j, dlogit, dbeta)
        scaled = dright * (rate * ik * ik)
        inner = split(jnp.where(strict, -dot3(split(scaled), updates, NT), 0.0))
        dk = head(dkl_ref, j) + (dot2(inner, k) + dot2(inner, k, TN))
        dk = dk + tail * dot3(updates, back, NT)
        dk = dk - dot3(split(scaled * keep), split(s_ref[j]), NT)
        dk = dk - k32 * (ik * ik * jnp.sum(k32 * dk, axis=-1, keepdims=True))
        put(dk_ref, j, dk)

    db_ref[...] = jnp.transpose(dbeta)


def exchange_sum(value, axis):
    size = lax.axis_size(axis)
    step = 1
    while step < size:
        value = value + lax.ppermute(value, axis, [(i, i ^ step) for i in range(size)])
        step *= 2
    return value


def call(kernel, ins, outs, flops, name, limit=16):
    return pl.pallas_call(
        kernel,
        out_shape=outs,
        compiler_params=pltpu.CompilerParams(vmem_limit_bytes=limit * 1024 * 1024),
        cost_estimate=pl.CostEstimate(flops=flops, bytes_accessed=4_000_000, transcendentals=0),
        name=name,
    )(*ins)


def shape(*sizes, dtype=F32):
    return jax.ShapeDtypeStruct(sizes, dtype)


def send(value, pairs):
    return lax.ppermute(value, "seq", pairs)


def relay_forward(ab, ids, spans):
    half = spans // 2
    at = ab[:ROWS].reshape(HEADS, DIM, DIM)
    bt = ab[ROWS : 2 * ROWS].reshape(HEADS, DIM, DIM)
    prior = send(ids[:, ids.shape[1] - 1 :], [(s, s + 1) for s in range(spans - 1)])
    joined = (prior == ids[:, :1]).astype(F32)
    entering = jnp.zeros((HEADS, DIM, DIM), F32)
    outgoing = bt
    for turn in range(half):
        pairs = [(turn, turn + 1)]
        if turn == 0:
            pairs += [(s, s + 1) for s in range(half, spans - 1)]
        entering = entering + joined[:, :, None] * send(outgoing, pairs)
        if turn < half - 1:
            dims = (((2,), (1,)), ((0,), (0,)))
            outgoing = lax.dot_general(at, entering, dims, precision=HIGHEST) + bt
    return entering, joined


def relay_backward(ab, c, spans):
    half = spans // 2
    at = ab[:ROWS].reshape(HEADS, DIM, DIM)
    joined = c[ROWS : ROWS + 1, :1]
    cs = c[:ROWS].reshape(HEADS, DIM, DIM)
    back = jnp.zeros((HEADS, DIM, DIM), F32)
    outgoing = cs
    for turn in range(half):
        pairs = [(half - turn, half - turn - 1)]
        if turn == 0:
            pairs += [(s, s - 1) for s in range(half + 1, spans)]
        back = back + send(outgoing, pairs)
        if turn < half - 1:
            dims = (((1,), (1,)), ((0,), (0,)))
            outgoing = lax.dot_general(at, back, dims, precision=HIGHEST) * joined + cs
    return back


def local(
    query_heads, key_heads, value_heads, beta_logits, segment_ids, output_cotangent, norm_gain
):
    q, k, v = query_heads[0], key_heads[0], value_heads[0]
    beta, ids, cot = jnp.transpose(beta_logits[0]), segment_ids, output_cotangent[0]
    gain = norm_gain[None]
    tokens = q.shape[0]
    spans = lax.axis_size("seq")
    short = spans == 8

    wide, wide16 = shape(tokens, ROWS), shape(tokens, ROWS, dtype=BF16)
    states = shape(HEADS, DIM, DIM)
    square = shape(HEADS, tokens, tokens, dtype=BF16)
    one, two = shape(ROWS + META, DIM), shape(2 * ROWS + META, DIM)
    row = shape(1, DIM)
    unit = 2 * HEADS * tokens**3

    ab, th, tl, z = call(
        kernel_a, (ids, k, v, beta), (two, square, square, shape(HEADS, DIM, tokens)),
        20 * unit, "span_state", 60,
    )
    if short:
        r1 = send(ab, [(0, 1), (2, 3), (4, 5), (5, 6), (6, 7)])
        pair, mid, pair_map = call(
            kernel_join, (ids, ab, r1), (two, one, shape(ROWS, DIM)), unit, "join"
        )
        r3 = send(pair, [(3, 4)])
        r2 = send(mid, [(1, 4)])
        r4 = send(mid, [(1, 2)])
    o0, eff, uw = call(
        kernel_b, (ids, q, k, v, beta, th, tl),
        (wide, wide, shape(HEADS, tokens, 2 * DIM)), 8 * unit, "span_out",
    )
    if short:
        r5 = send(r4, [(2, 3)])
        far_map = send(pair_map, [(3, 1)])
        mixed, draw, c, entering, dgain = call(
            kernel_c, (ids, q, o0, eff, r1, r3, r2, r4, r5, cot, gain),
            (wide16, wide, one, states, row), 4 * unit, "span_norm",
        )
        n1 = send(c, [(3, 2)])
        n3 = send(c, [(4, 1)])
        n4 = send(c, [(4, 3), (5, 4), (6, 5), (7, 6)])
        h = call(kernel_back, (ab, c, n1), one, unit, "back")
        n2 = send(h, [(2, 1)])
    else:
        entering, joined = relay_forward(ab, ids, spans)
        mixed, draw, c, dgain = call(
            kernel_c_known, (joined, q, o0, eff, entering, cot, gain),
            (wide16, wide, one, row), 4 * unit, "span_norm",
        )
    dq, update, dright, dkl = call(
        kernel_d, (ids, q, k, th, tl, draw, uw, entering), (wide16, wide, wide, wide),
        12 * unit, "span_query_grad",
    )
    if short:
        back, last = call(
            kernel_back_far, (ab, c, far_map, n2, n3, n4), (states, shape(ROWS, DIM)), unit,
            "back_far",
        )
        far = send(last, [(1, 0), (3, 2)])
        last, dgain = lax.optimization_barrier((last, dgain))
    else:
        back = relay_backward(ab, c, spans)
        far = jnp.zeros((ROWS, DIM), F32)
    gain_total = exchange_sum(exchange_sum(dgain, "seq"), "dp")[0]
    dk, dv, dbeta = call(
        kernel_e, (ids, k, v, beta, z, update, dright, dkl, entering, back, far),
        (wide16, wide16, shape(HEADS, tokens)), 12 * unit, "span_key_grad",
    )
    return (mixed[None], dq[None], dk[None], dv[None], jnp.transpose(dbeta)[None], gain_total)


def solution(mesh):
    rows = P("dp", "seq", None)
    return jax.shard_map(
        local,
        mesh=mesh,
        in_specs=(rows, rows, rows, rows, P("dp", "seq"), rows, P()),
        out_specs=(rows, rows, rows, rows, rows, P()),
        check_vma=False,
    )
```

```python
import functools

import jax
import jax.numpy as jnp
from jax import lax
from jax.experimental import pallas as pl
from jax.experimental.pallas import tpu as pltpu
from jax.sharding import PartitionSpec as P

HEADS = 8
DIM = 128
BASE = 16
ROWS = HEADS * DIM
META = 8
HIGHEST = lax.Precision.HIGHEST
F32 = jnp.float32
BF16 = jnp.bfloat16

NN = (((1,), (0,)), ((), ()))
NT = (((1,), (1,)), ((), ()))
TN = (((0,), (0,)), ((), ()))


def split(x):
    hi = x.astype(BF16)
    return hi, (x - hi.astype(F32)).astype(BF16)


def mm(a, b, dims=NN):
    return lax.dot_general(a, b, dims, preferred_element_type=F32)


def dot3(a, b, dims=NN):
    return mm(a[0], b[0], dims) + (mm(a[0], b[1], dims) + mm(a[1], b[0], dims))


def dot2(a, b, dims=NN):
    return mm(a[0], b, dims) + mm(a[1], b, dims)


def dot2r(a, b, dims=NN):
    return mm(a, b[0], dims) + mm(a, b[1], dims)


def cat(parts, axis):
    return jnp.concatenate(parts, axis=axis)


def pack3(a, b):
    left = cat([a[0], a[1]], 1)
    right = cat([cat([b[0], b[1]], 1), cat([b[0], jnp.zeros_like(b[0])], 1)], 0)
    out = mm(left, right)
    return out[:, :DIM] + out[:, DIM:]


def pack3_nt(a, b):
    left = cat([a[0], a[1]], 1)
    right = cat([cat([b[0], b[0]], 1), cat([b[1], jnp.zeros_like(b[1])], 1)], 0)
    out = mm(left, right, NT)
    return out[:, :DIM] + out[:, DIM:]


def outer3(a, b):
    return mm(cat([a[0], a[1]], 1), cat([b[0], b[0]], 1), NT) + mm(a[0], b[1], NT)


def wide3(a, b, dims=NN):
    out = mm(a[0], cat([b[0], b[1]], 1), dims)
    return out[:, :DIM] + (out[:, DIM:] + mm(a[1], b[0], dims))


def id_masks(ids_ref):
    row = ids_ref[...].astype(F32)
    n = row.shape[1]
    ii = lax.broadcasted_iota(jnp.int32, (n, n), 0)
    jj = lax.broadcasted_iota(jnp.int32, (n, n), 1)
    col = jnp.sum(jnp.where(ii == jj, row, 0.0), axis=1, keepdims=True)
    same = col == row
    first, last = row[:, :1], row[:, n - 1 :]
    keep = (col == first).astype(F32)
    tail = (col == last).astype(F32)
    through = (first == last).astype(F32)
    return same, ii, jj, keep, tail, through


def head(ref, j):
    return ref[:, DIM * j : DIM * (j + 1)]


def block(ref, j):
    return ref.at[DIM * j : DIM * (j + 1)]


def notes(*values):
    lane = lax.broadcasted_iota(jnp.int32, (META, DIM), 1)
    out = jnp.zeros((META, DIM), F32)
    for at, value in enumerate(values):
        out = jnp.where(lane == at, value, out)
    return out


def note(rows, at):
    return rows[:1, at : at + 1]


def put(ref, j, value):
    ref[:, DIM * j : DIM * (j + 1)] = value.astype(ref.dtype)


def inv_norm(x):
    return lax.rsqrt(jnp.sum(x * x, axis=-1, keepdims=True) + 1e-06)


def logit_of(beta_ref, j):
    beta = jnp.transpose(beta_ref[...])
    lane = lax.broadcasted_iota(jnp.int32, beta.shape, 1)
    return jnp.sum(jnp.where(lane == j, beta, 0.0), axis=1, keepdims=True)


def base_inverses(blocks):
    n, base = DIM, BASE
    groups = n // base
    lane = lax.broadcasted_iota(jnp.int32, (base, n), 1)
    row = lax.broadcasted_iota(jnp.int32, (base, n), 0)
    compact = []
    for block in blocks:
        kept = [
            jnp.where(lane // base == g, block[g * base : (g + 1) * base], 0.0)
            for g in range(groups)
        ]
        while len(kept) > 1:
            kept = [x + y for x, y in zip(kept[0::2], kept[1::2])]
        compact.append(kept[0])
    ii = lax.broadcasted_iota(jnp.int32, (n, n), 0)
    jj = lax.broadcasted_iota(jnp.int32, (n, n), 1)
    together = ii // base == jj // base
    pick = jnp.concatenate(
        [(together & (ii % base == j)).astype(F32).astype(BF16) for j in range(base - 1)], axis=1
    )
    high, low = split(jnp.concatenate(compact, axis=0))
    columns = mm(high, pick) + mm(low, pick)
    start = (lane % base == row).astype(F32)
    ts = [start for _ in blocks]
    for j in range(base - 1):
        part = columns[:, j * n : (j + 1) * n]
        ts = [
            t - part[i * base : (i + 1) * base] * t[j : j + 1] for i, t in enumerate(ts)
        ]
    return [
        jnp.concatenate([jnp.where(lane // base == g, t, 0.0) for g in range(groups)], axis=0)
        for t in ts
    ]


def inverse(blocks):
    n = DIM
    ii = lax.broadcasted_iota(jnp.int32, (n, n), 0)
    jj = lax.broadcasted_iota(jnp.int32, (n, n), 1)

    def off(block, s):
        inside = (ii // (2 * s) == jj // (2 * s)) & (ii // s != jj // s)
        return jnp.where(inside, block, 0.0)

    ts = base_inverses(blocks)
    s = BASE
    while s < n:
        offs = [split(off(b, s)) for b in blocks]
        tss = [split(t) for t in ts]
        mids = [dot3(o, t) for o, t in zip(offs, tss)]
        mids = [split(m) for m in mids]
        ts = [t - dot3(p, m) for t, p, m in zip(ts, tss, mids)]
        s *= 2
    return ts


def kernel_a(
    ids_in, k_in, v_in, beta_in, ab_ref, th_ref, tl_ref, z_ref,
    ids_ref, k_ref, v_ref, beta_ref, sems,
):
    copies = [
        pltpu.make_async_copy(source, target, sems.at[at])
        for at, (source, target) in enumerate(
            ((ids_in, ids_ref), (k_in, k_ref), (beta_in, beta_ref), (v_in, v_ref))
        )
    ]
    for copy in copies:
        copy.start()
    for copy in copies[:3]:
        copy.wait()
    same, ii, jj, keep, tail, through = id_masks(ids_ref)
    strict = same & (ii > jj)
    heads = range(HEADS)
    ks = [head(k_ref, j) for j in heads]
    k32 = [k.astype(F32) for k in ks]
    iks = [inv_norm(k) for k in k32]
    rates = [jax.nn.sigmoid(logit_of(beta_ref, j)) for j in heads]
    cs = [r * i * i for r, i in zip(rates, iks)]
    ns = [jnp.where(strict, mm(k, k, NT), 0.0) * c for k, c in zip(ks, cs)]
    blocks = []
    for n in ns:
        blocks += [n[:DIM, :DIM], n[DIM:, DIM:]]
    ts = inverse(blocks)
    t1s = [split(t) for t in ts[0::2]]
    t2s = [split(t) for t in ts[1::2]]
    mids = [split(dot3(split(n[DIM:, :DIM]), t)) for n, t in zip(ns, t1s)]
    lows = [split(-dot3(t, m)) for t, m in zip(t2s, mids)]
    zero = jnp.zeros((DIM, DIM), BF16)
    fulls = [
        tuple(
            jnp.concatenate(
                [
                    jnp.concatenate([t1[p], zero], axis=1),
                    jnp.concatenate([lo[p], t2[p]], axis=1),
                ],
                axis=0,
            )
            for p in range(2)
        )
        for t1, t2, lo in zip(t1s, t2s, lows)
    ]
    eye = (
        lax.broadcasted_iota(jnp.int32, (DIM, DIM), 0)
        == lax.broadcasted_iota(jnp.int32, (DIM, DIM), 1)
    ).astype(F32)
    zs = [dot2r((k * tail).astype(BF16), full, TN) for k, full in zip(k32, fulls)]
    copies[3].wait()
    for j in heads:
        right = writes(head(v_ref, j).astype(F32), k32[j], rates[j], iks[j], keep)
        both = dot3(split(zs[j]), split(right))
        block(ab_ref, j)[...] = eye * through - both[:, DIM:]
        block(ab_ref, HEADS + j)[...] = both[:, :DIM]
        th_ref[j] = fulls[j][0]
        tl_ref[j] = fulls[j][1]
        z_ref[j] = zs[j]
    row = ids_ref[...].astype(F32)
    ab_ref[2 * ROWS :] = notes(row[:, :1], row[:, row.shape[1] - 1 :], 1.0)


def writes(value, key, rate, ik, keep):
    return jnp.concatenate([value * (rate * ik), key * (rate * ik * ik * keep)], axis=1)


def kernel_b(
    ids_ref, q_ref, k_ref, v_ref, beta_ref, th_ref, tl_ref, z_ref,
    o_ref, e_ref, uw_ref, ph_ref, pl_ref, zh_ref, zl_ref,
):
    same, ii, jj, keep, tail, through = id_masks(ids_ref)
    causal = same & (ii >= jj)
    for j in range(HEADS):
        q, k = head(q_ref, j), head(k_ref, j)
        k32 = k.astype(F32)
        rate = jax.nn.sigmoid(logit_of(beta_ref, j))
        right = split(writes(head(v_ref, j).astype(F32), k32, rate, inv_norm(k32), keep))
        solve = (th_ref[j], tl_ref[j])
        uw_ref[j] = dot3(solve, right)
        scores = jnp.where(causal, mm(q, k, NT), 0.0)
        through_solve = split(dot3(split(scores), solve))
        both = dot3(through_solve, right)
        put(o_ref, j, both[:, :DIM])
        put(e_ref, j, q.astype(F32) * keep - both[:, DIM:])
        ph_ref[j] = jnp.transpose(through_solve[0])
        pl_ref[j] = jnp.transpose(through_solve[1])
        ends = split(jnp.transpose(z_ref[j]))
        put(zh_ref, j, ends[0])
        put(zl_ref, j, ends[1])


def kernel_join(ids_ref, ab_ref, prev_ref, both_ref, mid_ref, side_ref):
    row = ids_ref[...].astype(F32)
    last = row[:, row.shape[1] - 1 :]
    before = prev_ref[2 * ROWS :]
    joined = (note(before, 1) == row[:, :1]).astype(F32)
    maps = lax.axis_index("seq") == 3
    for j in range(HEADS):
        right = cat([block(prev_ref, j)[...], block(prev_ref, HEADS + j)[...]], 1)
        made = joined * dot3(split(block(ab_ref, j)[...]), split(right))
        block(both_ref, j)[...] = made[:, :DIM]
        offset = made[:, DIM:] + block(ab_ref, HEADS + j)[...]
        block(both_ref, HEADS + j)[...] = offset
        block(mid_ref, j)[...] = offset
        block(side_ref, j)[...] = jnp.where(maps, made[:, :DIM], offset)
    after = notes(note(before, 0), last, 1.0)
    both_ref[2 * ROWS :] = after
    mid_ref[ROWS:] = after
    side_ref[ROWS:] = after


def kernel_apply(both_ref, mid_ref, out_ref):
    after, middle = both_ref[2 * ROWS :], mid_ref[ROWS:]
    inner = (note(middle, 1) == note(after, 0)).astype(F32)
    for j in range(HEADS):
        made = pack3(split(block(both_ref, j)[...]), split(inner * block(mid_ref, j)[...]))
        block(out_ref, j)[...] = made + block(both_ref, HEADS + j)[...]
    out_ref[ROWS:] = after


def kernel_c(
    ids_ref, q_ref, o_ref, e_ref, prev_ref, m2_ref, m3_ref, m4_ref, cot_ref, gain_ref,
    y_ref, do_ref, c_ref, s_ref, dg_ref,
):
    first = ids_ref[...].astype(F32)[:, :1]
    before = prev_ref[2 * ROWS :]
    direct_side = lax.axis_index("seq") != 1

    def side(rows):
        return jnp.where(direct_side, rows, 0.0)

    middle = side(m2_ref[ROWS:]) + m3_ref[ROWS:] + m4_ref[ROWS:]
    known = note(before, 2)
    inner = (note(middle, 1) == note(before, 0)).astype(F32)
    direct = (1.0 - known) * (note(middle, 1) == first).astype(F32)
    joined = known * (note(before, 1) == first).astype(F32)
    states = []
    for j in range(HEADS):
        mid = side(block(m2_ref, j)[...]) + block(m3_ref, j)[...] + block(m4_ref, j)[...]
        made = pack3(split(block(prev_ref, j)[...]), split(inner * mid))
        states.append(joined * (made + block(prev_ref, HEADS + j)[...]) + direct * mid)
        s_ref[j] = states[j]
    norm_part(
        states, joined + direct, q_ref, o_ref, e_ref, cot_ref, gain_ref, y_ref, do_ref, c_ref,
        dg_ref,
    )


def kernel_c_known(
    joined_ref, q_ref, o_ref, e_ref, s_ref, cot_ref, gain_ref, y_ref, do_ref, c_ref, dg_ref
):
    states = [s_ref[j] for j in range(HEADS)]
    norm_part(
        states, joined_ref[...], q_ref, o_ref, e_ref, cot_ref, gain_ref, y_ref, do_ref, c_ref,
        dg_ref,
    )


def norm_part(
    states, joined, q_ref, o_ref, e_ref, cot_ref, gain_ref, y_ref, do_ref, c_ref, dg_ref
):
    gain = gain_ref[...]
    dgain = jnp.zeros((1, DIM), F32)
    for j in range(HEADS):
        iq = inv_norm(head(q_ref, j).astype(F32))
        effective = split(head(e_ref, j))
        raw = head(o_ref, j) + pack3(effective, split(states[j]))
        out = raw * iq
        inv = lax.rsqrt(jnp.mean(out * out, axis=-1, keepdims=True) + 1e-05)
        unit = out * inv
        put(y_ref, j, unit * gain)
        cot = head(cot_ref, j).astype(F32)
        dgain = dgain + jnp.sum(cot * unit, axis=0, keepdims=True)
        pulled = cot * gain
        dout = inv * (pulled - unit * jnp.mean(pulled * unit, axis=-1, keepdims=True))
        draw = dout * iq
        put(do_ref, j, draw)
        block(c_ref, j)[...] = joined * wide3(effective, split(draw), TN)
    c_ref[ROWS:] = notes(joined)
    dg_ref[...] = dgain


def kernel_back(ab_ref, c_ref, back_ref, out_ref):
    joined = note(c_ref[ROWS:], 0)
    for j in range(HEADS):
        made = wide3(split(block(ab_ref, j)[...]), split(block(back_ref, j)[...]), TN)
        block(out_ref, j)[...] = block(c_ref, j)[...] + joined * made
    out_ref[ROWS:] = c_ref[ROWS:]


def kernel_back_far(ab_ref, c_ref, map_ref, h_ref, far_ref, near_ref, g_ref, out_ref):
    joined = note(c_ref[ROWS:], 0)
    beyond = note(h_ref[ROWS:], 0)
    for j in range(HEADS):
        far = wide3(split(block(map_ref, j)[...]), split(block(far_ref, j)[...]), TN)
        back = block(near_ref, j)[...] + block(h_ref, j)[...] + beyond * far
        g_ref[j] = back
        made = wide3(split(block(ab_ref, j)[...]), split(back), TN)
        block(out_ref, j)[...] = block(c_ref, j)[...] + joined * made


def kernel_d(
    ids_ref, q_ref, k_ref, ph_ref, pl_ref, do_ref, uw_ref, s_ref,
    dq_ref, u_ref, dr_ref, dk_ref,
):
    same, ii, jj, keep, tail, through = id_masks(ids_ref)
    causal = same & (ii >= jj)
    for j in range(HEADS):
        q, k = head(q_ref, j), head(k_ref, j)
        q32 = q.astype(F32)
        state = split(s_ref[j])
        uw = uw_ref[j]
        update = uw[:, :DIM] - pack3(split(uw[:, DIM:]), state)
        draw = head(do_ref, j)
        draws = split(draw)
        weights = split(jnp.where(causal, outer3(draws, split(update)), 0.0))
        dq = keep * pack3_nt(draws, state) + dot2(weights, k)
        iq = inv_norm(q32)
        dq = dq - q32 * (iq * iq * jnp.sum(q32 * dq, axis=-1, keepdims=True))
        put(dq_ref, j, dq)
        put(u_ref, j, update)
        put(dr_ref, j, wide3((ph_ref[j], pl_ref[j]), draws))
        put(dk_ref, j, dot2(weights, q, TN))


def kernel_e(
    ids_ref, k_ref, v_ref, beta_ref, zh_ref, zl_ref, u_ref, dr_ref, dkl_ref, s_ref, g_ref, h_ref,
    dk_ref, dv_ref, db_ref,
):
    same, ii, jj, keep, tail, through = id_masks(ids_ref)
    strict = same & (ii > jj)
    shape = (db_ref.shape[1], db_ref.shape[0])
    lane = lax.broadcasted_iota(jnp.int32, shape, 1)
    dbeta = jnp.zeros(shape, F32)
    heads = range(HEADS)
    for j in heads:
        k = head(k_ref, j)
        k32 = k.astype(F32)
        ik = inv_norm(k32)
        logit = logit_of(beta_ref, j)
        rate = jax.nn.sigmoid(logit)
        update = head(u_ref, j)
        updates = split(update)
        back = split(g_ref[j] + block(h_ref, j)[...])
        dright = head(dr_ref, j) + pack3((head(zh_ref, j), head(zl_ref, j)), back)
        put(dv_ref, j, dright * (rate * ik))
        dlogit = jax.nn.sigmoid(-logit) * jnp.sum(dright * update, axis=-1, keepdims=True)
        dbeta = jnp.where(lane == j, dlogit, dbeta)
        scaled = dright * (rate * ik * ik)
        inner = split(jnp.where(strict, outer3(split(-scaled), updates), 0.0))
        dk = head(dkl_ref, j) + (dot2(inner, k) + dot2(inner, k, TN))
        dk = dk + tail * pack3_nt(updates, back)
        dk = dk - keep * pack3_nt(split(scaled), split(s_ref[j]))
        dk = dk - k32 * (ik * ik * jnp.sum(k32 * dk, axis=-1, keepdims=True))
        put(dk_ref, j, dk)

    db_ref[...] = jnp.transpose(dbeta)


def call(kernel, ins, outs, flops, name, **extra):
    return pl.pallas_call(
        kernel,
        out_shape=outs,
        compiler_params=pltpu.CompilerParams(vmem_limit_bytes=16 * 1024 * 1024),
        cost_estimate=pl.CostEstimate(flops=flops, bytes_accessed=4_000_000, transcendentals=0),
        name=name,
        **extra,
    )(*ins)


def shape(*sizes, dtype=F32):
    return jax.ShapeDtypeStruct(sizes, dtype)


def send(value, pairs):
    return lax.ppermute(value, "seq", pairs)


def relay_forward(ab, ids, spans):
    half = spans // 2
    at = ab[:ROWS].reshape(HEADS, DIM, DIM)
    bt = ab[ROWS : 2 * ROWS].reshape(HEADS, DIM, DIM)
    prior = send(ids[:, ids.shape[1] - 1 :], [(s, s + 1) for s in range(spans - 1)])
    joined = (prior == ids[:, :1]).astype(F32)
    entering = jnp.zeros((HEADS, DIM, DIM), F32)
    outgoing = bt
    for turn in range(half):
        pairs = [(turn, turn + 1)]
        if turn == 0:
            pairs += [(s, s + 1) for s in range(half, spans - 1)]
        entering = entering + joined[:, :, None] * send(outgoing, pairs)
        if turn < half - 1:
            dims = (((2,), (1,)), ((0,), (0,)))
            outgoing = lax.dot_general(at, entering, dims, precision=HIGHEST) + bt
    return entering, joined


def relay_backward(ab, c, spans):
    half = spans // 2
    at = ab[:ROWS].reshape(HEADS, DIM, DIM)
    joined = c[ROWS : ROWS + 1, :1]
    cs = c[:ROWS].reshape(HEADS, DIM, DIM)
    back = jnp.zeros((HEADS, DIM, DIM), F32)
    outgoing = cs
    for turn in range(half):
        pairs = [(half - turn, half - turn - 1)]
        if turn == 0:
            pairs += [(s, s - 1) for s in range(half + 1, spans)]
        back = back + send(outgoing, pairs)
        if turn < half - 1:
            dims = (((1,), (1,)), ((0,), (0,)))
            outgoing = lax.dot_general(at, back, dims, precision=HIGHEST) * joined + cs
    return back


def local(
    query_heads, key_heads, value_heads, beta_logits, segment_ids, output_cotangent, norm_gain
):
    q, k, v = query_heads[0], key_heads[0], value_heads[0]
    beta, ids, cot = jnp.transpose(beta_logits[0]), segment_ids, output_cotangent[0]
    gain = norm_gain[None]
    tokens = q.shape[0]
    spans = lax.axis_size("seq")
    short = spans == 8

    wide, wide16 = shape(tokens, ROWS), shape(tokens, ROWS, dtype=BF16)
    states = shape(HEADS, DIM, DIM)
    square = shape(HEADS, tokens, tokens, dtype=BF16)
    one, two = shape(ROWS + META, DIM), shape(2 * ROWS + META, DIM)
    row = shape(1, DIM)
    unit = 2 * HEADS * tokens**3

    ab, th, tl, z = call(
        kernel_a, (ids, k, v, beta), (two, square, square, shape(HEADS, DIM, tokens)),
        20 * unit, "span_state",
        in_specs=[pl.BlockSpec(memory_space=pltpu.HBM)] * 4,
        scratch_shapes=[
            pltpu.VMEM(ids.shape, ids.dtype),
            pltpu.VMEM(k.shape, k.dtype),
            pltpu.VMEM(v.shape, v.dtype),
            pltpu.VMEM(beta.shape, beta.dtype),
            pltpu.SemaphoreType.DMA((4,)),
        ],
    )
    if short:
        r1 = send(ab, [(0, 1), (2, 3)])
        pair, mid, side = call(kernel_join, (ids, ab, r1), (two, one, one), unit, "join")
        m3 = send(mid, [(1, 3)])
        side = send(side, [(1, 2), (3, 1), (4, 5), (5, 6), (6, 7)])
    o0, eff, uw, ph, pl_, zh, zl = call(
        kernel_b, (ids, q, k, v, beta, th, tl, z),
        (
            wide, wide, shape(HEADS, tokens, 2 * DIM), square, square, wide16, wide16,
        ),
        11 * unit, "span_out",
    )
    if short:
        m3, side, o0 = lax.optimization_barrier((m3, side, o0))
        m4 = send(call(kernel_apply, (pair, m3), one, unit, "apply"), [(3, 4)])
        mixed, draw, c, entering, dgain = call(
            kernel_c, (ids, q, o0, eff, r1, side, m3, m4, cot, gain),
            (wide16, wide, one, states, row), 4 * unit, "span_norm",
        )
        n3 = send(c, [(4, 1)])
        n4 = send(c, [(4, 3)])
        n1 = send(c, [(3, 2)])
        n2 = send(call(kernel_back, (ab, c, n1), one, unit, "back"), [(2, 1)])
    else:
        entering, joined = relay_forward(ab, ids, spans)
        mixed, draw, c, dgain = call(
            kernel_c_known, (joined, q, o0, eff, entering, cot, gain),
            (wide16, wide, one, row), 4 * unit, "span_norm",
        )
    dq, update, dright, dkl = call(
        kernel_d, (ids, q, k, ph, pl_, draw, uw, entering), (wide16, wide, wide, wide),
        12 * unit, "span_query_grad",
    )
    if short:
        n3, n4, update = lax.optimization_barrier((n3, n4, update))
        back, last = call(
            kernel_back_far, (ab, c, side, n2, n3, n4), (states, shape(ROWS, DIM)), unit,
            "back_far",
        )
        far = send(last, [(1, 0), (3, 2), (5, 4), (6, 5), (7, 6)])
    else:
        back = relay_backward(ab, c, spans)
        far = jnp.zeros((ROWS, DIM), F32)
    dk, dv, dbeta = call(
        kernel_e, (ids, k, v, beta, zh, zl, update, dright, dkl, entering, back, far),
        (wide16, wide16, shape(HEADS, tokens)), 12 * unit, "span_key_grad",
    )
    dgain, dbeta = lax.optimization_barrier((dgain, dbeta))
    devices = spans * lax.axis_size("dp")
    copies = jnp.broadcast_to(dgain, (devices, DIM))[:, None]
    gain_total = jnp.sum(lax.all_to_all(copies, ("seq", "dp"), 0, 0), axis=(0, 1))
    return (mixed[None], dq[None], dk[None], dv[None], jnp.transpose(dbeta)[None], gain_total)


def solution(mesh):
    rows = P("dp", "seq", None)
    return jax.shard_map(
        local,
        mesh=mesh,
        in_specs=(rows, rows, rows, rows, P("dp", "seq"), rows, P()),
        out_specs=(rows, rows, rows, rows, rows, P()),
        check_vma=False,
    )
```

```python
import functools

import jax
import jax.numpy as jnp
from jax import lax
from jax.experimental import pallas as pl
from jax.experimental.pallas import tpu as pltpu
from jax.sharding import PartitionSpec as P

HEADS = 8
DIM = 128
BASE = 16
ROWS = HEADS * DIM
META = 8
HIGHEST = lax.Precision.HIGHEST
F32 = jnp.float32
BF16 = jnp.bfloat16

NN = (((1,), (0,)), ((), ()))
NT = (((1,), (1,)), ((), ()))
TN = (((0,), (0,)), ((), ()))


def split(x):
    hi = x.astype(BF16)
    return hi, (x - hi.astype(F32)).astype(BF16)


def mm(a, b, dims=NN):
    return lax.dot_general(a, b, dims, preferred_element_type=F32)


def dot3(a, b, dims=NN):
    return mm(a[0], b[0], dims) + (mm(a[0], b[1], dims) + mm(a[1], b[0], dims))


def dot2(a, b, dims=NN):
    return mm(a[0], b, dims) + mm(a[1], b, dims)


def dot2r(a, b, dims=NN):
    return mm(a, b[0], dims) + mm(a, b[1], dims)


def cat(parts, axis):
    return jnp.concatenate(parts, axis=axis)


def pack3(a, b):
    left = cat([a[0], a[1]], 1)
    right = cat([cat([b[0], b[1]], 1), cat([b[0], jnp.zeros_like(b[0])], 1)], 0)
    out = mm(left, right)
    return out[:, :DIM] + out[:, DIM:]


def pack3_nt(a, b):
    left = cat([a[0], a[1]], 1)
    right = cat([cat([b[0], b[0]], 1), cat([b[1], jnp.zeros_like(b[1])], 1)], 0)
    out = mm(left, right, NT)
    return out[:, :DIM] + out[:, DIM:]


def outer3(a, b):
    return mm(cat([a[0], a[1]], 1), cat([b[0], b[0]], 1), NT) + mm(a[0], b[1], NT)


def wide3(a, b, dims=NN):
    out = mm(a[0], cat([b[0], b[1]], 1), dims)
    return out[:, :DIM] + (out[:, DIM:] + mm(a[1], b[0], dims))


def id_masks(ids_ref):
    row = ids_ref[...].astype(F32)
    n = row.shape[1]
    ii = lax.broadcasted_iota(jnp.int32, (n, n), 0)
    jj = lax.broadcasted_iota(jnp.int32, (n, n), 1)
    col = jnp.sum(jnp.where(ii == jj, row, 0.0), axis=1, keepdims=True)
    same = col == row
    first, last = row[:, :1], row[:, n - 1 :]
    keep = (col == first).astype(F32)
    tail = (col == last).astype(F32)
    through = (first == last).astype(F32)
    return same, ii, jj, keep, tail, through


def head(ref, j):
    return ref[:, DIM * j : DIM * (j + 1)]


def block(ref, j):
    return ref.at[DIM * j : DIM * (j + 1)]


def notes(*values):
    lane = lax.broadcasted_iota(jnp.int32, (META, DIM), 1)
    out = jnp.zeros((META, DIM), F32)
    for at, value in enumerate(values):
        out = jnp.where(lane == at, value, out)
    return out


def note(rows, at):
    return rows[:1, at : at + 1]


def put(ref, j, value):
    ref[:, DIM * j : DIM * (j + 1)] = value.astype(ref.dtype)


def inv_norm(x):
    return lax.rsqrt(jnp.sum(x * x, axis=-1, keepdims=True) + 1e-06)


def logit_of(beta_ref, j):
    beta = jnp.transpose(beta_ref[...])
    lane = lax.broadcasted_iota(jnp.int32, beta.shape, 1)
    return jnp.sum(jnp.where(lane == j, beta, 0.0), axis=1, keepdims=True)


def base_inverses(blocks):
    n, base = DIM, BASE
    groups = n // base
    lane = lax.broadcasted_iota(jnp.int32, (base, n), 1)
    row = lax.broadcasted_iota(jnp.int32, (base, n), 0)
    compact = []
    for block in blocks:
        kept = [
            jnp.where(lane // base == g, block[g * base : (g + 1) * base], 0.0)
            for g in range(groups)
        ]
        while len(kept) > 1:
            kept = [x + y for x, y in zip(kept[0::2], kept[1::2])]
        compact.append(kept[0])
    ii = lax.broadcasted_iota(jnp.int32, (n, n), 0)
    jj = lax.broadcasted_iota(jnp.int32, (n, n), 1)
    together = ii // base == jj // base
    pick = jnp.concatenate(
        [(together & (ii % base == j)).astype(F32).astype(BF16) for j in range(base - 1)], axis=1
    )
    high, low = split(jnp.concatenate(compact, axis=0))
    columns = mm(high, pick) + mm(low, pick)
    start = (lane % base == row).astype(F32)
    ts = [start for _ in blocks]
    for j in range(base - 1):
        part = columns[:, j * n : (j + 1) * n]
        ts = [
            t - part[i * base : (i + 1) * base] * t[j : j + 1] for i, t in enumerate(ts)
        ]
    return [
        jnp.concatenate([jnp.where(lane // base == g, t, 0.0) for g in range(groups)], axis=0)
        for t in ts
    ]


def inverse(blocks):
    n = DIM
    ii = lax.broadcasted_iota(jnp.int32, (n, n), 0)
    jj = lax.broadcasted_iota(jnp.int32, (n, n), 1)

    def off(block, s):
        inside = (ii // (2 * s) == jj // (2 * s)) & (ii // s != jj // s)
        return jnp.where(inside, block, 0.0)

    ts = base_inverses(blocks)
    s = BASE
    while s < n:
        offs = [split(off(b, s)) for b in blocks]
        tss = [split(t) for t in ts]
        mids = [dot3(o, t) for o, t in zip(offs, tss)]
        mids = [split(m) for m in mids]
        ts = [t - dot3(p, m) for t, p, m in zip(ts, tss, mids)]
        s *= 2
    return ts


def kernel_a(
    ids_in, k_in, v_in, beta_in, ab_ref, b_ref, th_ref, tl_ref, z_ref,
    ids_ref, k_ref, v_ref, beta_ref, sems,
):
    copies = [
        pltpu.make_async_copy(source, target, sems.at[at])
        for at, (source, target) in enumerate(
            ((ids_in, ids_ref), (k_in, k_ref), (beta_in, beta_ref), (v_in, v_ref))
        )
    ]
    for copy in copies:
        copy.start()
    for copy in copies[:3]:
        copy.wait()
    same, ii, jj, keep, tail, through = id_masks(ids_ref)
    strict = same & (ii > jj)
    heads = range(HEADS)
    ks = [head(k_ref, j) for j in heads]
    k32 = [k.astype(F32) for k in ks]
    iks = [inv_norm(k) for k in k32]
    rates = [jax.nn.sigmoid(logit_of(beta_ref, j)) for j in heads]
    cs = [r * i * i for r, i in zip(rates, iks)]
    ns = [jnp.where(strict, mm(k, k, NT), 0.0) * c for k, c in zip(ks, cs)]
    blocks = []
    for n in ns:
        blocks += [n[:DIM, :DIM], n[DIM:, DIM:]]
    ts = inverse(blocks)
    t1s = [split(t) for t in ts[0::2]]
    t2s = [split(t) for t in ts[1::2]]
    mids = [split(dot3(split(n[DIM:, :DIM]), t)) for n, t in zip(ns, t1s)]
    lows = [split(-dot3(t, m)) for t, m in zip(t2s, mids)]
    zero = jnp.zeros((DIM, DIM), BF16)
    fulls = [
        tuple(
            jnp.concatenate(
                [
                    jnp.concatenate([t1[p], zero], axis=1),
                    jnp.concatenate([lo[p], t2[p]], axis=1),
                ],
                axis=0,
            )
            for p in range(2)
        )
        for t1, t2, lo in zip(t1s, t2s, lows)
    ]
    eye = (
        lax.broadcasted_iota(jnp.int32, (DIM, DIM), 0)
        == lax.broadcasted_iota(jnp.int32, (DIM, DIM), 1)
    ).astype(F32)
    zs = [dot2r((k * tail).astype(BF16), full, TN) for k, full in zip(k32, fulls)]
    copies[3].wait()
    for j in heads:
        right = writes(head(v_ref, j).astype(F32), k32[j], rates[j], iks[j], keep)
        both = dot3(split(zs[j]), split(right))
        block(ab_ref, j)[...] = eye * through - both[:, DIM:]
        block(ab_ref, HEADS + j)[...] = both[:, :DIM]
        block(b_ref, j)[...] = both[:, :DIM]
        th_ref[j] = fulls[j][0]
        tl_ref[j] = fulls[j][1]
        z_ref[j] = zs[j]
    row = ids_ref[...].astype(F32)
    after = notes(row[:, :1], row[:, row.shape[1] - 1 :], 1.0)
    ab_ref[2 * ROWS :] = after
    b_ref[ROWS:] = after


def writes(value, key, rate, ik, keep):
    return jnp.concatenate([value * (rate * ik), key * (rate * ik * ik * keep)], axis=1)


def kernel_b(
    ids_ref, q_ref, k_ref, v_ref, beta_ref, th_ref, tl_ref, z_ref,
    o_ref, e_ref, uw_ref, ph_ref, pl_ref, zh_ref, zl_ref,
):
    same, ii, jj, keep, tail, through = id_masks(ids_ref)
    causal = same & (ii >= jj)
    for j in range(HEADS):
        q, k = head(q_ref, j), head(k_ref, j)
        k32 = k.astype(F32)
        rate = jax.nn.sigmoid(logit_of(beta_ref, j))
        right = split(writes(head(v_ref, j).astype(F32), k32, rate, inv_norm(k32), keep))
        solve = (th_ref[j], tl_ref[j])
        uw_ref[j] = dot3(solve, right)
        scores = jnp.where(causal, mm(q, k, NT), 0.0)
        through_solve = split(dot3(split(scores), solve))
        both = dot3(through_solve, right)
        put(o_ref, j, both[:, :DIM])
        put(e_ref, j, q.astype(F32) * keep - both[:, DIM:])
        ph_ref[j] = jnp.transpose(through_solve[0])
        pl_ref[j] = jnp.transpose(through_solve[1])
        ends = split(jnp.transpose(z_ref[j]))
        put(zh_ref, j, ends[0])
        put(zl_ref, j, ends[1])


def kernel_step(ids_ref, ab_ref, prev_ref, out_ref):
    row = ids_ref[...].astype(F32)
    joined = (note(prev_ref[ROWS:], 1) == row[:, :1]).astype(F32)
    for j in range(HEADS):
        made = pack3(split(block(ab_ref, j)[...]), split(block(prev_ref, j)[...]))
        block(out_ref, j)[...] = joined * made + block(ab_ref, HEADS + j)[...]
    out_ref[ROWS:] = ab_ref[2 * ROWS :]


def kernel_join(ids_ref, ab_ref, prev_ref, both_ref, map_ref):
    row = ids_ref[...].astype(F32)
    last = row[:, row.shape[1] - 1 :]
    before = prev_ref[2 * ROWS :]
    joined = (note(before, 1) == row[:, :1]).astype(F32)
    for j in range(HEADS):
        right = cat([block(prev_ref, j)[...], block(prev_ref, HEADS + j)[...]], 1)
        made = joined * dot3(split(block(ab_ref, j)[...]), split(right))
        block(map_ref, j)[...] = made[:, :DIM]
        block(both_ref, j)[...] = made[:, :DIM]
        block(both_ref, HEADS + j)[...] = made[:, DIM:] + block(ab_ref, HEADS + j)[...]
    both_ref[2 * ROWS :] = notes(note(before, 0), last, 1.0)


def kernel_apply(both_ref, mid_ref, out_ref):
    after, middle = both_ref[2 * ROWS :], mid_ref[ROWS:]
    inner = (note(middle, 1) == note(after, 0)).astype(F32)
    for j in range(HEADS):
        made = pack3(split(block(both_ref, j)[...]), split(inner * block(mid_ref, j)[...]))
        block(out_ref, j)[...] = made + block(both_ref, HEADS + j)[...]
    out_ref[ROWS:] = after


def kernel_c(
    ids_ref, q_ref, o_ref, e_ref, prev_ref, m1_ref, m2_ref, m3_ref, m4_ref, cot_ref, gain_ref,
    y_ref, do_ref, c_ref, s_ref, dg_ref,
):
    first = ids_ref[...].astype(F32)[:, :1]
    before = prev_ref[2 * ROWS :]
    parts = (m1_ref, m2_ref, m3_ref, m4_ref)
    middle = sum(part[ROWS:] for part in parts)
    known = note(before, 2)
    inner = (note(middle, 1) == note(before, 0)).astype(F32)
    direct = (1.0 - known) * (note(middle, 1) == first).astype(F32)
    joined = known * (note(before, 1) == first).astype(F32)
    states = []
    for j in range(HEADS):
        mid = sum(block(part, j)[...] for part in parts)
        made = pack3(split(block(prev_ref, j)[...]), split(inner * mid))
        states.append(joined * (made + block(prev_ref, HEADS + j)[...]) + direct * mid)
        s_ref[j] = states[j]
    norm_part(
        states, joined + direct, q_ref, o_ref, e_ref, cot_ref, gain_ref, y_ref, do_ref, c_ref,
        dg_ref,
    )


def kernel_c_known(
    joined_ref, q_ref, o_ref, e_ref, s_ref, cot_ref, gain_ref, y_ref, do_ref, c_ref, dg_ref
):
    states = [s_ref[j] for j in range(HEADS)]
    norm_part(
        states, joined_ref[...], q_ref, o_ref, e_ref, cot_ref, gain_ref, y_ref, do_ref, c_ref,
        dg_ref,
    )


def norm_part(
    states, joined, q_ref, o_ref, e_ref, cot_ref, gain_ref, y_ref, do_ref, c_ref, dg_ref
):
    gain = gain_ref[...]
    dgain = jnp.zeros((1, DIM), F32)
    for j in range(HEADS):
        iq = inv_norm(head(q_ref, j).astype(F32))
        effective = split(head(e_ref, j))
        raw = head(o_ref, j) + pack3(effective, split(states[j]))
        out = raw * iq
        inv = lax.rsqrt(jnp.mean(out * out, axis=-1, keepdims=True) + 1e-05)
        unit = out * inv
        put(y_ref, j, unit * gain)
        cot = head(cot_ref, j).astype(F32)
        dgain = dgain + jnp.sum(cot * unit, axis=0, keepdims=True)
        pulled = cot * gain
        dout = inv * (pulled - unit * jnp.mean(pulled * unit, axis=-1, keepdims=True))
        draw = dout * iq
        put(do_ref, j, draw)
        block(c_ref, j)[...] = joined * wide3(effective, split(draw), TN)
    c_ref[ROWS:] = notes(joined)
    dg_ref[...] = dgain


def kernel_back(ab_ref, c_ref, back_ref, out_ref):
    joined = note(c_ref[ROWS:], 0)
    for j in range(HEADS):
        made = wide3(split(block(ab_ref, j)[...]), split(block(back_ref, j)[...]), TN)
        block(out_ref, j)[...] = block(c_ref, j)[...] + joined * made
    out_ref[ROWS:] = c_ref[ROWS:]


def kernel_back_far(ab_ref, c_ref, map_ref, h_ref, far_ref, near_ref, g_ref, out_ref):
    joined = note(c_ref[ROWS:], 0)
    beyond = note(h_ref[ROWS:], 0)
    backs = []
    for j in range(HEADS):
        far = wide3(split(block(map_ref, j)[...]), split(block(far_ref, j)[...]), TN)
        backs.append(block(near_ref, j)[...] + block(h_ref, j)[...] + beyond * far)
        g_ref[j] = backs[j]
    for j in range(HEADS):
        made = wide3(split(block(ab_ref, j)[...]), split(backs[j]), TN)
        block(out_ref, j)[...] = block(c_ref, j)[...] + joined * made


def kernel_d(
    ids_ref, q_ref, k_ref, ph_ref, pl_ref, do_ref, uw_ref, s_ref,
    dq_ref, u_ref, dr_ref, dk_ref,
):
    same, ii, jj, keep, tail, through = id_masks(ids_ref)
    causal = same & (ii >= jj)
    for j in range(HEADS):
        q, k = head(q_ref, j), head(k_ref, j)
        q32 = q.astype(F32)
        state = split(s_ref[j])
        uw = uw_ref[j]
        update = uw[:, :DIM] - pack3(split(uw[:, DIM:]), state)
        draw = head(do_ref, j)
        draws = split(draw)
        weights = split(jnp.where(causal, outer3(draws, split(update)), 0.0))
        dq = keep * pack3_nt(draws, state) + dot2(weights, k)
        iq = inv_norm(q32)
        dq = dq - q32 * (iq * iq * jnp.sum(q32 * dq, axis=-1, keepdims=True))
        put(dq_ref, j, dq)
        put(u_ref, j, update)
        put(dr_ref, j, wide3((ph_ref[j], pl_ref[j]), draws))
        put(dk_ref, j, dot2(weights, q, TN))


def kernel_e(
    ids_ref, k_ref, v_ref, beta_ref, zh_ref, zl_ref, u_ref, dr_ref, dkl_ref, s_ref, g_ref, h_ref,
    dk_ref, dv_ref, db_ref,
):
    same, ii, jj, keep, tail, through = id_masks(ids_ref)
    strict = same & (ii > jj)
    shape = (db_ref.shape[1], db_ref.shape[0])
    lane = lax.broadcasted_iota(jnp.int32, shape, 1)
    dbeta = jnp.zeros(shape, F32)
    heads = range(HEADS)
    for j in heads:
        k = head(k_ref, j)
        k32 = k.astype(F32)
        ik = inv_norm(k32)
        logit = logit_of(beta_ref, j)
        rate = jax.nn.sigmoid(logit)
        update = head(u_ref, j)
        updates = split(update)
        back = split(g_ref[j] + block(h_ref, j)[...])
        dright = head(dr_ref, j) + pack3((head(zh_ref, j), head(zl_ref, j)), back)
        put(dv_ref, j, dright * (rate * ik))
        dlogit = jax.nn.sigmoid(-logit) * jnp.sum(dright * update, axis=-1, keepdims=True)
        dbeta = jnp.where(lane == j, dlogit, dbeta)
        scaled = dright * (rate * ik * ik)
        inner = split(jnp.where(strict, outer3(split(-scaled), updates), 0.0))
        dk = head(dkl_ref, j) + (dot2(inner, k) + dot2(inner, k, TN))
        dk = dk + tail * pack3_nt(updates, back)
        dk = dk - keep * pack3_nt(split(scaled), split(s_ref[j]))
        dk = dk - k32 * (ik * ik * jnp.sum(k32 * dk, axis=-1, keepdims=True))
        put(dk_ref, j, dk)

    db_ref[...] = jnp.transpose(dbeta)


def call(kernel, ins, outs, flops, name, **extra):
    return pl.pallas_call(
        kernel,
        out_shape=outs,
        compiler_params=pltpu.CompilerParams(vmem_limit_bytes=16 * 1024 * 1024),
        cost_estimate=pl.CostEstimate(flops=flops, bytes_accessed=4_000_000, transcendentals=0),
        name=name,
        **extra,
    )(*ins)


def shape(*sizes, dtype=F32):
    return jax.ShapeDtypeStruct(sizes, dtype)


def send(value, pairs):
    return lax.ppermute(value, "seq", pairs)


def relay_forward(ab, ids, spans):
    half = spans // 2
    at = ab[:ROWS].reshape(HEADS, DIM, DIM)
    bt = ab[ROWS : 2 * ROWS].reshape(HEADS, DIM, DIM)
    prior = send(ids[:, ids.shape[1] - 1 :], [(s, s + 1) for s in range(spans - 1)])
    joined = (prior == ids[:, :1]).astype(F32)
    entering = jnp.zeros((HEADS, DIM, DIM), F32)
    outgoing = bt
    for turn in range(half):
        pairs = [(turn, turn + 1)]
        if turn == 0:
            pairs += [(s, s + 1) for s in range(half, spans - 1)]
        entering = entering + joined[:, :, None] * send(outgoing, pairs)
        if turn < half - 1:
            dims = (((2,), (1,)), ((0,), (0,)))
            outgoing = lax.dot_general(at, entering, dims, precision=HIGHEST) + bt
    return entering, joined


def relay_backward(ab, c, spans):
    half = spans // 2
    at = ab[:ROWS].reshape(HEADS, DIM, DIM)
    joined = c[ROWS : ROWS + 1, :1]
    cs = c[:ROWS].reshape(HEADS, DIM, DIM)
    back = jnp.zeros((HEADS, DIM, DIM), F32)
    outgoing = cs
    for turn in range(half):
        pairs = [(half - turn, half - turn - 1)]
        if turn == 0:
            pairs += [(s, s - 1) for s in range(half + 1, spans)]
        back = back + send(outgoing, pairs)
        if turn < half - 1:
            dims = (((1,), (1,)), ((0,), (0,)))
            outgoing = lax.dot_general(at, back, dims, precision=HIGHEST) * joined + cs
    return back


def local(
    query_heads, key_heads, value_heads, beta_logits, segment_ids, output_cotangent, norm_gain
):
    q, k, v = query_heads[0], key_heads[0], value_heads[0]
    beta, ids, cot = jnp.transpose(beta_logits[0]), segment_ids, output_cotangent[0]
    gain = norm_gain[None]
    tokens = q.shape[0]
    spans = lax.axis_size("seq")
    short = spans == 8

    wide, wide16 = shape(tokens, ROWS), shape(tokens, ROWS, dtype=BF16)
    states = shape(HEADS, DIM, DIM)
    square = shape(HEADS, tokens, tokens, dtype=BF16)
    one, two = shape(ROWS + META, DIM), shape(2 * ROWS + META, DIM)
    row = shape(1, DIM)
    unit = 2 * HEADS * tokens**3

    ab, bm, th, tl, z = call(
        kernel_a, (ids, k, v, beta), (two, one, square, square, shape(HEADS, DIM, tokens)),
        20 * unit, "span_state",
        in_specs=[pl.BlockSpec(memory_space=pltpu.HBM)] * 4,
        scratch_shapes=[
            pltpu.VMEM(ids.shape, ids.dtype),
            pltpu.VMEM(k.shape, k.dtype),
            pltpu.VMEM(v.shape, v.dtype),
            pltpu.VMEM(beta.shape, beta.dtype),
            pltpu.SemaphoreType.DMA((4,)),
        ],
    )
    if short:
        r1 = send(bm, [(0, 1)])
        r3 = send(ab, [(2, 3)])
        mid = call(kernel_step, (ids, ab, r1), one, unit, "step")
        m3 = send(mid, [(1, 3)])
        r3, mid = lax.optimization_barrier((r3, mid))
        pair, pair_map = call(
            kernel_join, (ids, ab, r3), (two, shape(ROWS, DIM)), unit, "join"
        )
        far_map = send(pair_map, [(3, 1)])
        th, pair = lax.optimization_barrier((th, pair))
    o0, eff, uw, ph, pl_, zh, zl = call(
        kernel_b, (ids, q, k, v, beta, th, tl, z),
        (
            wide, wide, shape(HEADS, tokens, 2 * DIM), square, square, wide16, wide16,
        ),
        11 * unit, "span_out",
    )
    if short:
        mid, o0 = lax.optimization_barrier((mid, o0))
        m3, far_map, o0 = lax.optimization_barrier((m3, far_map, o0))
        m2 = send(mid, [(1, 2), (4, 5), (5, 6), (6, 7)])
        m4 = send(call(kernel_apply, (pair, m3), one, unit, "apply"), [(3, 4)])
        mixed, draw, c, entering, dgain = call(
            kernel_c, (ids, q, o0, eff, r3, r1, m2, m3, m4, cot, gain),
            (wide16, wide, one, states, row), 4 * unit, "span_norm",
        )
        n3 = send(c, [(4, 1)])
        n4 = send(c, [(4, 3)])
        n1 = send(c, [(3, 2)])
        h = call(kernel_back, (ab, c, n1), one, unit, "back")
        n2 = send(h, [(2, 1)])
    else:
        entering, joined = relay_forward(ab, ids, spans)
        mixed, draw, c, dgain = call(
            kernel_c_known, (joined, q, o0, eff, entering, cot, gain),
            (wide16, wide, one, row), 4 * unit, "span_norm",
        )
    dq, update, dright, dkl = call(
        kernel_d, (ids, q, k, ph, pl_, draw, uw, entering), (wide16, wide, wide, wide),
        12 * unit, "span_query_grad",
    )
    if short:
        n3, n4, update = lax.optimization_barrier((n3, n4, update))
        back, last = call(
            kernel_back_far, (ab, c, far_map, n2, n3, n4), (states, shape(ROWS, DIM)), unit,
            "back_far",
        )
        far = send(last, [(1, 0), (3, 2), (5, 4), (6, 5), (7, 6)])
    else:
        back = relay_backward(ab, c, spans)
        far = jnp.zeros((ROWS, DIM), F32)
    dk, dv, dbeta = call(
        kernel_e, (ids, k, v, beta, zh, zl, update, dright, dkl, entering, back, far),
        (wide16, wide16, shape(HEADS, tokens)), 12 * unit, "span_key_grad",
    )
    dgain, dbeta = lax.optimization_barrier((dgain, dbeta))
    devices = spans * lax.axis_size("dp")
    copies = jnp.broadcast_to(dgain, (devices, DIM))[:, None]
    gain_total = jnp.sum(lax.all_to_all(copies, ("seq", "dp"), 0, 0), axis=(0, 1))
    return (mixed[None], dq[None], dk[None], dv[None], jnp.transpose(dbeta)[None], gain_total)


def solution(mesh):
    rows = P("dp", "seq", None)
    return jax.shard_map(
        local,
        mesh=mesh,
        in_specs=(rows, rows, rows, rows, P("dp", "seq"), rows, P()),
        out_specs=(rows, rows, rows, rows, rows, P()),
        check_vma=False,
    )
```

```python
import functools

import jax
import jax.numpy as jnp
from jax import lax
from jax.experimental import pallas as pl
from jax.experimental.pallas import tpu as pltpu
from jax.sharding import PartitionSpec as P

HEADS = 8
DIM = 128
BASE = 16
TOGETHER = 4
ROWS = HEADS * DIM
META = 8
HIGHEST = lax.Precision.HIGHEST
F32 = jnp.float32
BF16 = jnp.bfloat16

NN = (((1,), (0,)), ((), ()))
NT = (((1,), (1,)), ((), ()))
TN = (((0,), (0,)), ((), ()))


def split(x):
    hi = x.astype(BF16)
    return hi, (x - hi.astype(F32)).astype(BF16)


def mm(a, b, dims=NN):
    return lax.dot_general(a, b, dims, preferred_element_type=F32)


def dot3(a, b, dims=NN):
    return mm(a[0], b[0], dims) + (mm(a[0], b[1], dims) + mm(a[1], b[0], dims))


def dot2(a, b, dims=NN):
    return mm(a[0], b, dims) + mm(a[1], b, dims)


def dot2r(a, b, dims=NN):
    return mm(a, b[0], dims) + mm(a, b[1], dims)


def cat(parts, axis):
    return jnp.concatenate(parts, axis=axis)


def pack3(a, b):
    left = cat([a[0], a[1]], 1)
    right = cat([cat([b[0], b[1]], 1), cat([b[0], jnp.zeros_like(b[0])], 1)], 0)
    out = mm(left, right)
    return out[:, :DIM] + out[:, DIM:]


def pack3_nt(a, b):
    left = cat([a[0], a[1]], 1)
    right = cat([cat([b[0], b[0]], 1), cat([b[1], jnp.zeros_like(b[1])], 1)], 0)
    out = mm(left, right, NT)
    return out[:, :DIM] + out[:, DIM:]


def outer3(a, b):
    return mm(cat([a[0], a[1]], 1), cat([b[0], b[0]], 1), NT) + mm(a[0], b[1], NT)


def wide3(a, b, dims=NN):
    out = mm(a[0], cat([b[0], b[1]], 1), dims)
    return out[:, :DIM] + (out[:, DIM:] + mm(a[1], b[0], dims))


def id_masks(ids_ref):
    row = ids_ref[...].astype(F32)
    n = row.shape[1]
    ii = lax.broadcasted_iota(jnp.int32, (n, n), 0)
    jj = lax.broadcasted_iota(jnp.int32, (n, n), 1)
    col = jnp.sum(jnp.where(ii == jj, row, 0.0), axis=1, keepdims=True)
    same = col == row
    first, last = row[:, :1], row[:, n - 1 :]
    keep = (col == first).astype(F32)
    tail = (col == last).astype(F32)
    through = (first == last).astype(F32)
    return same, ii, jj, keep, tail, through


def head(ref, j):
    return ref[:, DIM * j : DIM * (j + 1)]


def block(ref, j):
    return ref.at[DIM * j : DIM * (j + 1)]


def notes(*values):
    lane = lax.broadcasted_iota(jnp.int32, (META, DIM), 1)
    out = jnp.zeros((META, DIM), F32)
    for at, value in enumerate(values):
        out = jnp.where(lane == at, value, out)
    return out


def note(rows, at):
    return rows[:1, at : at + 1]


def put(ref, j, value):
    ref[:, DIM * j : DIM * (j + 1)] = value.astype(ref.dtype)


def inv_norm(x):
    return lax.rsqrt(jnp.sum(x * x, axis=-1, keepdims=True) + 1e-06)


def logit_of(beta_ref, j):
    beta = jnp.transpose(beta_ref[...])
    lane = lax.broadcasted_iota(jnp.int32, beta.shape, 1)
    return jnp.sum(jnp.where(lane == j, beta, 0.0), axis=1, keepdims=True)


def base_inverses(blocks):
    n, base = DIM, BASE
    groups = n // base
    lane = lax.broadcasted_iota(jnp.int32, (base, n), 1)
    row = lax.broadcasted_iota(jnp.int32, (base, n), 0)
    compact = []
    for block in blocks:
        kept = [
            jnp.where(lane // base == g, block[g * base : (g + 1) * base], 0.0)
            for g in range(groups)
        ]
        while len(kept) > 1:
            kept = [x + y for x, y in zip(kept[0::2], kept[1::2])]
        compact.append(kept[0])
    ii = lax.broadcasted_iota(jnp.int32, (n, n), 0)
    jj = lax.broadcasted_iota(jnp.int32, (n, n), 1)
    together = ii // base == jj // base
    pick = jnp.concatenate(
        [(together & (ii % base == j)).astype(F32).astype(BF16) for j in range(base - 1)], axis=1
    )
    high, low = split(jnp.concatenate(compact, axis=0))
    columns = mm(high, pick) + mm(low, pick)
    start = (lane % base == row).astype(F32)
    ts = [start for _ in blocks]
    for j in range(base - 1):
        part = columns[:, j * n : (j + 1) * n]
        ts = [
            t - part[i * base : (i + 1) * base] * t[j : j + 1] for i, t in enumerate(ts)
        ]
    return [
        jnp.concatenate([jnp.where(lane // base == g, t, 0.0) for g in range(groups)], axis=0)
        for t in ts
    ]


def inverse(blocks):
    n = DIM
    ii = lax.broadcasted_iota(jnp.int32, (n, n), 0)
    jj = lax.broadcasted_iota(jnp.int32, (n, n), 1)

    def off(block, s):
        inside = (ii // (2 * s) == jj // (2 * s)) & (ii // s != jj // s)
        return jnp.where(inside, block, 0.0)

    ts = base_inverses(blocks)
    s = BASE
    while s < n:
        offs = [split(off(b, s)) for b in blocks]
        tss = [split(t) for t in ts]
        mids = [dot3(o, t) for o, t in zip(offs, tss)]
        mids = [split(m) for m in mids]
        ts = [t - dot3(p, m) for t, p, m in zip(ts, tss, mids)]
        s *= 2
    return ts


def kernel_a(
    ids_in, k_in, v_in, beta_in, ab_ref, b_ref, th_ref, tl_ref, z_ref,
    ids_ref, k_ref, v_ref, beta_ref, sems,
):
    copies = [
        pltpu.make_async_copy(source, target, sems.at[at])
        for at, (source, target) in enumerate(
            ((ids_in, ids_ref), (k_in, k_ref), (beta_in, beta_ref), (v_in, v_ref))
        )
    ]
    for copy in copies:
        copy.start()
    for copy in copies[:3]:
        copy.wait()
    same, ii, jj, keep, tail, through = id_masks(ids_ref)
    strict = same & (ii > jj)
    heads = range(HEADS)
    ks = [head(k_ref, j) for j in heads]
    k32 = [k.astype(F32) for k in ks]
    iks = [inv_norm(k) for k in k32]
    rates = [jax.nn.sigmoid(logit_of(beta_ref, j)) for j in heads]
    cs = [r * i * i for r, i in zip(rates, iks)]
    ns = [jnp.where(strict, mm(k, k, NT), 0.0) * c for k, c in zip(ks, cs)]
    blocks = []
    for n in ns:
        blocks += [n[:DIM, :DIM], n[DIM:, DIM:]]
    ts = inverse(blocks)
    t1s = [split(t) for t in ts[0::2]]
    t2s = [split(t) for t in ts[1::2]]
    mids = [split(dot3(split(n[DIM:, :DIM]), t)) for n, t in zip(ns, t1s)]
    lows = [split(-dot3(t, m)) for t, m in zip(t2s, mids)]
    zero = jnp.zeros((DIM, DIM), BF16)
    fulls = [
        tuple(
            jnp.concatenate(
                [
                    jnp.concatenate([t1[p], zero], axis=1),
                    jnp.concatenate([lo[p], t2[p]], axis=1),
                ],
                axis=0,
            )
            for p in range(2)
        )
        for t1, t2, lo in zip(t1s, t2s, lows)
    ]
    eye = (
        lax.broadcasted_iota(jnp.int32, (DIM, DIM), 0)
        == lax.broadcasted_iota(jnp.int32, (DIM, DIM), 1)
    ).astype(F32)
    zs = [dot2r((k * tail).astype(BF16), full, TN) for k, full in zip(k32, fulls)]
    copies[3].wait()
    for j in heads:
        right = writes(head(v_ref, j).astype(F32), k32[j], rates[j], iks[j], keep)
        both = dot3(split(zs[j]), split(right))
        block(ab_ref, j)[...] = eye * through - both[:, DIM:]
        block(ab_ref, HEADS + j)[...] = both[:, :DIM]
        block(b_ref, j)[...] = both[:, :DIM]
        th_ref[j] = fulls[j][0]
        tl_ref[j] = fulls[j][1]
        z_ref[j] = zs[j]
    row = ids_ref[...].astype(F32)
    after = notes(row[:, :1], row[:, row.shape[1] - 1 :], 1.0)
    ab_ref[2 * ROWS :] = after
    b_ref[ROWS:] = after


def writes(value, key, rate, ik, keep):
    return jnp.concatenate([value * (rate * ik), key * (rate * ik * ik * keep)], axis=1)


def kernel_b(
    ids_ref, q_ref, k_ref, v_ref, beta_ref, th_ref, tl_ref, z_ref,
    o_ref, e_ref, uw_ref, ph_ref, pl_ref, zh_ref, zl_ref,
):
    same, ii, jj, keep, tail, through = id_masks(ids_ref)
    causal = same & (ii >= jj)
    for start in range(0, HEADS, TOGETHER):
        heads = range(start, start + TOGETHER)
        solve = [(th_ref[j], tl_ref[j]) for j in heads]
        right = []
        for j in heads:
            k32 = head(k_ref, j).astype(F32)
            rate = jax.nn.sigmoid(logit_of(beta_ref, j))
            value = head(v_ref, j).astype(F32)
            right.append(split(writes(value, k32, rate, inv_norm(k32), keep)))
        scores = [
            split(jnp.where(causal, mm(head(q_ref, j), head(k_ref, j), NT), 0.0)) for j in heads
        ]
        solved = [split(lower3(x, t)) for x, t in zip(scores, solve)]
        for at, j in enumerate(heads):
            both = dot3(solved[at], right[at])
            put(o_ref, j, both[:, :DIM])
            put(e_ref, j, head(q_ref, j).astype(F32) * keep - both[:, DIM:])
            uw_ref[j] = dot3(solve[at], right[at])
            ph_ref[j] = jnp.transpose(solved[at][0])
            pl_ref[j] = jnp.transpose(solved[at][1])
            ends = split(jnp.transpose(z_ref[j]))
            put(zh_ref, j, ends[0])
            put(zl_ref, j, ends[1])


def lower3(a, b):
    n = a[0].shape[0] // 2
    top = pack3([p[:n, :n] for p in a], [p[:n, :n] for p in b])
    low = dot3([p[n:] for p in a], b)
    return cat([cat([top, jnp.zeros_like(top)], 1), low], 0)


def kernel_step(ids_ref, ab_ref, prev_ref, out_ref):
    row = ids_ref[...].astype(F32)
    joined = (note(prev_ref[ROWS:], 1) == row[:, :1]).astype(F32)
    for j in range(HEADS):
        made = pack3(split(block(ab_ref, j)[...]), split(block(prev_ref, j)[...]))
        block(out_ref, j)[...] = joined * made + block(ab_ref, HEADS + j)[...]
    out_ref[ROWS:] = ab_ref[2 * ROWS :]


def kernel_join(ids_ref, ab_ref, prev_ref, both_ref, map_ref):
    row = ids_ref[...].astype(F32)
    last = row[:, row.shape[1] - 1 :]
    before = prev_ref[2 * ROWS :]
    joined = (note(before, 1) == row[:, :1]).astype(F32)
    for j in range(HEADS):
        right = cat([block(prev_ref, j)[...], block(prev_ref, HEADS + j)[...]], 1)
        made = joined * dot3(split(block(ab_ref, j)[...]), split(right))
        block(map_ref, j)[...] = made[:, :DIM]
        block(both_ref, j)[...] = made[:, :DIM]
        block(both_ref, HEADS + j)[...] = made[:, DIM:] + block(ab_ref, HEADS + j)[...]
    both_ref[2 * ROWS :] = notes(note(before, 0), last, 1.0)


def kernel_apply(both_ref, mid_ref, out_ref):
    after, middle = both_ref[2 * ROWS :], mid_ref[ROWS:]
    inner = (note(middle, 1) == note(after, 0)).astype(F32)
    for j in range(HEADS):
        made = pack3(split(block(both_ref, j)[...]), split(inner * block(mid_ref, j)[...]))
        block(out_ref, j)[...] = made + block(both_ref, HEADS + j)[...]
    out_ref[ROWS:] = after


def kernel_c(
    ids_ref, q_ref, o_ref, e_ref, prev_ref, m1_ref, m2_ref, m3_ref, m4_ref, cot_ref, gain_ref,
    y_ref, do_ref, c_ref, s_ref, dg_ref,
):
    first = ids_ref[...].astype(F32)[:, :1]
    before = prev_ref[2 * ROWS :]
    parts = (m1_ref, m2_ref, m3_ref, m4_ref)
    middle = sum(part[ROWS:] for part in parts)
    known = note(before, 2)
    inner = (note(middle, 1) == note(before, 0)).astype(F32)
    direct = (1.0 - known) * (note(middle, 1) == first).astype(F32)
    joined = known * (note(before, 1) == first).astype(F32)
    states = []
    for j in range(HEADS):
        mid = sum(block(part, j)[...] for part in parts)
        made = pack3(split(block(prev_ref, j)[...]), split(inner * mid))
        states.append(joined * (made + block(prev_ref, HEADS + j)[...]) + direct * mid)
        s_ref[j] = states[j]
    norm_part(
        states, joined + direct, q_ref, o_ref, e_ref, cot_ref, gain_ref, y_ref, do_ref, c_ref,
        dg_ref,
    )


def kernel_c_known(
    joined_ref, q_ref, o_ref, e_ref, s_ref, cot_ref, gain_ref, y_ref, do_ref, c_ref, dg_ref
):
    states = [s_ref[j] for j in range(HEADS)]
    norm_part(
        states, joined_ref[...], q_ref, o_ref, e_ref, cot_ref, gain_ref, y_ref, do_ref, c_ref,
        dg_ref,
    )


def norm_part(
    states, joined, q_ref, o_ref, e_ref, cot_ref, gain_ref, y_ref, do_ref, c_ref, dg_ref
):
    gain = gain_ref[...]
    dgain = jnp.zeros((1, DIM), F32)
    for start in range(0, HEADS, TOGETHER):
        heads = range(start, start + TOGETHER)
        iq = [inv_norm(head(q_ref, j).astype(F32)) for j in heads]
        effective = [split(head(e_ref, j)) for j in heads]
        out = [
            i * (head(o_ref, j) + pack3(e, split(states[j])))
            for j, e, i in zip(heads, effective, iq)
        ]
        inv = [
            lax.rsqrt(jnp.mean(x * x, axis=-1, keepdims=True) + 1e-05) for x in out
        ]
        unit = [x * i for x, i in zip(out, inv)]
        cot = [head(cot_ref, j).astype(F32) for j in heads]
        pulled = [x * gain for x in cot]
        means = [jnp.mean(p * u, axis=-1, keepdims=True) for p, u in zip(pulled, unit)]
        draw = [
            (i * r) * (p - u * m) for i, r, p, u, m in zip(inv, iq, pulled, unit, means)
        ]
        for at, j in enumerate(heads):
            put(do_ref, j, draw[at])
            block(c_ref, j)[...] = joined * wide3(effective[at], split(draw[at]), TN)
            put(y_ref, j, unit[at] * gain)
            dgain = dgain + jnp.sum(cot[at] * unit[at], axis=0, keepdims=True)
    c_ref[ROWS:] = notes(joined)
    dg_ref[...] = dgain


def kernel_back(ab_ref, c_ref, back_ref, out_ref):
    joined = note(c_ref[ROWS:], 0)
    for j in range(HEADS):
        made = wide3(split(block(ab_ref, j)[...]), split(block(back_ref, j)[...]), TN)
        block(out_ref, j)[...] = block(c_ref, j)[...] + joined * made
    out_ref[ROWS:] = c_ref[ROWS:]


def kernel_back_far(ab_ref, c_ref, map_ref, h_ref, far_ref, near_ref, g_ref, out_ref):
    joined = note(c_ref[ROWS:], 0)
    beyond = note(h_ref[ROWS:], 0)
    backs = []
    for j in range(HEADS):
        far = wide3(split(block(map_ref, j)[...]), split(block(far_ref, j)[...]), TN)
        backs.append(block(near_ref, j)[...] + block(h_ref, j)[...] + beyond * far)
        g_ref[j] = backs[j]
    for j in range(HEADS):
        made = wide3(split(block(ab_ref, j)[...]), split(backs[j]), TN)
        block(out_ref, j)[...] = block(c_ref, j)[...] + joined * made


def kernel_d(
    ids_ref, q_ref, k_ref, ph_ref, pl_ref, do_ref, uw_ref, s_ref,
    dq_ref, u_ref, dr_ref, dk_ref,
):
    same, ii, jj, keep, tail, through = id_masks(ids_ref)
    causal = same & (ii >= jj)
    for start in range(0, HEADS, TOGETHER):
        heads = range(start, start + TOGETHER)
        state = [split(s_ref[j]) for j in heads]
        update = [
            uw_ref[j, :, :DIM] - pack3(split(uw_ref[j, :, DIM:]), x)
            for j, x in zip(heads, state)
        ]
        draws = [split(head(do_ref, j)) for j in heads]
        weights = [
            split(jnp.where(causal, outer3(d, split(u)), 0.0)) for d, u in zip(draws, update)
        ]
        for at, j in enumerate(heads):
            q, k = head(q_ref, j), head(k_ref, j)
            q32 = q.astype(F32)
            dq = keep * pack3_nt(draws[at], state[at]) + dot2(weights[at], k)
            iq = inv_norm(q32)
            dq = dq - q32 * (iq * iq * jnp.sum(q32 * dq, axis=-1, keepdims=True))
            put(dq_ref, j, dq)
            put(u_ref, j, update[at])
            put(dr_ref, j, wide3((ph_ref[j], pl_ref[j]), draws[at]))
            put(dk_ref, j, dot2(weights[at], q, TN))


def kernel_e(
    ids_ref, k_ref, v_ref, beta_ref, zh_ref, zl_ref, u_ref, dr_ref, dkl_ref, s_ref, g_ref, h_ref,
    dk_ref, dv_ref, db_ref,
):
    same, ii, jj, keep, tail, through = id_masks(ids_ref)
    strict = same & (ii > jj)
    shape = (db_ref.shape[1], db_ref.shape[0])
    lane = lax.broadcasted_iota(jnp.int32, shape, 1)
    dbeta = jnp.zeros(shape, F32)
    for start in range(0, HEADS, TOGETHER):
        heads = range(start, start + TOGETHER)
        k32 = [head(k_ref, j).astype(F32) for j in heads]
        ik = [inv_norm(k) for k in k32]
        logit = [logit_of(beta_ref, j) for j in heads]
        rate = [jax.nn.sigmoid(x) for x in logit]
        back = [split(g_ref[j] + block(h_ref, j)[...]) for j in heads]
        dright = [
            head(dr_ref, j) + pack3((head(zh_ref, j), head(zl_ref, j)), g)
            for j, g in zip(heads, back)
        ]
        update = [head(u_ref, j) for j in heads]
        updates = [split(u) for u in update]
        scaled = [split(d * (-r * i * i)) for d, r, i in zip(dright, rate, ik)]
        inner = []
        for x, u in zip(scaled, updates):
            top = outer3([p[:DIM] for p in x], [p[:DIM] for p in u])
            low = outer3([p[DIM:] for p in x], u)
            top = jnp.where(strict[:DIM, :DIM], top, 0.0)
            low = jnp.where(strict[DIM:], low, 0.0)
            left, right = low[:, :DIM], low[:, DIM:]
            top = cat([top + jnp.transpose(top), jnp.transpose(left)], 1)
            low = cat([left, right + jnp.transpose(right)], 1)
            inner.append(split(cat([top, low], 0)))
        for at, j in enumerate(heads):
            put(dv_ref, j, dright[at] * (rate[at] * ik[at]))
            dlogit = jax.nn.sigmoid(-logit[at]) * jnp.sum(
                dright[at] * update[at], axis=-1, keepdims=True
            )
            dbeta = jnp.where(lane == j, dlogit, dbeta)
            dk = head(dkl_ref, j) + dot2(inner[at], head(k_ref, j))
            dk = dk + tail * pack3_nt(updates[at], back[at])
            dk = dk + keep * pack3_nt(scaled[at], split(s_ref[j]))
            dk = dk - k32[at] * (ik[at] * ik[at] * jnp.sum(k32[at] * dk, axis=-1, keepdims=True))
            put(dk_ref, j, dk)
    db_ref[...] = jnp.transpose(dbeta)


def call(kernel, ins, outs, flops, name, **extra):
    return pl.pallas_call(
        kernel,
        out_shape=outs,
        compiler_params=pltpu.CompilerParams(vmem_limit_bytes=16 * 1024 * 1024),
        cost_estimate=pl.CostEstimate(flops=flops, bytes_accessed=4_000_000, transcendentals=0),
        name=name,
        **extra,
    )(*ins)


def shape(*sizes, dtype=F32):
    return jax.ShapeDtypeStruct(sizes, dtype)


def send(value, pairs):
    return lax.ppermute(value, "seq", pairs)


def relay_forward(ab, ids, spans):
    half = spans // 2
    at = ab[:ROWS].reshape(HEADS, DIM, DIM)
    bt = ab[ROWS : 2 * ROWS].reshape(HEADS, DIM, DIM)
    prior = send(ids[:, ids.shape[1] - 1 :], [(s, s + 1) for s in range(spans - 1)])
    joined = (prior == ids[:, :1]).astype(F32)
    entering = jnp.zeros((HEADS, DIM, DIM), F32)
    outgoing = bt
    for turn in range(half):
        pairs = [(turn, turn + 1)]
        if turn == 0:
            pairs += [(s, s + 1) for s in range(half, spans - 1)]
        entering = entering + joined[:, :, None] * send(outgoing, pairs)
        if turn < half - 1:
            dims = (((2,), (1,)), ((0,), (0,)))
            outgoing = lax.dot_general(at, entering, dims, precision=HIGHEST) + bt
    return entering, joined


def relay_backward(ab, c, spans):
    half = spans // 2
    at = ab[:ROWS].reshape(HEADS, DIM, DIM)
    joined = c[ROWS : ROWS + 1, :1]
    cs = c[:ROWS].reshape(HEADS, DIM, DIM)
    back = jnp.zeros((HEADS, DIM, DIM), F32)
    outgoing = cs
    for turn in range(half):
        pairs = [(half - turn, half - turn - 1)]
        if turn == 0:
            pairs += [(s, s - 1) for s in range(half + 1, spans)]
        back = back + send(outgoing, pairs)
        if turn < half - 1:
            dims = (((1,), (1,)), ((0,), (0,)))
            outgoing = lax.dot_general(at, back, dims, precision=HIGHEST) * joined + cs
    return back


def local(
    query_heads, key_heads, value_heads, beta_logits, segment_ids, output_cotangent, norm_gain
):
    q, k, v = query_heads[0], key_heads[0], value_heads[0]
    beta, ids, cot = jnp.transpose(beta_logits[0]), segment_ids, output_cotangent[0]
    gain = norm_gain[None]
    tokens = q.shape[0]
    spans = lax.axis_size("seq")
    short = spans == 8

    wide, wide16 = shape(tokens, ROWS), shape(tokens, ROWS, dtype=BF16)
    states = shape(HEADS, DIM, DIM)
    square = shape(HEADS, tokens, tokens, dtype=BF16)
    one, two = shape(ROWS + META, DIM), shape(2 * ROWS + META, DIM)
    row = shape(1, DIM)
    unit = 2 * HEADS * tokens**3

    ab, bm, th, tl, z = call(
        kernel_a, (ids, k, v, beta), (two, one, square, square, shape(HEADS, DIM, tokens)),
        20 * unit, "span_state",
        in_specs=[pl.BlockSpec(memory_space=pltpu.HBM)] * 4,
        scratch_shapes=[
            pltpu.VMEM(ids.shape, ids.dtype),
            pltpu.VMEM(k.shape, k.dtype),
            pltpu.VMEM(v.shape, v.dtype),
            pltpu.VMEM(beta.shape, beta.dtype),
            pltpu.SemaphoreType.DMA((4,)),
        ],
    )
    if short:
        r1 = send(bm, [(0, 1)])
        r3 = send(ab, [(2, 3)])
        mid = call(kernel_step, (ids, ab, r1), one, unit, "step")
        m3 = send(mid, [(1, 3)])
        r3, mid = lax.optimization_barrier((r3, mid))
        pair, pair_map = call(
            kernel_join, (ids, ab, r3), (two, shape(ROWS, DIM)), unit, "join"
        )
        far_map = send(pair_map, [(3, 1)])
        th, pair = lax.optimization_barrier((th, pair))
    o0, eff, uw, ph, pl_, zh, zl = call(
        kernel_b, (ids, q, k, v, beta, th, tl, z),
        (
            wide, wide, shape(HEADS, tokens, 2 * DIM), square, square, wide16, wide16,
        ),
        11 * unit, "span_out",
    )
    if short:
        mid, o0 = lax.optimization_barrier((mid, o0))
        m3, far_map, o0 = lax.optimization_barrier((m3, far_map, o0))
        m2 = send(mid, [(1, 2), (4, 5), (5, 6), (6, 7)])
        m4 = send(call(kernel_apply, (pair, m3), one, unit, "apply"), [(3, 4)])
        mixed, draw, c, entering, dgain = call(
            kernel_c, (ids, q, o0, eff, r3, r1, m2, m3, m4, cot, gain),
            (wide16, wide, one, states, row), 4 * unit, "span_norm",
        )
        n3 = send(c, [(4, 1)])
        n4 = send(c, [(4, 3)])
        n1 = send(c, [(3, 2)])
        h = call(kernel_back, (ab, c, n1), one, unit, "back")
        n2 = send(h, [(2, 1)])
    else:
        entering, joined = relay_forward(ab, ids, spans)
        mixed, draw, c, dgain = call(
            kernel_c_known, (joined, q, o0, eff, entering, cot, gain),
            (wide16, wide, one, row), 4 * unit, "span_norm",
        )
    rows = lax.axis_size("dp")
    got = lax.ppermute(dgain, "dp", [(i, i ^ 1) for i in range(rows)])
    dq, update, dright, dkl = call(
        kernel_d, (ids, q, k, ph, pl_, draw, uw, entering), (wide16, wide, wide, wide),
        12 * unit, "span_query_grad",
    )
    got, update = lax.optimization_barrier((got, update))
    dgain = dgain + got
    step = 2
    while step < rows:
        dgain = dgain + lax.ppermute(dgain, "dp", [(i, i ^ step) for i in range(rows)])
        step *= 2
    if short:
        n3, n4, update = lax.optimization_barrier((n3, n4, update))
        back, last = call(
            kernel_back_far, (ab, c, far_map, n2, n3, n4), (states, shape(ROWS, DIM)), unit,
            "back_far",
        )
        far = send(last, [(1, 0), (3, 2), (5, 4), (6, 5), (7, 6)])
    else:
        back = relay_backward(ab, c, spans)
        far = jnp.zeros((ROWS, DIM), F32)
    dk, dv, dbeta = call(
        kernel_e, (ids, k, v, beta, zh, zl, update, dright, dkl, entering, back, far),
        (wide16, wide16, shape(HEADS, tokens)), 12 * unit, "span_key_grad",
    )
    dgain, dbeta = lax.optimization_barrier((dgain, dbeta))
    copies = jnp.broadcast_to(dgain, (spans, DIM))[:, None]
    gain_total = jnp.sum(lax.all_to_all(copies, "seq", 0, 0), axis=(0, 1))
    return (mixed[None], dq[None], dk[None], dv[None], jnp.transpose(dbeta)[None], gain_total)


def solution(mesh):
    rows = P("dp", "seq", None)
    return jax.shard_map(
        local,
        mesh=mesh,
        in_specs=(rows, rows, rows, rows, P("dp", "seq"), rows, P()),
        out_specs=(rows, rows, rows, rows, rows, P()),
        check_vma=False,
    )
```

```python
import functools

import jax
import jax.numpy as jnp
from jax import lax
from jax.experimental import pallas as pl
from jax.experimental.pallas import tpu as pltpu
from jax.sharding import PartitionSpec as P

HEADS = 8
DIM = 128
BASE = 16
TOGETHER = 4
ROWS = HEADS * DIM
META = 8
HIGHEST = lax.Precision.HIGHEST
F32 = jnp.float32
BF16 = jnp.bfloat16

NN = (((1,), (0,)), ((), ()))
NT = (((1,), (1,)), ((), ()))
TN = (((0,), (0,)), ((), ()))


def split(x):
    hi = x.astype(BF16)
    return hi, (x - hi.astype(F32)).astype(BF16)


def mm(a, b, dims=NN):
    return lax.dot_general(a, b, dims, preferred_element_type=F32)


def dot3(a, b, dims=NN):
    return mm(a[0], b[0], dims) + (mm(a[0], b[1], dims) + mm(a[1], b[0], dims))


def dot2(a, b, dims=NN):
    return mm(a[0], b, dims) + mm(a[1], b, dims)


def dot2r(a, b, dims=NN):
    return mm(a, b[0], dims) + mm(a, b[1], dims)


def cat(parts, axis):
    return jnp.concatenate(parts, axis=axis)


def pack3(a, b):
    left = cat([a[0], a[1]], 1)
    right = cat([cat([b[0], b[1]], 1), cat([b[0], jnp.zeros_like(b[0])], 1)], 0)
    out = mm(left, right)
    return out[:, :DIM] + out[:, DIM:]


def pack3_nt(a, b):
    left = cat([a[0], a[1]], 1)
    right = cat([cat([b[0], b[0]], 1), cat([b[1], jnp.zeros_like(b[1])], 1)], 0)
    out = mm(left, right, NT)
    return out[:, :DIM] + out[:, DIM:]


def outer3(a, b):
    return mm(cat([a[0], a[1]], 1), cat([b[0], b[0]], 1), NT) + mm(a[0], b[1], NT)


def wide3(a, b, dims=NN):
    out = mm(a[0], cat([b[0], b[1]], 1), dims)
    return out[:, :DIM] + (out[:, DIM:] + mm(a[1], b[0], dims))


def id_masks(ids_ref):
    row = ids_ref[...].astype(F32)
    n = row.shape[1]
    ii = lax.broadcasted_iota(jnp.int32, (n, n), 0)
    jj = lax.broadcasted_iota(jnp.int32, (n, n), 1)
    col = jnp.sum(jnp.where(ii == jj, row, 0.0), axis=1, keepdims=True)
    same = col == row
    first, last = row[:, :1], row[:, n - 1 :]
    keep = (col == first).astype(F32)
    tail = (col == last).astype(F32)
    through = (first == last).astype(F32)
    return same, ii, jj, keep, tail, through


def head(ref, j):
    return ref[:, DIM * j : DIM * (j + 1)]


def block(ref, j):
    return ref.at[DIM * j : DIM * (j + 1)]


def notes(*values):
    lane = lax.broadcasted_iota(jnp.int32, (META, DIM), 1)
    out = jnp.zeros((META, DIM), F32)
    for at, value in enumerate(values):
        out = jnp.where(lane == at, value, out)
    return out


def note(rows, at):
    return rows[:1, at : at + 1]


def put(ref, j, value):
    ref[:, DIM * j : DIM * (j + 1)] = value.astype(ref.dtype)


def inv_norm(x):
    return lax.rsqrt(jnp.sum(x * x, axis=-1, keepdims=True) + 1e-06)


def logit_of(beta_ref, j):
    beta = jnp.transpose(beta_ref[...])
    lane = lax.broadcasted_iota(jnp.int32, beta.shape, 1)
    return jnp.sum(jnp.where(lane == j, beta, 0.0), axis=1, keepdims=True)


def base_inverses(blocks):
    n, base = DIM, BASE
    groups = n // base
    lane = lax.broadcasted_iota(jnp.int32, (base, n), 1)
    row = lax.broadcasted_iota(jnp.int32, (base, n), 0)
    compact = []
    for block in blocks:
        kept = [
            jnp.where(lane // base == g, block[g * base : (g + 1) * base], 0.0)
            for g in range(groups)
        ]
        while len(kept) > 1:
            kept = [x + y for x, y in zip(kept[0::2], kept[1::2])]
        compact.append(kept[0])
    ii = lax.broadcasted_iota(jnp.int32, (n, n), 0)
    jj = lax.broadcasted_iota(jnp.int32, (n, n), 1)
    together = ii // base == jj // base
    pick = jnp.concatenate(
        [(together & (ii % base == j)).astype(F32).astype(BF16) for j in range(base - 1)], axis=1
    )
    high, low = split(jnp.concatenate(compact, axis=0))
    columns = mm(high, pick) + mm(low, pick)
    start = (lane % base == row).astype(F32)
    ts = [start for _ in blocks]
    for j in range(base - 1):
        part = columns[:, j * n : (j + 1) * n]
        ts = [
            t - part[i * base : (i + 1) * base] * t[j : j + 1] for i, t in enumerate(ts)
        ]
    return [
        jnp.concatenate([jnp.where(lane // base == g, t, 0.0) for g in range(groups)], axis=0)
        for t in ts
    ]


def inverse(blocks):
    n = DIM
    ii = lax.broadcasted_iota(jnp.int32, (n, n), 0)
    jj = lax.broadcasted_iota(jnp.int32, (n, n), 1)

    def off(block, s):
        inside = (ii // (2 * s) == jj // (2 * s)) & (ii // s != jj // s)
        return jnp.where(inside, block, 0.0)

    ts = base_inverses(blocks)
    s = BASE
    while s < n:
        offs = [split(off(b, s)) for b in blocks]
        tss = [split(t) for t in ts]
        mids = [dot3(o, t) for o, t in zip(offs, tss)]
        mids = [split(m) for m in mids]
        ts = [t - dot3(p, m) for t, p, m in zip(ts, tss, mids)]
        s *= 2
    return ts


def kernel_a(ids_ref, k_ref, v_ref, beta_ref, ab_ref, b_ref, th_ref, tl_ref, z_ref):
    same, ii, jj, keep, tail, through = id_masks(ids_ref)
    strict = same & (ii > jj)
    heads = range(HEADS)
    ks = [head(k_ref, j) for j in heads]
    k32 = [k.astype(F32) for k in ks]
    iks = [inv_norm(k) for k in k32]
    rates = [jax.nn.sigmoid(logit_of(beta_ref, j)) for j in heads]
    cs = [r * i * i for r, i in zip(rates, iks)]
    ns = [jnp.where(strict, mm(k, k, NT), 0.0) * c for k, c in zip(ks, cs)]
    blocks = []
    for n in ns:
        blocks += [n[:DIM, :DIM], n[DIM:, DIM:]]
    ts = inverse(blocks)
    t1s = [split(t) for t in ts[0::2]]
    t2s = [split(t) for t in ts[1::2]]
    mids = [split(dot3(split(n[DIM:, :DIM]), t)) for n, t in zip(ns, t1s)]
    lows = [split(-dot3(t, m)) for t, m in zip(t2s, mids)]
    zero = jnp.zeros((DIM, DIM), BF16)
    fulls = [
        tuple(
            jnp.concatenate(
                [
                    jnp.concatenate([t1[p], zero], axis=1),
                    jnp.concatenate([lo[p], t2[p]], axis=1),
                ],
                axis=0,
            )
            for p in range(2)
        )
        for t1, t2, lo in zip(t1s, t2s, lows)
    ]
    eye = (
        lax.broadcasted_iota(jnp.int32, (DIM, DIM), 0)
        == lax.broadcasted_iota(jnp.int32, (DIM, DIM), 1)
    ).astype(F32)
    zs = [dot2r((k * tail).astype(BF16), full, TN) for k, full in zip(k32, fulls)]
    for j in heads:
        right = writes(head(v_ref, j).astype(F32), k32[j], rates[j], iks[j], keep)
        both = dot3(split(zs[j]), split(right))
        block(ab_ref, j)[...] = eye * through - both[:, DIM:]
        block(ab_ref, HEADS + j)[...] = both[:, :DIM]
        block(b_ref, j)[...] = both[:, :DIM]
        th_ref[j] = fulls[j][0]
        tl_ref[j] = fulls[j][1]
        z_ref[j] = zs[j]
    row = ids_ref[...].astype(F32)
    after = notes(row[:, :1], row[:, row.shape[1] - 1 :], 1.0)
    ab_ref[2 * ROWS :] = after
    b_ref[ROWS:] = after


def writes(value, key, rate, ik, keep):
    return jnp.concatenate([value * (rate * ik), key * (rate * ik * ik * keep)], axis=1)


def kernel_b(
    ids_ref, q_ref, k_ref, v_ref, beta_ref, th_ref, tl_ref, z_ref,
    o_ref, e_ref, uw_ref, ph_ref, pl_ref, zh_ref, zl_ref,
):
    same, ii, jj, keep, tail, through = id_masks(ids_ref)
    causal = same & (ii >= jj)
    for start in range(0, HEADS, TOGETHER):
        heads = range(start, start + TOGETHER)
        solve = [(th_ref[j], tl_ref[j]) for j in heads]
        right = []
        for j in heads:
            k32 = head(k_ref, j).astype(F32)
            rate = jax.nn.sigmoid(logit_of(beta_ref, j))
            value = head(v_ref, j).astype(F32)
            right.append(split(writes(value, k32, rate, inv_norm(k32), keep)))
        scores = [
            split(jnp.where(causal, mm(head(q_ref, j), head(k_ref, j), NT), 0.0)) for j in heads
        ]
        solved = [split(lower3(x, t)) for x, t in zip(scores, solve)]
        for at, j in enumerate(heads):
            both = dot3(solved[at], right[at])
            put(o_ref, j, both[:, :DIM])
            put(e_ref, j, head(q_ref, j).astype(F32) * keep - both[:, DIM:])
            uw_ref[j] = dot3(solve[at], right[at])
            ph_ref[j] = jnp.transpose(solved[at][0])
            pl_ref[j] = jnp.transpose(solved[at][1])
            ends = split(jnp.transpose(z_ref[j]))
            put(zh_ref, j, ends[0])
            put(zl_ref, j, ends[1])


def lower3(a, b):
    n = a[0].shape[0] // 2
    top = pack3([p[:n, :n] for p in a], [p[:n, :n] for p in b])
    low = dot3([p[n:] for p in a], b)
    return cat([cat([top, jnp.zeros_like(top)], 1), low], 0)


def kernel_step(ids_ref, ab_ref, prev_ref, out_ref):
    row = ids_ref[...].astype(F32)
    joined = (note(prev_ref[ROWS:], 1) == row[:, :1]).astype(F32)
    for j in range(HEADS):
        made = pack3(split(block(ab_ref, j)[...]), split(block(prev_ref, j)[...]))
        block(out_ref, j)[...] = joined * made + block(ab_ref, HEADS + j)[...]
    out_ref[ROWS:] = ab_ref[2 * ROWS :]


def kernel_join(ids_ref, ab_ref, prev_ref, both_ref, map_ref):
    row = ids_ref[...].astype(F32)
    last = row[:, row.shape[1] - 1 :]
    before = prev_ref[2 * ROWS :]
    joined = (note(before, 1) == row[:, :1]).astype(F32)
    for j in range(HEADS):
        right = cat([block(prev_ref, j)[...], block(prev_ref, HEADS + j)[...]], 1)
        made = joined * dot3(split(block(ab_ref, j)[...]), split(right))
        block(map_ref, j)[...] = made[:, :DIM]
        block(both_ref, j)[...] = made[:, :DIM]
        block(both_ref, HEADS + j)[...] = made[:, DIM:] + block(ab_ref, HEADS + j)[...]
    both_ref[2 * ROWS :] = notes(note(before, 0), last, 1.0)


def kernel_apply(both_ref, mid_ref, out_ref):
    after, middle = both_ref[2 * ROWS :], mid_ref[ROWS:]
    inner = (note(middle, 1) == note(after, 0)).astype(F32)
    for j in range(HEADS):
        made = pack3(split(block(both_ref, j)[...]), split(inner * block(mid_ref, j)[...]))
        block(out_ref, j)[...] = made + block(both_ref, HEADS + j)[...]
    out_ref[ROWS:] = after


def kernel_c(
    ids_ref, q_ref, o_ref, e_ref, prev_ref, m1_ref, m2_ref, m3_ref, m4_ref, cot_ref, gain_ref,
    y_ref, do_ref, c_ref, s_ref, dg_ref,
):
    first = ids_ref[...].astype(F32)[:, :1]
    before = prev_ref[2 * ROWS :]
    parts = (m1_ref, m2_ref, m3_ref, m4_ref)
    middle = sum(part[ROWS:] for part in parts)
    known = note(before, 2)
    inner = (note(middle, 1) == note(before, 0)).astype(F32)
    direct = (1.0 - known) * (note(middle, 1) == first).astype(F32)
    joined = known * (note(before, 1) == first).astype(F32)
    states = []
    for j in range(HEADS):
        mid = sum(block(part, j)[...] for part in parts)
        made = pack3(split(block(prev_ref, j)[...]), split(inner * mid))
        states.append(joined * (made + block(prev_ref, HEADS + j)[...]) + direct * mid)
        s_ref[j] = states[j]
    norm_part(
        states, joined + direct, q_ref, o_ref, e_ref, cot_ref, gain_ref, y_ref, do_ref, c_ref,
        dg_ref,
    )


def kernel_c_known(
    joined_ref, q_ref, o_ref, e_ref, s_ref, cot_ref, gain_ref, y_ref, do_ref, c_ref, dg_ref
):
    states = [s_ref[j] for j in range(HEADS)]
    norm_part(
        states, joined_ref[...], q_ref, o_ref, e_ref, cot_ref, gain_ref, y_ref, do_ref, c_ref,
        dg_ref,
    )


def norm_part(
    states, joined, q_ref, o_ref, e_ref, cot_ref, gain_ref, y_ref, do_ref, c_ref, dg_ref
):
    gain = gain_ref[...]
    dgain = jnp.zeros((1, DIM), F32)
    for start in range(0, HEADS, TOGETHER):
        heads = range(start, start + TOGETHER)
        iq = [inv_norm(head(q_ref, j).astype(F32)) for j in heads]
        effective = [split(head(e_ref, j)) for j in heads]
        out = [
            i * (head(o_ref, j) + pack3(e, split(states[j])))
            for j, e, i in zip(heads, effective, iq)
        ]
        inv = [
            lax.rsqrt(jnp.mean(x * x, axis=-1, keepdims=True) + 1e-05) for x in out
        ]
        unit = [x * i for x, i in zip(out, inv)]
        cot = [head(cot_ref, j).astype(F32) for j in heads]
        pulled = [x * gain for x in cot]
        means = [jnp.mean(p * u, axis=-1, keepdims=True) for p, u in zip(pulled, unit)]
        draw = [
            (i * r) * (p - u * m) for i, r, p, u, m in zip(inv, iq, pulled, unit, means)
        ]
        for at, j in enumerate(heads):
            put(do_ref, j, draw[at])
            block(c_ref, j)[...] = joined * wide3(effective[at], split(draw[at]), TN)
            put(y_ref, j, unit[at] * gain)
            dgain = dgain + jnp.sum(cot[at] * unit[at], axis=0, keepdims=True)
    c_ref[ROWS:] = notes(joined)
    dg_ref[...] = dgain


def kernel_back(ab_ref, c_ref, back_ref, out_ref):
    joined = note(c_ref[ROWS:], 0)
    for j in range(HEADS):
        made = wide3(split(block(ab_ref, j)[...]), split(block(back_ref, j)[...]), TN)
        block(out_ref, j)[...] = block(c_ref, j)[...] + joined * made
    out_ref[ROWS:] = c_ref[ROWS:]


def kernel_back_far(ab_ref, c_ref, map_ref, h_ref, far_ref, near_ref, g_ref, out_ref):
    joined = note(c_ref[ROWS:], 0)
    beyond = note(h_ref[ROWS:], 0)
    backs = []
    for j in range(HEADS):
        far = wide3(split(block(map_ref, j)[...]), split(block(far_ref, j)[...]), TN)
        backs.append(block(near_ref, j)[...] + block(h_ref, j)[...] + beyond * far)
        g_ref[j] = backs[j]
    for j in range(HEADS):
        made = wide3(split(block(ab_ref, j)[...]), split(backs[j]), TN)
        block(out_ref, j)[...] = block(c_ref, j)[...] + joined * made


def kernel_d(
    ids_ref, q_ref, k_ref, ph_ref, pl_ref, do_ref, uw_ref, s_ref,
    dq_ref, u_ref, dr_ref, dk_ref,
):
    same, ii, jj, keep, tail, through = id_masks(ids_ref)
    causal = same & (ii >= jj)
    for start in range(0, HEADS, TOGETHER):
        heads = range(start, start + TOGETHER)
        state = [split(s_ref[j]) for j in heads]
        update = [
            uw_ref[j, :, :DIM] - pack3(split(uw_ref[j, :, DIM:]), x)
            for j, x in zip(heads, state)
        ]
        draws = [split(head(do_ref, j)) for j in heads]
        weights = [
            split(jnp.where(causal, outer3(d, split(u)), 0.0)) for d, u in zip(draws, update)
        ]
        for at, j in enumerate(heads):
            q, k = head(q_ref, j), head(k_ref, j)
            q32 = q.astype(F32)
            dq = keep * pack3_nt(draws[at], state[at]) + dot2(weights[at], k)
            iq = inv_norm(q32)
            dq = dq - q32 * (iq * iq * jnp.sum(q32 * dq, axis=-1, keepdims=True))
            put(dq_ref, j, dq)
            put(u_ref, j, update[at])
            put(dr_ref, j, wide3((ph_ref[j], pl_ref[j]), draws[at]))
            put(dk_ref, j, dot2(weights[at], q, TN))


def kernel_e(
    ids_ref, k_ref, v_ref, beta_ref, zh_ref, zl_ref, u_ref, dr_ref, dkl_ref, s_ref, g_ref, h_ref,
    dk_ref, dv_ref, db_ref,
):
    same, ii, jj, keep, tail, through = id_masks(ids_ref)
    strict = same & (ii > jj)
    shape = (db_ref.shape[1], db_ref.shape[0])
    lane = lax.broadcasted_iota(jnp.int32, shape, 1)
    dbeta = jnp.zeros(shape, F32)
    for start in range(0, HEADS, TOGETHER):
        heads = range(start, start + TOGETHER)
        k32 = [head(k_ref, j).astype(F32) for j in heads]
        ik = [inv_norm(k) for k in k32]
        logit = [logit_of(beta_ref, j) for j in heads]
        rate = [jax.nn.sigmoid(x) for x in logit]
        back = [split(g_ref[j] + block(h_ref, j)[...]) for j in heads]
        dright = [
            head(dr_ref, j) + pack3((head(zh_ref, j), head(zl_ref, j)), g)
            for j, g in zip(heads, back)
        ]
        update = [head(u_ref, j) for j in heads]
        updates = [split(u) for u in update]
        scaled = [split(d * (-r * i * i)) for d, r, i in zip(dright, rate, ik)]
        inner = []
        for x, u in zip(scaled, updates):
            top = outer3([p[:DIM] for p in x], [p[:DIM] for p in u])
            low = outer3([p[DIM:] for p in x], u)
            top = jnp.where(strict[:DIM, :DIM], top, 0.0)
            low = jnp.where(strict[DIM:], low, 0.0)
            left, right = low[:, :DIM], low[:, DIM:]
            top = cat([top + jnp.transpose(top), jnp.transpose(left)], 1)
            low = cat([left, right + jnp.transpose(right)], 1)
            inner.append(split(cat([top, low], 0)))
        for at, j in enumerate(heads):
            put(dv_ref, j, dright[at] * (rate[at] * ik[at]))
            dlogit = jax.nn.sigmoid(-logit[at]) * jnp.sum(
                dright[at] * update[at], axis=-1, keepdims=True
            )
            dbeta = jnp.where(lane == j, dlogit, dbeta)
            dk = head(dkl_ref, j) + dot2(inner[at], head(k_ref, j))
            dk = dk + tail * pack3_nt(updates[at], back[at])
            dk = dk + keep * pack3_nt(scaled[at], split(s_ref[j]))
            dk = dk - k32[at] * (ik[at] * ik[at] * jnp.sum(k32[at] * dk, axis=-1, keepdims=True))
            put(dk_ref, j, dk)
    db_ref[...] = jnp.transpose(dbeta)


def call(kernel, ins, outs, flops, name, **extra):
    return pl.pallas_call(
        kernel,
        out_shape=outs,
        compiler_params=pltpu.CompilerParams(vmem_limit_bytes=16 * 1024 * 1024),
        cost_estimate=pl.CostEstimate(flops=flops, bytes_accessed=4_000_000, transcendentals=0),
        name=name,
        **extra,
    )(*ins)


def shape(*sizes, dtype=F32):
    return jax.ShapeDtypeStruct(sizes, dtype)


def send(value, pairs):
    return lax.ppermute(value, "seq", pairs)


def relay_forward(ab, ids, spans):
    half = spans // 2
    at = ab[:ROWS].reshape(HEADS, DIM, DIM)
    bt = ab[ROWS : 2 * ROWS].reshape(HEADS, DIM, DIM)
    prior = send(ids[:, ids.shape[1] - 1 :], [(s, s + 1) for s in range(spans - 1)])
    joined = (prior == ids[:, :1]).astype(F32)
    entering = jnp.zeros((HEADS, DIM, DIM), F32)
    outgoing = bt
    for turn in range(half):
        pairs = [(turn, turn + 1)]
        if turn == 0:
            pairs += [(s, s + 1) for s in range(half, spans - 1)]
        entering = entering + joined[:, :, None] * send(outgoing, pairs)
        if turn < half - 1:
            dims = (((2,), (1,)), ((0,), (0,)))
            outgoing = lax.dot_general(at, entering, dims, precision=HIGHEST) + bt
    return entering, joined


def relay_backward(ab, c, spans):
    half = spans // 2
    at = ab[:ROWS].reshape(HEADS, DIM, DIM)
    joined = c[ROWS : ROWS + 1, :1]
    cs = c[:ROWS].reshape(HEADS, DIM, DIM)
    back = jnp.zeros((HEADS, DIM, DIM), F32)
    outgoing = cs
    for turn in range(half):
        pairs = [(half - turn, half - turn - 1)]
        if turn == 0:
            pairs += [(s, s - 1) for s in range(half + 1, spans)]
        back = back + send(outgoing, pairs)
        if turn < half - 1:
            dims = (((1,), (1,)), ((0,), (0,)))
            outgoing = lax.dot_general(at, back, dims, precision=HIGHEST) * joined + cs
    return back


def local(
    query_heads, key_heads, value_heads, beta_logits, segment_ids, output_cotangent, norm_gain
):
    q, k, v = query_heads[0], key_heads[0], value_heads[0]
    beta, ids, cot = jnp.transpose(beta_logits[0]), segment_ids, output_cotangent[0]
    gain = norm_gain[None]
    tokens = q.shape[0]
    spans = lax.axis_size("seq")
    short = spans == 8

    wide, wide16 = shape(tokens, ROWS), shape(tokens, ROWS, dtype=BF16)
    states = shape(HEADS, DIM, DIM)
    square = shape(HEADS, tokens, tokens, dtype=BF16)
    one, two = shape(ROWS + META, DIM), shape(2 * ROWS + META, DIM)
    row = shape(1, DIM)
    unit = 2 * HEADS * tokens**3

    ab, bm, th, tl, z = call(
        kernel_a, (ids, k, v, beta), (two, one, square, square, shape(HEADS, DIM, tokens)),
        20 * unit, "span_state",
    )
    if short:
        r1 = send(bm, [(0, 1)])
        r3 = send(ab, [(2, 3)])
        mid = call(kernel_step, (ids, ab, r1), one, unit, "step")
        m3 = send(mid, [(1, 3)])
        r3, mid = lax.optimization_barrier((r3, mid))
        pair, pair_map = call(
            kernel_join, (ids, ab, r3), (two, shape(ROWS, DIM)), unit, "join"
        )
        far_map = send(pair_map, [(3, 1)])
        th, pair = lax.optimization_barrier((th, pair))
    o0, eff, uw, ph, pl_, zh, zl = call(
        kernel_b, (ids, q, k, v, beta, th, tl, z),
        (
            wide, wide, shape(HEADS, tokens, 2 * DIM), square, square, wide16, wide16,
        ),
        11 * unit, "span_out",
    )
    if short:
        mid, o0 = lax.optimization_barrier((mid, o0))
        m3, far_map, o0 = lax.optimization_barrier((m3, far_map, o0))
        m2 = send(mid, [(1, 2), (4, 5), (5, 6), (6, 7)])
        m4 = send(call(kernel_apply, (pair, m3), one, unit, "apply"), [(3, 4)])
        mixed, draw, c, entering, dgain = call(
            kernel_c, (ids, q, o0, eff, r3, r1, m2, m3, m4, cot, gain),
            (wide16, wide, one, states, row), 4 * unit, "span_norm",
        )
        n3 = send(c, [(4, 1)])
        n4 = send(c, [(4, 3)])
        n1 = send(c, [(3, 2)])
        h = call(kernel_back, (ab, c, n1), one, unit, "back")
        n2 = send(h, [(2, 1)])
    else:
        entering, joined = relay_forward(ab, ids, spans)
        mixed, draw, c, dgain = call(
            kernel_c_known, (joined, q, o0, eff, entering, cot, gain),
            (wide16, wide, one, row), 4 * unit, "span_norm",
        )
    rows = lax.axis_size("dp")
    got = lax.ppermute(dgain, "dp", [(i, i ^ 1) for i in range(rows)])
    dq, update, dright, dkl = call(
        kernel_d, (ids, q, k, ph, pl_, draw, uw, entering), (wide16, wide, wide, wide),
        12 * unit, "span_query_grad",
    )
    got, update = lax.optimization_barrier((got, update))
    dgain = dgain + got
    step = 2
    while 2 * step < rows:
        dgain = dgain + lax.ppermute(dgain, "dp", [(i, i ^ step) for i in range(rows)])
        step *= 2
    got = lax.ppermute(dgain, "dp", [(i, i ^ step) for i in range(rows)])
    if short:
        n3, n4, update = lax.optimization_barrier((n3, n4, update))
        back, last = call(
            kernel_back_far, (ab, c, far_map, n2, n3, n4), (states, shape(ROWS, DIM)), unit,
            "back_far",
        )
        far = send(last, [(1, 0), (3, 2), (5, 4), (6, 5), (7, 6)])
    else:
        back = relay_backward(ab, c, spans)
        far = jnp.zeros((ROWS, DIM), F32)
    dk, dv, dbeta = call(
        kernel_e, (ids, k, v, beta, zh, zl, update, dright, dkl, entering, back, far),
        (wide16, wide16, shape(HEADS, tokens)), 12 * unit, "span_key_grad",
    )
    got, dbeta = lax.optimization_barrier((got, dbeta))
    dgain = dgain + got
    copies = jnp.broadcast_to(dgain, (spans, DIM))[:, None]
    gain_total = jnp.sum(lax.all_to_all(copies, "seq", 0, 0), axis=(0, 1))
    return (mixed[None], dq[None], dk[None], dv[None], jnp.transpose(dbeta)[None], gain_total)


def solution(mesh):
    rows = P("dp", "seq", None)
    return jax.shard_map(
        local,
        mesh=mesh,
        in_specs=(rows, rows, rows, rows, P("dp", "seq"), rows, P()),
        out_specs=(rows, rows, rows, rows, rows, P()),
        check_vma=False,
    )
```

```python
import functools

import jax
import jax.numpy as jnp
from jax import lax
from jax.experimental import pallas as pl
from jax.experimental.pallas import tpu as pltpu
from jax.sharding import PartitionSpec as P

HEADS = 8
DIM = 128
BASE = 16
TOGETHER = 4
ROWS = HEADS * DIM
META = 8
HIGHEST = lax.Precision.HIGHEST
F32 = jnp.float32
BF16 = jnp.bfloat16

NN = (((1,), (0,)), ((), ()))
NT = (((1,), (1,)), ((), ()))
TN = (((0,), (0,)), ((), ()))


def split(x):
    hi = x.astype(BF16)
    return hi, (x - hi.astype(F32)).astype(BF16)


def mm(a, b, dims=NN):
    return lax.dot_general(a, b, dims, preferred_element_type=F32)


def dot3(a, b, dims=NN):
    return mm(a[0], b[0], dims) + (mm(a[0], b[1], dims) + mm(a[1], b[0], dims))


def dot2(a, b, dims=NN):
    return mm(a[0], b, dims) + mm(a[1], b, dims)


def dot2r(a, b, dims=NN):
    return mm(a, b[0], dims) + mm(a, b[1], dims)


def cat(parts, axis):
    return jnp.concatenate(parts, axis=axis)


def pack3(a, b):
    left = cat([a[0], a[1]], 1)
    right = cat([cat([b[0], b[1]], 1), cat([b[0], jnp.zeros_like(b[0])], 1)], 0)
    out = mm(left, right)
    return out[:, :DIM] + out[:, DIM:]


def pack3_nt(a, b):
    left = cat([a[0], a[1]], 1)
    right = cat([cat([b[0], b[0]], 1), cat([b[1], jnp.zeros_like(b[1])], 1)], 0)
    out = mm(left, right, NT)
    return out[:, :DIM] + out[:, DIM:]


def outer3(a, b):
    return mm(cat([a[0], a[1]], 1), cat([b[0], b[0]], 1), NT) + mm(a[0], b[1], NT)


def wide3(a, b, dims=NN):
    out = mm(a[0], cat([b[0], b[1]], 1), dims)
    return out[:, :DIM] + (out[:, DIM:] + mm(a[1], b[0], dims))


def id_masks(ids_ref):
    row = ids_ref[...].astype(F32)
    n = row.shape[1]
    ii = lax.broadcasted_iota(jnp.int32, (n, n), 0)
    jj = lax.broadcasted_iota(jnp.int32, (n, n), 1)
    col = jnp.sum(jnp.where(ii == jj, row, 0.0), axis=1, keepdims=True)
    same = col == row
    first, last = row[:, :1], row[:, n - 1 :]
    keep = (col == first).astype(F32)
    tail = (col == last).astype(F32)
    through = (first == last).astype(F32)
    return same, ii, jj, keep, tail, through


def head(ref, j):
    return ref[:, DIM * j : DIM * (j + 1)]


def block(ref, j):
    return ref.at[DIM * j : DIM * (j + 1)]


def notes(*values):
    lane = lax.broadcasted_iota(jnp.int32, (META, DIM), 1)
    out = jnp.zeros((META, DIM), F32)
    for at, value in enumerate(values):
        out = jnp.where(lane == at, value, out)
    return out


def note(rows, at):
    return rows[:1, at : at + 1]


def put(ref, j, value):
    ref[:, DIM * j : DIM * (j + 1)] = value.astype(ref.dtype)


def inv_norm(x):
    return lax.rsqrt(jnp.sum(x * x, axis=-1, keepdims=True) + 1e-06)


def logit_of(beta_ref, j):
    beta = jnp.transpose(beta_ref[...])
    lane = lax.broadcasted_iota(jnp.int32, beta.shape, 1)
    return jnp.sum(jnp.where(lane == j, beta, 0.0), axis=1, keepdims=True)


def base_inverses(blocks):
    n, base = DIM, BASE
    groups = n // base
    lane = lax.broadcasted_iota(jnp.int32, (base, n), 1)
    row = lax.broadcasted_iota(jnp.int32, (base, n), 0)
    compact = []
    for block in blocks:
        kept = [
            jnp.where(lane // base == g, block[g * base : (g + 1) * base], 0.0)
            for g in range(groups)
        ]
        while len(kept) > 1:
            kept = [x + y for x, y in zip(kept[0::2], kept[1::2])]
        compact.append(kept[0])
    ii = lax.broadcasted_iota(jnp.int32, (n, n), 0)
    jj = lax.broadcasted_iota(jnp.int32, (n, n), 1)
    together = ii // base == jj // base
    pick = jnp.concatenate(
        [(together & (ii % base == j)).astype(F32).astype(BF16) for j in range(base - 1)], axis=1
    )
    high, low = split(jnp.concatenate(compact, axis=0))
    columns = mm(high, pick) + mm(low, pick)
    start = (lane % base == row).astype(F32)
    ts = [start for _ in blocks]
    for j in range(base - 1):
        part = columns[:, j * n : (j + 1) * n]
        ts = [
            t - part[i * base : (i + 1) * base] * t[j : j + 1] for i, t in enumerate(ts)
        ]
    return [
        jnp.concatenate([jnp.where(lane // base == g, t, 0.0) for g in range(groups)], axis=0)
        for t in ts
    ]


def inverse(blocks):
    n = DIM
    ii = lax.broadcasted_iota(jnp.int32, (n, n), 0)
    jj = lax.broadcasted_iota(jnp.int32, (n, n), 1)

    def off(block, s):
        inside = (ii // (2 * s) == jj // (2 * s)) & (ii // s != jj // s)
        return jnp.where(inside, block, 0.0)

    ts = base_inverses(blocks)
    s = BASE
    while s < n:
        offs = [split(off(b, s)) for b in blocks]
        tss = [split(t) for t in ts]
        mids = [pack3(o, t) for o, t in zip(offs, tss)]
        mids = [split(m) for m in mids]
        ts = [t - pack3(p, m) for t, p, m in zip(ts, tss, mids)]
        s *= 2
    return ts


def kernel_a(ids_ref, k_ref, v_ref, beta_ref, ab_ref, b_ref, th_ref, tl_ref, z_ref):
    same, ii, jj, keep, tail, through = id_masks(ids_ref)
    strict = same & (ii > jj)
    heads = range(HEADS)
    ks = [head(k_ref, j) for j in heads]
    k32 = [k.astype(F32) for k in ks]
    iks = [inv_norm(k) for k in k32]
    rates = [jax.nn.sigmoid(logit_of(beta_ref, j)) for j in heads]
    cs = [r * i * i for r, i in zip(rates, iks)]
    ns = [jnp.where(strict, mm(k, k, NT), 0.0) * c for k, c in zip(ks, cs)]
    blocks = []
    for n in ns:
        blocks += [n[:DIM, :DIM], n[DIM:, DIM:]]
    ts = inverse(blocks)
    t1s = [split(t) for t in ts[0::2]]
    t2s = [split(t) for t in ts[1::2]]
    mids = [split(pack3(split(n[DIM:, :DIM]), t)) for n, t in zip(ns, t1s)]
    lows = [split(-pack3(t, m)) for t, m in zip(t2s, mids)]
    zero = jnp.zeros((DIM, DIM), BF16)
    fulls = [
        tuple(
            jnp.concatenate(
                [
                    jnp.concatenate([t1[p], zero], axis=1),
                    jnp.concatenate([lo[p], t2[p]], axis=1),
                ],
                axis=0,
            )
            for p in range(2)
        )
        for t1, t2, lo in zip(t1s, t2s, lows)
    ]
    eye = (
        lax.broadcasted_iota(jnp.int32, (DIM, DIM), 0)
        == lax.broadcasted_iota(jnp.int32, (DIM, DIM), 1)
    ).astype(F32)
    zs = [dot2r((k * tail).astype(BF16), full, TN) for k, full in zip(k32, fulls)]
    for j in heads:
        right = writes(head(v_ref, j).astype(F32), k32[j], rates[j], iks[j], keep)
        both = dot3(split(zs[j]), split(right))
        block(ab_ref, j)[...] = eye * through - both[:, DIM:]
        block(ab_ref, HEADS + j)[...] = both[:, :DIM]
        block(b_ref, j)[...] = both[:, :DIM]
        th_ref[j] = fulls[j][0]
        tl_ref[j] = fulls[j][1]
        z_ref[j] = zs[j]
    row = ids_ref[...].astype(F32)
    after = notes(row[:, :1], row[:, row.shape[1] - 1 :], 1.0)
    ab_ref[2 * ROWS :] = after
    b_ref[ROWS:] = after


def writes(value, key, rate, ik, keep):
    return jnp.concatenate([value * (rate * ik), key * (rate * ik * ik * keep)], axis=1)


def kernel_b(
    ids_ref, q_ref, k_ref, v_ref, beta_ref, th_ref, tl_ref, z_ref,
    o_ref, e_ref, uw_ref, ph_ref, pl_ref, zh_ref, zl_ref,
):
    same, ii, jj, keep, tail, through = id_masks(ids_ref)
    causal = same & (ii >= jj)
    for start in range(0, HEADS, TOGETHER):
        heads = range(start, start + TOGETHER)
        solve = [(th_ref[j], tl_ref[j]) for j in heads]
        right = []
        for j in heads:
            k32 = head(k_ref, j).astype(F32)
            rate = jax.nn.sigmoid(logit_of(beta_ref, j))
            value = head(v_ref, j).astype(F32)
            right.append(split(writes(value, k32, rate, inv_norm(k32), keep)))
        scores = [
            split(jnp.where(causal, mm(head(q_ref, j), head(k_ref, j), NT), 0.0)) for j in heads
        ]
        solved = [split(lower3(x, t)) for x, t in zip(scores, solve)]
        for at, j in enumerate(heads):
            both = dot3(solved[at], right[at])
            put(o_ref, j, both[:, :DIM])
            put(e_ref, j, head(q_ref, j).astype(F32) * keep - both[:, DIM:])
            uw_ref[j] = dot3(solve[at], right[at])
            ph_ref[j] = jnp.transpose(solved[at][0])
            pl_ref[j] = jnp.transpose(solved[at][1])
            ends = split(jnp.transpose(z_ref[j]))
            put(zh_ref, j, ends[0])
            put(zl_ref, j, ends[1])


def lower3(a, b):
    n = a[0].shape[0] // 2
    top = pack3([p[:n, :n] for p in a], [p[:n, :n] for p in b])
    low = dot3([p[n:] for p in a], b)
    return cat([cat([top, jnp.zeros_like(top)], 1), low], 0)


def kernel_step(ids_ref, ab_ref, prev_ref, out_ref):
    row = ids_ref[...].astype(F32)
    joined = (note(prev_ref[ROWS:], 1) == row[:, :1]).astype(F32)
    for j in range(HEADS):
        made = pack3(split(block(ab_ref, j)[...]), split(block(prev_ref, j)[...]))
        block(out_ref, j)[...] = joined * made + block(ab_ref, HEADS + j)[...]
    out_ref[ROWS:] = ab_ref[2 * ROWS :]


def kernel_join(ids_ref, ab_ref, prev_ref, both_ref, map_ref):
    row = ids_ref[...].astype(F32)
    last = row[:, row.shape[1] - 1 :]
    before = prev_ref[2 * ROWS :]
    joined = (note(before, 1) == row[:, :1]).astype(F32)
    for j in range(HEADS):
        right = cat([block(prev_ref, j)[...], block(prev_ref, HEADS + j)[...]], 1)
        made = joined * dot3(split(block(ab_ref, j)[...]), split(right))
        block(map_ref, j)[...] = made[:, :DIM]
        block(both_ref, j)[...] = made[:, :DIM]
        block(both_ref, HEADS + j)[...] = made[:, DIM:] + block(ab_ref, HEADS + j)[...]
    both_ref[2 * ROWS :] = notes(note(before, 0), last, 1.0)


def kernel_apply(both_ref, mid_ref, out_ref):
    after, middle = both_ref[2 * ROWS :], mid_ref[ROWS:]
    inner = (note(middle, 1) == note(after, 0)).astype(F32)
    for j in range(HEADS):
        made = pack3(split(block(both_ref, j)[...]), split(inner * block(mid_ref, j)[...]))
        block(out_ref, j)[...] = made + block(both_ref, HEADS + j)[...]
    out_ref[ROWS:] = after


def kernel_c(
    ids_ref, q_ref, o_ref, e_ref, prev_ref, m1_ref, m2_ref, m3_ref, m4_ref, cot_ref, gain_ref,
    y_ref, do_ref, c_ref, s_ref, dg_ref,
):
    first = ids_ref[...].astype(F32)[:, :1]
    before = prev_ref[2 * ROWS :]
    parts = (m1_ref, m2_ref, m3_ref, m4_ref)
    middle = sum(part[ROWS:] for part in parts)
    known = note(before, 2)
    inner = (note(middle, 1) == note(before, 0)).astype(F32)
    direct = (1.0 - known) * (note(middle, 1) == first).astype(F32)
    joined = known * (note(before, 1) == first).astype(F32)
    states = []
    for j in range(HEADS):
        mid = sum(block(part, j)[...] for part in parts)
        made = pack3(split(block(prev_ref, j)[...]), split(inner * mid))
        states.append(joined * (made + block(prev_ref, HEADS + j)[...]) + direct * mid)
        s_ref[j] = states[j]
    norm_part(
        states, joined + direct, q_ref, o_ref, e_ref, cot_ref, gain_ref, y_ref, do_ref, c_ref,
        dg_ref,
    )


def kernel_c_known(
    joined_ref, q_ref, o_ref, e_ref, s_ref, cot_ref, gain_ref, y_ref, do_ref, c_ref, dg_ref
):
    states = [s_ref[j] for j in range(HEADS)]
    norm_part(
        states, joined_ref[...], q_ref, o_ref, e_ref, cot_ref, gain_ref, y_ref, do_ref, c_ref,
        dg_ref,
    )


def norm_part(
    states, joined, q_ref, o_ref, e_ref, cot_ref, gain_ref, y_ref, do_ref, c_ref, dg_ref
):
    gain = gain_ref[...]
    dgain = jnp.zeros((1, DIM), F32)
    for start in range(0, HEADS, TOGETHER):
        heads = range(start, start + TOGETHER)
        iq = [inv_norm(head(q_ref, j).astype(F32)) for j in heads]
        effective = [split(head(e_ref, j)) for j in heads]
        out = [
            i * (head(o_ref, j) + pack3(e, split(states[j])))
            for j, e, i in zip(heads, effective, iq)
        ]
        inv = [
            lax.rsqrt(jnp.mean(x * x, axis=-1, keepdims=True) + 1e-05) for x in out
        ]
        unit = [x * i for x, i in zip(out, inv)]
        cot = [head(cot_ref, j).astype(F32) for j in heads]
        pulled = [x * gain for x in cot]
        means = [jnp.mean(p * u, axis=-1, keepdims=True) for p, u in zip(pulled, unit)]
        draw = [
            (i * r) * (p - u * m) for i, r, p, u, m in zip(inv, iq, pulled, unit, means)
        ]
        for at, j in enumerate(heads):
            put(do_ref, j, draw[at])
            block(c_ref, j)[...] = joined * wide3(effective[at], split(draw[at]), TN)
            put(y_ref, j, unit[at] * gain)
            dgain = dgain + jnp.sum(cot[at] * unit[at], axis=0, keepdims=True)
    c_ref[ROWS:] = notes(joined)
    dg_ref[...] = dgain


def kernel_back(ab_ref, c_ref, back_ref, out_ref):
    joined = note(c_ref[ROWS:], 0)
    for j in range(HEADS):
        made = wide3(split(block(ab_ref, j)[...]), split(block(back_ref, j)[...]), TN)
        block(out_ref, j)[...] = block(c_ref, j)[...] + joined * made
    out_ref[ROWS:] = c_ref[ROWS:]


def kernel_back_far(ab_ref, c_ref, map_ref, h_ref, far_ref, near_ref, g_ref, out_ref):
    joined = note(c_ref[ROWS:], 0)
    beyond = note(h_ref[ROWS:], 0)
    backs = []
    for j in range(HEADS):
        far = wide3(split(block(map_ref, j)[...]), split(block(far_ref, j)[...]), TN)
        backs.append(block(near_ref, j)[...] + block(h_ref, j)[...] + beyond * far)
        g_ref[j] = backs[j]
    for j in range(HEADS):
        made = wide3(split(block(ab_ref, j)[...]), split(backs[j]), TN)
        block(out_ref, j)[...] = block(c_ref, j)[...] + joined * made


def kernel_d(
    ids_ref, q_ref, k_ref, ph_ref, pl_ref, do_ref, uw_ref, s_ref,
    dq_ref, u_ref, dr_ref, dk_ref,
):
    same, ii, jj, keep, tail, through = id_masks(ids_ref)
    causal = same & (ii >= jj)
    for start in range(0, HEADS, TOGETHER):
        heads = range(start, start + TOGETHER)
        state = [split(s_ref[j]) for j in heads]
        update = [
            uw_ref[j, :, :DIM] - pack3(split(uw_ref[j, :, DIM:]), x)
            for j, x in zip(heads, state)
        ]
        draws = [split(head(do_ref, j)) for j in heads]
        weights = [
            split(jnp.where(causal, outer3(d, split(u)), 0.0)) for d, u in zip(draws, update)
        ]
        for at, j in enumerate(heads):
            q, k = head(q_ref, j), head(k_ref, j)
            q32 = q.astype(F32)
            dq = keep * pack3_nt(draws[at], state[at]) + dot2(weights[at], k)
            iq = inv_norm(q32)
            dq = dq - q32 * (iq * iq * jnp.sum(q32 * dq, axis=-1, keepdims=True))
            put(dq_ref, j, dq)
            put(u_ref, j, update[at])
            put(dr_ref, j, wide3((ph_ref[j], pl_ref[j]), draws[at]))
            put(dk_ref, j, dot2(weights[at], q, TN))


def kernel_e(
    ids_ref, k_ref, v_ref, beta_ref, zh_ref, zl_ref, u_ref, dr_ref, dkl_ref, s_ref, g_ref, h_ref,
    dk_ref, dv_ref, db_ref,
):
    same, ii, jj, keep, tail, through = id_masks(ids_ref)
    strict = same & (ii > jj)
    shape = (db_ref.shape[1], db_ref.shape[0])
    lane = lax.broadcasted_iota(jnp.int32, shape, 1)
    dbeta = jnp.zeros(shape, F32)
    for start in range(0, HEADS, TOGETHER):
        heads = range(start, start + TOGETHER)
        k32 = [head(k_ref, j).astype(F32) for j in heads]
        ik = [inv_norm(k) for k in k32]
        logit = [logit_of(beta_ref, j) for j in heads]
        rate = [jax.nn.sigmoid(x) for x in logit]
        back = [split(g_ref[j] + block(h_ref, j)[...]) for j in heads]
        dright = [
            head(dr_ref, j) + pack3((head(zh_ref, j), head(zl_ref, j)), g)
            for j, g in zip(heads, back)
        ]
        update = [head(u_ref, j) for j in heads]
        updates = [split(u) for u in update]
        scaled = [split(d * (-r * i * i)) for d, r, i in zip(dright, rate, ik)]
        inner = []
        for x, u in zip(scaled, updates):
            top = outer3([p[:DIM] for p in x], [p[:DIM] for p in u])
            low = outer3([p[DIM:] for p in x], u)
            top = jnp.where(strict[:DIM, :DIM], top, 0.0)
            low = jnp.where(strict[DIM:], low, 0.0)
            left, right = low[:, :DIM], low[:, DIM:]
            top = cat([top + jnp.transpose(top), jnp.transpose(left)], 1)
            low = cat([left, right + jnp.transpose(right)], 1)
            inner.append(split(cat([top, low], 0)))
        for at, j in enumerate(heads):
            put(dv_ref, j, dright[at] * (rate[at] * ik[at]))
            dlogit = jax.nn.sigmoid(-logit[at]) * jnp.sum(
                dright[at] * update[at], axis=-1, keepdims=True
            )
            dbeta = jnp.where(lane == j, dlogit, dbeta)
            dk = head(dkl_ref, j) + dot2(inner[at], head(k_ref, j))
            dk = dk + tail * pack3_nt(updates[at], back[at])
            dk = dk + keep * pack3_nt(scaled[at], split(s_ref[j]))
            dk = dk - k32[at] * (ik[at] * ik[at] * jnp.sum(k32[at] * dk, axis=-1, keepdims=True))
            put(dk_ref, j, dk)
    db_ref[...] = jnp.transpose(dbeta)


def call(kernel, ins, outs, flops, name, **extra):
    return pl.pallas_call(
        kernel,
        out_shape=outs,
        compiler_params=pltpu.CompilerParams(vmem_limit_bytes=16 * 1024 * 1024),
        cost_estimate=pl.CostEstimate(flops=flops, bytes_accessed=4_000_000, transcendentals=0),
        name=name,
        **extra,
    )(*ins)


def shape(*sizes, dtype=F32):
    return jax.ShapeDtypeStruct(sizes, dtype)


def send(value, pairs):
    return lax.ppermute(value, "seq", pairs)


def relay_forward(ab, ids, spans):
    half = spans // 2
    at = ab[:ROWS].reshape(HEADS, DIM, DIM)
    bt = ab[ROWS : 2 * ROWS].reshape(HEADS, DIM, DIM)
    prior = send(ids[:, ids.shape[1] - 1 :], [(s, s + 1) for s in range(spans - 1)])
    joined = (prior == ids[:, :1]).astype(F32)
    entering = jnp.zeros((HEADS, DIM, DIM), F32)
    outgoing = bt
    for turn in range(half):
        pairs = [(turn, turn + 1)]
        if turn == 0:
            pairs += [(s, s + 1) for s in range(half, spans - 1)]
        entering = entering + joined[:, :, None] * send(outgoing, pairs)
        if turn < half - 1:
            dims = (((2,), (1,)), ((0,), (0,)))
            outgoing = lax.dot_general(at, entering, dims, precision=HIGHEST) + bt
    return entering, joined


def relay_backward(ab, c, spans):
    half = spans // 2
    at = ab[:ROWS].reshape(HEADS, DIM, DIM)
    joined = c[ROWS : ROWS + 1, :1]
    cs = c[:ROWS].reshape(HEADS, DIM, DIM)
    back = jnp.zeros((HEADS, DIM, DIM), F32)
    outgoing = cs
    for turn in range(half):
        pairs = [(half - turn, half - turn - 1)]
        if turn == 0:
            pairs += [(s, s - 1) for s in range(half + 1, spans)]
        back = back + send(outgoing, pairs)
        if turn < half - 1:
            dims = (((1,), (1,)), ((0,), (0,)))
            outgoing = lax.dot_general(at, back, dims, precision=HIGHEST) * joined + cs
    return back


def local(
    query_heads, key_heads, value_heads, beta_logits, segment_ids, output_cotangent, norm_gain
):
    q, k, v = query_heads[0], key_heads[0], value_heads[0]
    beta, ids, cot = jnp.transpose(beta_logits[0]), segment_ids, output_cotangent[0]
    gain = norm_gain[None]
    tokens = q.shape[0]
    spans = lax.axis_size("seq")
    short = spans == 8

    wide, wide16 = shape(tokens, ROWS), shape(tokens, ROWS, dtype=BF16)
    states = shape(HEADS, DIM, DIM)
    square = shape(HEADS, tokens, tokens, dtype=BF16)
    one, two = shape(ROWS + META, DIM), shape(2 * ROWS + META, DIM)
    row = shape(1, DIM)
    unit = 2 * HEADS * tokens**3

    ab, bm, th, tl, z = call(
        kernel_a, (ids, k, v, beta), (two, one, square, square, shape(HEADS, DIM, tokens)),
        20 * unit, "span_state",
    )
    if short:
        r1 = send(bm, [(0, 1)])
        r3 = send(ab, [(2, 3)])
        mid = call(kernel_step, (ids, ab, r1), one, unit, "step")
        m3 = send(mid, [(1, 3)])
        r3, mid = lax.optimization_barrier((r3, mid))
        pair, pair_map = call(
            kernel_join, (ids, ab, r3), (two, shape(ROWS, DIM)), unit, "join"
        )
        far_map = send(pair_map, [(3, 1)])
        th, pair = lax.optimization_barrier((th, pair))
    o0, eff, uw, ph, pl_, zh, zl = call(
        kernel_b, (ids, q, k, v, beta, th, tl, z),
        (
            wide, wide, shape(HEADS, tokens, 2 * DIM), square, square, wide16, wide16,
        ),
        11 * unit, "span_out",
    )
    if short:
        mid, o0 = lax.optimization_barrier((mid, o0))
        m3, far_map, o0 = lax.optimization_barrier((m3, far_map, o0))
        m2 = send(mid, [(1, 2), (4, 5), (5, 6), (6, 7)])
        m4 = send(call(kernel_apply, (pair, m3), one, unit, "apply"), [(3, 4)])
        mixed, draw, c, entering, dgain = call(
            kernel_c, (ids, q, o0, eff, r3, r1, m2, m3, m4, cot, gain),
            (wide16, wide, one, states, row), 4 * unit, "span_norm",
        )
        n3 = send(c, [(4, 1)])
        n4 = send(c, [(4, 3)])
        n1 = send(c, [(3, 2)])
        h = call(kernel_back, (ab, c, n1), one, unit, "back")
        n2 = send(h, [(2, 1)])
    else:
        entering, joined = relay_forward(ab, ids, spans)
        mixed, draw, c, dgain = call(
            kernel_c_known, (joined, q, o0, eff, entering, cot, gain),
            (wide16, wide, one, row), 4 * unit, "span_norm",
        )
    rows = lax.axis_size("dp")
    got = lax.ppermute(dgain, "dp", [(i, i ^ 1) for i in range(rows)])
    dq, update, dright, dkl = call(
        kernel_d, (ids, q, k, ph, pl_, draw, uw, entering), (wide16, wide, wide, wide),
        12 * unit, "span_query_grad",
    )
    got, update = lax.optimization_barrier((got, update))
    dgain = dgain + got
    step = 2
    while 2 * step < rows:
        dgain = dgain + lax.ppermute(dgain, "dp", [(i, i ^ step) for i in range(rows)])
        step *= 2
    got = lax.ppermute(dgain, "dp", [(i, i ^ step) for i in range(rows)])
    if short:
        n3, n4, update = lax.optimization_barrier((n3, n4, update))
        back, last = call(
            kernel_back_far, (ab, c, far_map, n2, n3, n4), (states, shape(ROWS, DIM)), unit,
            "back_far",
        )
        far = send(last, [(1, 0), (3, 2), (5, 4), (6, 5), (7, 6)])
    else:
        back = relay_backward(ab, c, spans)
        far = jnp.zeros((ROWS, DIM), F32)
    dk, dv, dbeta = call(
        kernel_e, (ids, k, v, beta, zh, zl, update, dright, dkl, entering, back, far),
        (wide16, wide16, shape(HEADS, tokens)), 12 * unit, "span_key_grad",
    )
    got, dbeta = lax.optimization_barrier((got, dbeta))
    dgain = dgain + got
    copies = jnp.broadcast_to(dgain, (spans, DIM))[:, None]
    gain_total = jnp.sum(lax.all_to_all(copies, "seq", 0, 0), axis=(0, 1))
    return (mixed[None], dq[None], dk[None], dv[None], jnp.transpose(dbeta)[None], gain_total)


def solution(mesh):
    rows = P("dp", "seq", None)
    return jax.shard_map(
        local,
        mesh=mesh,
        in_specs=(rows, rows, rows, rows, P("dp", "seq"), rows, P()),
        out_specs=(rows, rows, rows, rows, rows, P()),
        check_vma=False,
    )
```

```python
import functools

import jax
import jax.numpy as jnp
from jax import lax
from jax.experimental import pallas as pl
from jax.experimental.pallas import tpu as pltpu
from jax.sharding import PartitionSpec as P

HEADS = 8
DIM = 128
BASE = 16
TOGETHER = 4
ROWS = HEADS * DIM
META = 8
HIGHEST = lax.Precision.HIGHEST
F32 = jnp.float32
BF16 = jnp.bfloat16

NN = (((1,), (0,)), ((), ()))
NT = (((1,), (1,)), ((), ()))
TN = (((0,), (0,)), ((), ()))


def split(x):
    hi = x.astype(BF16)
    return hi, (x - hi.astype(F32)).astype(BF16)


def mm(a, b, dims=NN):
    return lax.dot_general(a, b, dims, preferred_element_type=F32)


def dot3(a, b, dims=NN):
    return mm(a[0], b[0], dims) + (mm(a[0], b[1], dims) + mm(a[1], b[0], dims))


def dot2(a, b, dims=NN):
    return mm(a[0], b, dims) + mm(a[1], b, dims)


def dot2r(a, b, dims=NN):
    return mm(a, b[0], dims) + mm(a, b[1], dims)


def cat(parts, axis):
    return jnp.concatenate(parts, axis=axis)


def pack3(a, b):
    left = cat([a[0], a[1]], 1)
    right = cat([cat([b[0], b[1]], 1), cat([b[0], jnp.zeros_like(b[0])], 1)], 0)
    out = mm(left, right)
    return out[:, :DIM] + out[:, DIM:]


def pack3_nt(a, b):
    left = cat([a[0], a[1]], 1)
    right = cat([cat([b[0], b[0]], 1), cat([b[1], jnp.zeros_like(b[1])], 1)], 0)
    out = mm(left, right, NT)
    return out[:, :DIM] + out[:, DIM:]


def outer3(a, b):
    return mm(cat([a[0], a[1]], 1), cat([b[0], b[0]], 1), NT) + mm(a[0], b[1], NT)


def wide3(a, b, dims=NN):
    out = mm(a[0], cat([b[0], b[1]], 1), dims)
    return out[:, :DIM] + (out[:, DIM:] + mm(a[1], b[0], dims))


def id_masks(ids_ref):
    row = ids_ref[...].astype(F32)
    n = row.shape[1]
    ii = lax.broadcasted_iota(jnp.int32, (n, n), 0)
    jj = lax.broadcasted_iota(jnp.int32, (n, n), 1)
    col = jnp.sum(jnp.where(ii == jj, row, 0.0), axis=1, keepdims=True)
    same = col == row
    first, last = row[:, :1], row[:, n - 1 :]
    keep = (col == first).astype(F32)
    tail = (col == last).astype(F32)
    through = (first == last).astype(F32)
    return same, ii, jj, keep, tail, through


def head(ref, j):
    return ref[:, DIM * j : DIM * (j + 1)]


def block(ref, j):
    return ref.at[DIM * j : DIM * (j + 1)]


def notes(*values):
    lane = lax.broadcasted_iota(jnp.int32, (META, DIM), 1)
    out = jnp.zeros((META, DIM), F32)
    for at, value in enumerate(values):
        out = jnp.where(lane == at, value, out)
    return out


def note(rows, at):
    return rows[:1, at : at + 1]


def put(ref, j, value):
    ref[:, DIM * j : DIM * (j + 1)] = value.astype(ref.dtype)


def inv_norm(x):
    return lax.rsqrt(jnp.sum(x * x, axis=-1, keepdims=True) + 1e-06)


def logit_of(beta_ref, j):
    beta = jnp.transpose(beta_ref[...])
    lane = lax.broadcasted_iota(jnp.int32, beta.shape, 1)
    return jnp.sum(jnp.where(lane == j, beta, 0.0), axis=1, keepdims=True)


def base_inverses(blocks):
    n, base = DIM, BASE
    groups = n // base
    lane = lax.broadcasted_iota(jnp.int32, (base, n), 1)
    row = lax.broadcasted_iota(jnp.int32, (base, n), 0)
    compact = []
    for block in blocks:
        kept = [
            jnp.where(lane // base == g, block[g * base : (g + 1) * base], 0.0)
            for g in range(groups)
        ]
        while len(kept) > 1:
            kept = [x + y for x, y in zip(kept[0::2], kept[1::2])]
        compact.append(kept[0])
    ii = lax.broadcasted_iota(jnp.int32, (n, n), 0)
    jj = lax.broadcasted_iota(jnp.int32, (n, n), 1)
    together = ii // base == jj // base
    pick = jnp.concatenate(
        [(together & (ii % base == j)).astype(F32).astype(BF16) for j in range(base - 1)], axis=1
    )
    high, low = split(jnp.concatenate(compact, axis=0))
    columns = mm(high, pick) + mm(low, pick)
    start = (lane % base == row).astype(F32)
    ts = [start for _ in blocks]
    for j in range(base - 1):
        part = columns[:, j * n : (j + 1) * n]
        ts = [
            t - part[i * base : (i + 1) * base] * t[j : j + 1] for i, t in enumerate(ts)
        ]
    return [
        jnp.concatenate([jnp.where(lane // base == g, t, 0.0) for g in range(groups)], axis=0)
        for t in ts
    ]


def inverse(blocks):
    n = DIM
    ii = lax.broadcasted_iota(jnp.int32, (n, n), 0)
    jj = lax.broadcasted_iota(jnp.int32, (n, n), 1)

    def off(block, s):
        inside = (ii // (2 * s) == jj // (2 * s)) & (ii // s != jj // s)
        return jnp.where(inside, block, 0.0)

    ts = base_inverses(blocks)
    s = BASE
    inside = (ii // (4 * s) == jj // (4 * s)) & (ii // s != jj // s)
    tss = [split(t) for t in ts]
    steps = [split(pack3(t, split(jnp.where(inside, b, 0.0)))) for t, b in zip(tss, blocks)]
    squares = [split(pack3(m, m)) for m in steps]
    ts = [t - pack3(m, p) for t, m, p in zip(ts, steps, tss)]
    ts = [t + pack3(q, split(t)) for t, q in zip(ts, squares)]
    s *= 4
    while s < n:
        offs = [split(off(b, s)) for b in blocks]
        tss = [split(t) for t in ts]
        mids = [pack3(o, t) for o, t in zip(offs, tss)]
        mids = [split(m) for m in mids]
        ts = [t - pack3(p, m) for t, p, m in zip(ts, tss, mids)]
        s *= 2
    return ts


def kernel_a(ids_ref, k_ref, v_ref, beta_ref, ab_ref, b_ref, th_ref, tl_ref, z_ref):
    same, ii, jj, keep, tail, through = id_masks(ids_ref)
    strict = same & (ii > jj)
    heads = range(HEADS)
    ks = [head(k_ref, j) for j in heads]
    k32 = [k.astype(F32) for k in ks]
    iks = [inv_norm(k) for k in k32]
    rates = [jax.nn.sigmoid(logit_of(beta_ref, j)) for j in heads]
    cs = [r * i * i for r, i in zip(rates, iks)]
    ns = [jnp.where(strict, mm(k, k, NT), 0.0) * c for k, c in zip(ks, cs)]
    blocks = []
    for n in ns:
        blocks += [n[:DIM, :DIM], n[DIM:, DIM:]]
    ts = inverse(blocks)
    t1s = [split(t) for t in ts[0::2]]
    t2s = [split(t) for t in ts[1::2]]
    mids = [split(pack3(split(n[DIM:, :DIM]), t)) for n, t in zip(ns, t1s)]
    lows = [split(-pack3(t, m)) for t, m in zip(t2s, mids)]
    zero = jnp.zeros((DIM, DIM), BF16)
    fulls = [
        tuple(
            jnp.concatenate(
                [
                    jnp.concatenate([t1[p], zero], axis=1),
                    jnp.concatenate([lo[p], t2[p]], axis=1),
                ],
                axis=0,
            )
            for p in range(2)
        )
        for t1, t2, lo in zip(t1s, t2s, lows)
    ]
    eye = (
        lax.broadcasted_iota(jnp.int32, (DIM, DIM), 0)
        == lax.broadcasted_iota(jnp.int32, (DIM, DIM), 1)
    ).astype(F32)
    zs = [dot2r((k * tail).astype(BF16), full, TN) for k, full in zip(k32, fulls)]
    for j in heads:
        right = writes(head(v_ref, j).astype(F32), k32[j], rates[j], iks[j], keep)
        both = dot3(split(zs[j]), split(right))
        block(ab_ref, j)[...] = eye * through - both[:, DIM:]
        block(ab_ref, HEADS + j)[...] = both[:, :DIM]
        block(b_ref, j)[...] = both[:, :DIM]
        th_ref[j] = fulls[j][0]
        tl_ref[j] = fulls[j][1]
        z_ref[j] = zs[j]
    row = ids_ref[...].astype(F32)
    after = notes(row[:, :1], row[:, row.shape[1] - 1 :], 1.0)
    ab_ref[2 * ROWS :] = after
    b_ref[ROWS:] = after


def writes(value, key, rate, ik, keep):
    return jnp.concatenate([value * (rate * ik), key * (rate * ik * ik * keep)], axis=1)


def kernel_b(
    ids_ref, q_ref, k_ref, v_ref, beta_ref, th_ref, tl_ref, z_ref,
    o_ref, e_ref, uw_ref, ph_ref, pl_ref, zh_ref, zl_ref,
):
    same, ii, jj, keep, tail, through = id_masks(ids_ref)
    causal = same & (ii >= jj)
    for start in range(0, HEADS, TOGETHER):
        heads = range(start, start + TOGETHER)
        solve = [(th_ref[j], tl_ref[j]) for j in heads]
        right = []
        for j in heads:
            k32 = head(k_ref, j).astype(F32)
            rate = jax.nn.sigmoid(logit_of(beta_ref, j))
            value = head(v_ref, j).astype(F32)
            right.append(split(writes(value, k32, rate, inv_norm(k32), keep)))
        scores = [
            split(jnp.where(causal, mm(head(q_ref, j), head(k_ref, j), NT), 0.0)) for j in heads
        ]
        solved = [split(lower3(x, t)) for x, t in zip(scores, solve)]
        for at, j in enumerate(heads):
            both = dot3(solved[at], right[at])
            put(o_ref, j, both[:, :DIM])
            put(e_ref, j, head(q_ref, j).astype(F32) * keep - both[:, DIM:])
            uw_ref[j] = dot3(solve[at], right[at])
            ph_ref[j] = jnp.transpose(solved[at][0])
            pl_ref[j] = jnp.transpose(solved[at][1])
            ends = split(jnp.transpose(z_ref[j]))
            put(zh_ref, j, ends[0])
            put(zl_ref, j, ends[1])


def lower3(a, b):
    n = a[0].shape[0] // 2
    top = pack3([p[:n, :n] for p in a], [p[:n, :n] for p in b])
    low = dot3([p[n:] for p in a], b)
    return cat([cat([top, jnp.zeros_like(top)], 1), low], 0)


def kernel_step(ids_ref, ab_ref, prev_ref, out_ref):
    row = ids_ref[...].astype(F32)
    joined = (note(prev_ref[ROWS:], 1) == row[:, :1]).astype(F32)
    for j in range(HEADS):
        made = pack3(split(block(ab_ref, j)[...]), split(block(prev_ref, j)[...]))
        block(out_ref, j)[...] = joined * made + block(ab_ref, HEADS + j)[...]
    out_ref[ROWS:] = ab_ref[2 * ROWS :]


def kernel_join(ids_ref, ab_ref, prev_ref, both_ref, map_ref):
    row = ids_ref[...].astype(F32)
    last = row[:, row.shape[1] - 1 :]
    before = prev_ref[2 * ROWS :]
    joined = (note(before, 1) == row[:, :1]).astype(F32)
    for j in range(HEADS):
        right = cat([block(prev_ref, j)[...], block(prev_ref, HEADS + j)[...]], 1)
        made = joined * dot3(split(block(ab_ref, j)[...]), split(right))
        block(map_ref, j)[...] = made[:, :DIM]
        block(both_ref, j)[...] = made[:, :DIM]
        block(both_ref, HEADS + j)[...] = made[:, DIM:] + block(ab_ref, HEADS + j)[...]
    both_ref[2 * ROWS :] = notes(note(before, 0), last, 1.0)


def kernel_apply(both_ref, mid_ref, out_ref):
    after, middle = both_ref[2 * ROWS :], mid_ref[ROWS:]
    inner = (note(middle, 1) == note(after, 0)).astype(F32)
    for j in range(HEADS):
        made = pack3(split(block(both_ref, j)[...]), split(inner * block(mid_ref, j)[...]))
        block(out_ref, j)[...] = made + block(both_ref, HEADS + j)[...]
    out_ref[ROWS:] = after


def kernel_c(
    ids_ref, q_ref, o_ref, e_ref, prev_ref, m1_ref, m2_ref, m3_ref, m4_ref, cot_ref, gain_ref,
    y_ref, do_ref, c_ref, s_ref, dg_ref,
):
    first = ids_ref[...].astype(F32)[:, :1]
    before = prev_ref[2 * ROWS :]
    parts = (m1_ref, m2_ref, m3_ref, m4_ref)
    middle = sum(part[ROWS:] for part in parts)
    known = note(before, 2)
    inner = (note(middle, 1) == note(before, 0)).astype(F32)
    direct = (1.0 - known) * (note(middle, 1) == first).astype(F32)
    joined = known * (note(before, 1) == first).astype(F32)
    states = []
    for j in range(HEADS):
        mid = sum(block(part, j)[...] for part in parts)
        made = pack3(split(block(prev_ref, j)[...]), split(inner * mid))
        states.append(joined * (made + block(prev_ref, HEADS + j)[...]) + direct * mid)
        s_ref[j] = states[j]
    norm_part(
        states, joined + direct, q_ref, o_ref, e_ref, cot_ref, gain_ref, y_ref, do_ref, c_ref,
        dg_ref,
    )


def kernel_c_known(
    joined_ref, q_ref, o_ref, e_ref, s_ref, cot_ref, gain_ref, y_ref, do_ref, c_ref, dg_ref
):
    states = [s_ref[j] for j in range(HEADS)]
    norm_part(
        states, joined_ref[...], q_ref, o_ref, e_ref, cot_ref, gain_ref, y_ref, do_ref, c_ref,
        dg_ref,
    )


def norm_part(
    states, joined, q_ref, o_ref, e_ref, cot_ref, gain_ref, y_ref, do_ref, c_ref, dg_ref
):
    gain = gain_ref[...]
    dgain = jnp.zeros((1, DIM), F32)
    for start in range(0, HEADS, TOGETHER):
        heads = range(start, start + TOGETHER)
        iq = [inv_norm(head(q_ref, j).astype(F32)) for j in heads]
        effective = [split(head(e_ref, j)) for j in heads]
        out = [
            i * (head(o_ref, j) + pack3(e, split(states[j])))
            for j, e, i in zip(heads, effective, iq)
        ]
        inv = [
            lax.rsqrt(jnp.mean(x * x, axis=-1, keepdims=True) + 1e-05) for x in out
        ]
        unit = [x * i for x, i in zip(out, inv)]
        cot = [head(cot_ref, j).astype(F32) for j in heads]
        pulled = [x * gain for x in cot]
        means = [jnp.mean(p * u, axis=-1, keepdims=True) for p, u in zip(pulled, unit)]
        draw = [
            (i * r) * (p - u * m) for i, r, p, u, m in zip(inv, iq, pulled, unit, means)
        ]
        for at, j in enumerate(heads):
            put(do_ref, j, draw[at])
            block(c_ref, j)[...] = joined * wide3(effective[at], split(draw[at]), TN)
            put(y_ref, j, unit[at] * gain)
            dgain = dgain + jnp.sum(cot[at] * unit[at], axis=0, keepdims=True)
    c_ref[ROWS:] = notes(joined)
    dg_ref[...] = dgain


def kernel_back(ab_ref, c_ref, back_ref, out_ref):
    joined = note(c_ref[ROWS:], 0)
    for j in range(HEADS):
        made = wide3(split(block(ab_ref, j)[...]), split(block(back_ref, j)[...]), TN)
        block(out_ref, j)[...] = block(c_ref, j)[...] + joined * made
    out_ref[ROWS:] = c_ref[ROWS:]


def kernel_back_far(ab_ref, c_ref, map_ref, h_ref, far_ref, near_ref, g_ref, out_ref):
    joined = note(c_ref[ROWS:], 0)
    beyond = note(h_ref[ROWS:], 0)
    backs = []
    for j in range(HEADS):
        far = wide3(split(block(map_ref, j)[...]), split(block(far_ref, j)[...]), TN)
        backs.append(block(near_ref, j)[...] + block(h_ref, j)[...] + beyond * far)
        g_ref[j] = backs[j]
    for j in range(HEADS):
        made = wide3(split(block(ab_ref, j)[...]), split(backs[j]), TN)
        block(out_ref, j)[...] = block(c_ref, j)[...] + joined * made


def kernel_d(
    ids_ref, q_ref, k_ref, ph_ref, pl_ref, do_ref, uw_ref, s_ref,
    dq_ref, u_ref, dr_ref, dk_ref,
):
    same, ii, jj, keep, tail, through = id_masks(ids_ref)
    causal = same & (ii >= jj)
    for start in range(0, HEADS, TOGETHER):
        heads = range(start, start + TOGETHER)
        state = [split(s_ref[j]) for j in heads]
        update = [
            uw_ref[j, :, :DIM] - pack3(split(uw_ref[j, :, DIM:]), x)
            for j, x in zip(heads, state)
        ]
        draws = [split(head(do_ref, j)) for j in heads]
        weights = [
            split(jnp.where(causal, outer3(d, split(u)), 0.0)) for d, u in zip(draws, update)
        ]
        for at, j in enumerate(heads):
            q, k = head(q_ref, j), head(k_ref, j)
            q32 = q.astype(F32)
            dq = keep * pack3_nt(draws[at], state[at]) + dot2(weights[at], k)
            iq = inv_norm(q32)
            dq = dq - q32 * (iq * iq * jnp.sum(q32 * dq, axis=-1, keepdims=True))
            put(dq_ref, j, dq)
            put(u_ref, j, update[at])
            put(dr_ref, j, wide3((ph_ref[j], pl_ref[j]), draws[at]))
            put(dk_ref, j, dot2(weights[at], q, TN))


def kernel_e(
    ids_ref, k_ref, v_ref, beta_ref, zh_ref, zl_ref, u_ref, dr_ref, dkl_ref, s_ref, g_ref, h_ref,
    dk_ref, dv_ref, db_ref,
):
    same, ii, jj, keep, tail, through = id_masks(ids_ref)
    strict = same & (ii > jj)
    shape = (db_ref.shape[1], db_ref.shape[0])
    lane = lax.broadcasted_iota(jnp.int32, shape, 1)
    dbeta = jnp.zeros(shape, F32)
    for start in range(0, HEADS, TOGETHER):
        heads = range(start, start + TOGETHER)
        k32 = [head(k_ref, j).astype(F32) for j in heads]
        ik = [inv_norm(k) for k in k32]
        logit = [logit_of(beta_ref, j) for j in heads]
        rate = [jax.nn.sigmoid(x) for x in logit]
        back = [split(g_ref[j] + block(h_ref, j)[...]) for j in heads]
        dright = [
            head(dr_ref, j) + pack3((head(zh_ref, j), head(zl_ref, j)), g)
            for j, g in zip(heads, back)
        ]
        update = [head(u_ref, j) for j in heads]
        updates = [split(u) for u in update]
        scaled = [split(d * (-r * i * i)) for d, r, i in zip(dright, rate, ik)]
        inner = []
        for x, u in zip(scaled, updates):
            top = outer3([p[:DIM] for p in x], [p[:DIM] for p in u])
            low = outer3([p[DIM:] for p in x], u)
            top = jnp.where(strict[:DIM, :DIM], top, 0.0)
            low = jnp.where(strict[DIM:], low, 0.0)
            left, right = low[:, :DIM], low[:, DIM:]
            top = cat([top + jnp.transpose(top), jnp.transpose(left)], 1)
            low = cat([left, right + jnp.transpose(right)], 1)
            inner.append(split(cat([top, low], 0)))
        for at, j in enumerate(heads):
            put(dv_ref, j, dright[at] * (rate[at] * ik[at]))
            dlogit = jax.nn.sigmoid(-logit[at]) * jnp.sum(
                dright[at] * update[at], axis=-1, keepdims=True
            )
            dbeta = jnp.where(lane == j, dlogit, dbeta)
            dk = head(dkl_ref, j) + dot2(inner[at], head(k_ref, j))
            dk = dk + tail * pack3_nt(updates[at], back[at])
            dk = dk + keep * pack3_nt(scaled[at], split(s_ref[j]))
            dk = dk - k32[at] * (ik[at] * ik[at] * jnp.sum(k32[at] * dk, axis=-1, keepdims=True))
            put(dk_ref, j, dk)
    db_ref[...] = jnp.transpose(dbeta)


def call(kernel, ins, outs, flops, name, **extra):
    return pl.pallas_call(
        kernel,
        out_shape=outs,
        compiler_params=pltpu.CompilerParams(vmem_limit_bytes=16 * 1024 * 1024),
        cost_estimate=pl.CostEstimate(flops=flops, bytes_accessed=4_000_000, transcendentals=0),
        name=name,
        **extra,
    )(*ins)


def shape(*sizes, dtype=F32):
    return jax.ShapeDtypeStruct(sizes, dtype)


def send(value, pairs):
    return lax.ppermute(value, "seq", pairs)


def relay_forward(ab, ids, spans):
    half = spans // 2
    at = ab[:ROWS].reshape(HEADS, DIM, DIM)
    bt = ab[ROWS : 2 * ROWS].reshape(HEADS, DIM, DIM)
    prior = send(ids[:, ids.shape[1] - 1 :], [(s, s + 1) for s in range(spans - 1)])
    joined = (prior == ids[:, :1]).astype(F32)
    entering = jnp.zeros((HEADS, DIM, DIM), F32)
    outgoing = bt
    for turn in range(half):
        pairs = [(turn, turn + 1)]
        if turn == 0:
            pairs += [(s, s + 1) for s in range(half, spans - 1)]
        entering = entering + joined[:, :, None] * send(outgoing, pairs)
        if turn < half - 1:
            dims = (((2,), (1,)), ((0,), (0,)))
            outgoing = lax.dot_general(at, entering, dims, precision=HIGHEST) + bt
    return entering, joined


def relay_backward(ab, c, spans):
    half = spans // 2
    at = ab[:ROWS].reshape(HEADS, DIM, DIM)
    joined = c[ROWS : ROWS + 1, :1]
    cs = c[:ROWS].reshape(HEADS, DIM, DIM)
    back = jnp.zeros((HEADS, DIM, DIM), F32)
    outgoing = cs
    for turn in range(half):
        pairs = [(half - turn, half - turn - 1)]
        if turn == 0:
            pairs += [(s, s - 1) for s in range(half + 1, spans)]
        back = back + send(outgoing, pairs)
        if turn < half - 1:
            dims = (((1,), (1,)), ((0,), (0,)))
            outgoing = lax.dot_general(at, back, dims, precision=HIGHEST) * joined + cs
    return back


def local(
    query_heads, key_heads, value_heads, beta_logits, segment_ids, output_cotangent, norm_gain
):
    q, k, v = query_heads[0], key_heads[0], value_heads[0]
    beta, ids, cot = jnp.transpose(beta_logits[0]), segment_ids, output_cotangent[0]
    gain = norm_gain[None]
    tokens = q.shape[0]
    spans = lax.axis_size("seq")
    short = spans == 8

    wide, wide16 = shape(tokens, ROWS), shape(tokens, ROWS, dtype=BF16)
    states = shape(HEADS, DIM, DIM)
    square = shape(HEADS, tokens, tokens, dtype=BF16)
    one, two = shape(ROWS + META, DIM), shape(2 * ROWS + META, DIM)
    row = shape(1, DIM)
    unit = 2 * HEADS * tokens**3

    ab, bm, th, tl, z = call(
        kernel_a, (ids, k, v, beta), (two, one, square, square, shape(HEADS, DIM, tokens)),
        20 * unit, "span_state",
    )
    if short:
        r1 = send(bm, [(0, 1)])
        r3 = send(ab, [(2, 3)])
        mid = call(kernel_step, (ids, ab, r1), one, unit, "step")
        m3 = send(mid, [(1, 3)])
        r3, mid = lax.optimization_barrier((r3, mid))
        pair, pair_map = call(
            kernel_join, (ids, ab, r3), (two, shape(ROWS, DIM)), unit, "join"
        )
        far_map = send(pair_map, [(3, 1)])
        th, pair = lax.optimization_barrier((th, pair))
    o0, eff, uw, ph, pl_, zh, zl = call(
        kernel_b, (ids, q, k, v, beta, th, tl, z),
        (
            wide, wide, shape(HEADS, tokens, 2 * DIM), square, square, wide16, wide16,
        ),
        11 * unit, "span_out",
    )
    if short:
        mid, o0 = lax.optimization_barrier((mid, o0))
        m3, far_map, o0 = lax.optimization_barrier((m3, far_map, o0))
        m2 = send(mid, [(1, 2), (4, 5), (5, 6), (6, 7)])
        m4 = send(call(kernel_apply, (pair, m3), one, unit, "apply"), [(3, 4)])
        mixed, draw, c, entering, dgain = call(
            kernel_c, (ids, q, o0, eff, r3, r1, m2, m3, m4, cot, gain),
            (wide16, wide, one, states, row), 4 * unit, "span_norm",
        )
        n3 = send(c, [(4, 1)])
        n4 = send(c, [(4, 3)])
        n1 = send(c, [(3, 2)])
        h = call(kernel_back, (ab, c, n1), one, unit, "back")
        n2 = send(h, [(2, 1)])
    else:
        entering, joined = relay_forward(ab, ids, spans)
        mixed, draw, c, dgain = call(
            kernel_c_known, (joined, q, o0, eff, entering, cot, gain),
            (wide16, wide, one, row), 4 * unit, "span_norm",
        )
    rows = lax.axis_size("dp")
    got = lax.ppermute(dgain, "dp", [(i, i ^ 1) for i in range(rows)])
    dq, update, dright, dkl = call(
        kernel_d, (ids, q, k, ph, pl_, draw, uw, entering), (wide16, wide, wide, wide),
        12 * unit, "span_query_grad",
    )
    got, update = lax.optimization_barrier((got, update))
    dgain = dgain + got
    step = 2
    while 2 * step < rows:
        dgain = dgain + lax.ppermute(dgain, "dp", [(i, i ^ step) for i in range(rows)])
        step *= 2
    got = lax.ppermute(dgain, "dp", [(i, i ^ step) for i in range(rows)])
    if short:
        n3, n4, update = lax.optimization_barrier((n3, n4, update))
        back, last = call(
            kernel_back_far, (ab, c, far_map, n2, n3, n4), (states, shape(ROWS, DIM)), unit,
            "back_far",
        )
        far = send(last, [(1, 0), (3, 2), (5, 4), (6, 5), (7, 6)])
    else:
        back = relay_backward(ab, c, spans)
        far = jnp.zeros((ROWS, DIM), F32)
    dk, dv, dbeta = call(
        kernel_e, (ids, k, v, beta, zh, zl, update, dright, dkl, entering, back, far),
        (wide16, wide16, shape(HEADS, tokens)), 12 * unit, "span_key_grad",
    )
    got, dbeta = lax.optimization_barrier((got, dbeta))
    dgain = dgain + got
    copies = jnp.broadcast_to(dgain, (spans, DIM))[:, None]
    gain_total = jnp.sum(lax.all_to_all(copies, "seq", 0, 0), axis=(0, 1))
    return (mixed[None], dq[None], dk[None], dv[None], jnp.transpose(dbeta)[None], gain_total)


def solution(mesh):
    rows = P("dp", "seq", None)
    return jax.shard_map(
        local,
        mesh=mesh,
        in_specs=(rows, rows, rows, rows, P("dp", "seq"), rows, P()),
        out_specs=(rows, rows, rows, rows, rows, P()),
        check_vma=False,
    )
```
